32 devices in a mesh: expert: 4 (over z), row: 4 (over y, x), col: 2 (over core).
Axes of the slice: x: 2, y: 2, z: 4, core: 2. Of those that a mesh axis runs over, the one named last changes fastest.
Arguments:
- layer_input: bfloat16 [4096, 2048], P(('expert', 'row', 'col')), may hold values from -6 to 6
- norm_attn: float32 [2048], replicated, may hold values from 0.25 to 1.75
- w_query: bfloat16 [2048, 4096], P(None, ('row', 'col')), may hold values from -0.125 to 0.125
- w_key: bfloat16 [2048, 512], P(None, 'row'), may hold values from -0.125 to 0.125
- w_value: bfloat16 [2048, 512], P(None, 'row'), may hold values from -0.125 to 0.125
- q_gain: float32 [128], replicated, may hold values from 0.25 to 1.75
- k_gain: float32 [128], replicated, may hold values from 0.25 to 1.75
- w_out: bfloat16 [4096, 2048], P(('row', 'col')), may hold values from -0.375 to 0.375
- norm_moe: float32 [2048], replicated, may hold values from 0.25 to 1.75
- w_router: bfloat16 [2048, 32], replicated, may hold values from -0.0625 to 0.0625
- w_gate: bfloat16 [32, 2048, 768], P(('expert', 'row', 'col')), may hold values from -0.125 to 0.125
- w_up: bfloat16 [32, 2048, 768], P(('expert', 'row', 'col')), may hold values from -0.125 to 0.125
- w_down: bfloat16 [32, 768, 2048], P(('expert', 'row', 'col')), may hold values from -0.875 to 0.875
- seq_lengths: int32 [4, 4], P('expert'), may hold values from 64 to 512, as said below
- routes: int32 [4096, 8], P(('expert', 'row', 'col')), may hold values from 0 to 31, all different within a row; in each aligned block of 128 rows (0 to 127, 128 to 255, ...) at most 34 rows name the same one
- out_grad: bfloat16 [4096, 2048], P(('expert', 'row', 'col')), may hold values from -6 to 6
Outputs:
- out: bfloat16 [4096, 2048], P(('expert', 'row', 'col'))
- grad_x: bfloat16 [4096, 2048], P(('expert', 'row', 'col'))
- grad_norm_attn: float32 [2048], replicated
- grad_query: float32 [2048, 4096], P(None, ('row', 'col'))
- grad_key: float32 [2048, 512], P(None, 'row')
- grad_value: float32 [2048, 512], P(None, 'row')
- grad_q_gain: float32 [128], replicated
- grad_k_gain: float32 [128], replicated
- grad_out_proj: float32 [4096, 2048], P(('row', 'col'))
- grad_norm_moe: float32 [2048], replicated
- grad_router: float32 [2048, 32], replicated
- grad_gate: float32 [32, 2048, 768], P(('expert', 'row', 'col'))
- grad_up: float32 [32, 2048, 768], P(('expert', 'row', 'col'))
- grad_down: float32 [32, 768, 2048], P(('expert', 'row', 'col'))
The draws below stay inside these ranges and needn't reach their ends.
Inputs may be any that keep to these rules, and one draw needn't show every extreme that they name: `seq_lengths`: in every group one sequence has exactly 512 slots and the others 1024 // 16 to 170; the slots after them are padding. `routes`: the 8 experts of a slot differ; among the slots of one device no expert is named more than 34 times.
All inputs are finite; a program needn't handle non-finite values.
Results may differ from the reference program's by a relative error of at most 0.024.
Values may be sent and summed in bfloat16 or wider, within the bound.
No kernel may reach another device: no remote copies, remote signals or barrier semaphores. Data moves between devices by JAX's collectives and lax.ppermute only.
A program may use at most 192 MiB of HBM per device.

```python
import math
import jax
import jax.numpy as jnp
import numpy as np
from jax import lax

D = 2048
HEADS = 32
KV_HEADS = 4
HEAD_DIM = 128
FF = 768
TOPK = 8
TOK_DEV = 128
SEQS = 4
GROUPS = 4
GROUP_TOK = 1024
TOKENS = 4096
EXPERTS = 32
CAP = 34


def draw_seq_lengths(key, part):
    key_rest, key_long = jax.random.split(key)
    others = jax.random.randint(key_rest, (GROUPS, SEQS - 1), GROUP_TOK // 16, GROUP_TOK // (2 * (SEQS - 1)) + 1, dtype=jnp.int32)
    longest_at = jax.random.randint(key_long, (GROUPS, 1), 0, SEQS, dtype=jnp.int32)
    columns = jnp.arange(SEQS, dtype=jnp.int32)[None, :]
    padded = jnp.concatenate([others, others[:, :1]], axis=1)
    chosen = columns - (columns > longest_at).astype(jnp.int32)
    selected = jnp.take_along_axis(padded, chosen, axis=1)
    return jnp.where(columns == longest_at, GROUP_TOK // 2, selected).astype(jnp.int32)


def levels(own_key, extent, shards, low, top_value):
    level = 1.0
    for dim, shards_of in shards:
        draws = jax.random.uniform(jax.random.fold_in(jax.random.fold_in(own_key, 6), dim), (shards_of,), jnp.float32, low / len(shards), top_value / len(shards))
        level = level * jnp.repeat(jnp.exp(draws), extent[dim] // shards_of).reshape((-1,) + (1,) * (len(extent) - 1 - dim))
    return level


def assign_block(own_key, own, number, rows, number_of, top, most, skew):
    order = jax.random.permutation(own_key, number_of)
    crowded, usual = load_shares(number_of, rows * top, most, skew, True), load_shares(number_of, rows * top, most, skew, False)
    places = jnp.arange(number_of)

    def named(tallies, offset_by):
        used = int((tallies > 0).sum())
        fixed = max(1, used // 4)
        shifted = fixed + (places - fixed + offset_by * (used - fixed)) % max(1, number_of - fixed)
        return jnp.zeros((number_of,), jnp.int32).at[order[jnp.where(places < fixed, places, shifted)]].set(jnp.asarray(tallies, jnp.int32))

    tallies = jnp.where(number % 4 == 0, named(crowded, number // 4), named(usual, number - number // 4 - 1))
    mixed = jax.random.permutation(jax.random.fold_in(own, 3), number_of)
    source_of, taker = mixed[0:number_of // 2 * 2:2], mixed[1:number_of // 2 * 2:2]
    slack = jnp.minimum(tallies[source_of] - 1, most - tallies[taker]) // 2
    slack = jnp.where((source_of == order[0]) | (taker == order[0]) | (tallies[taker] == 0), 0, jnp.maximum(slack, 0))
    shifted = jax.random.randint(jax.random.fold_in(own, 4), (number_of // 2,), 0, 1 << 20) % (slack + 1)
    tallies = tallies.at[source_of].add(-shifted).at[taker].add(shifted)
    labels = jnp.searchsorted(jnp.cumsum(tallies), jnp.arange(rows * top), side="right").astype(jnp.int32)
    table = labels.reshape(top, rows).T
    table = table[jax.random.permutation(jax.random.fold_in(own, 1), rows)]
    offset_by = jax.random.randint(jax.random.fold_in(own, 2), (rows, 1), 0, top)
    return jnp.take_along_axis(table, (jnp.arange(top)[None, :] + offset_by) % top, axis=1)


def load_shares(count, total, most, skew, full):
    weights = [(1 << 20) // math.isqrt(grade ** skew) + 1 for grade in range(1, count + 1)]
    largest = most if full else min(most, max(-(-total // count), total * weights[0] // sum(weights)))
    least = 1 if total - largest >= count - 1 else 0
    counts, surplus = [largest] + [least] * (count - 1), total - largest - least * (count - 1)
    while surplus > 0:
        candidates = [i for i in range(1, count) if counts[i] < largest] or [i for i in range(1, count) if counts[i] < most]
        pool, budget = sum([weights[i] for i in candidates]), surplus
        for i in candidates:
            extra = min(most - counts[i], max(1, budget * weights[i] // pool), surplus)
            counts[i] = counts[i] + extra
            surplus = surplus - extra
    return np.array(counts)


def scatter_about(key, dims, spread, reach, cuts=(), kind=jnp.bfloat16):
    values = spread * jax.random.normal(key, dims, jnp.float32)
    if cuts:
        values = values * levels(key, dims, cuts, -0.22, 0.18)
    return jnp.clip(values, -reach, reach).astype(kind)


def setup_inputs(seed: int = 0) -> dict:
    streams_of = jax.random.split(jax.random.key(seed), 17)
    layer_input = scatter_about(streams_of[0], (TOKENS, D), 1.0, 6.0, ((0, 32),))
    norm_attn = jnp.clip(1.0 + 0.15 * jax.random.normal(streams_of[1], (D,), jnp.float32), 0.25, 1.75)
    w_query = scatter_about(streams_of[2], (D, HEADS * HEAD_DIM), D ** -0.5, 0.125, ((1, 8),))
    w_key = scatter_about(streams_of[3], (D, KV_HEADS * HEAD_DIM), D ** -0.5, 0.125, ((1, 4),))
    w_value = scatter_about(streams_of[4], (D, KV_HEADS * HEAD_DIM), D ** -0.5, 0.125, ((1, 4),))
    q_gain = jnp.clip(1.0 + 0.15 * jax.random.normal(streams_of[5], (HEAD_DIM,), jnp.float32), 0.25, 1.75)
    k_gain = jnp.clip(1.0 + 0.15 * jax.random.normal(streams_of[6], (HEAD_DIM,), jnp.float32), 0.25, 1.75)
    w_out = scatter_about(streams_of[7], (HEADS * HEAD_DIM, D), (HEADS * HEAD_DIM // 16) ** -0.5, 0.375, ((0, 8),))
    norm_moe = jnp.clip(1.0 + 0.15 * jax.random.normal(streams_of[8], (D,), jnp.float32), 0.25, 1.75)
    w_router = scatter_about(streams_of[9], (D, EXPERTS), (4 * D) ** -0.5, 0.0625)
    w_gate = scatter_about(streams_of[10], (EXPERTS, D, FF), D ** -0.5, 0.125, ((0, 32),))
    w_up = scatter_about(streams_of[11], (EXPERTS, D, FF), D ** -0.5, 0.125, ((0, 32),))
    w_down = scatter_about(streams_of[12], (EXPERTS, FF, D), (FF // 16) ** -0.5, 0.875, ((0, 32),))
    seq_lengths = draw_seq_lengths(jax.random.fold_in(streams_of[16], 71), 0)
    routes_keys = jax.random.split(jax.random.fold_in(streams_of[14], 1), TOKENS // TOK_DEV)
    routes_turns = jax.random.permutation(jax.random.fold_in(streams_of[14], 3), TOKENS // TOK_DEV)
    routes = jax.vmap(lambda own, number: assign_block(jax.random.fold_in(streams_of[14], 2), own, number, TOK_DEV, EXPERTS, TOPK, CAP, 1))(routes_keys, routes_turns).reshape((TOKENS, TOPK))
    out_grad = scatter_about(streams_of[15], (TOKENS, D), 1.0, 6.0, ((0, 32),))
    return {"layer_input": layer_input, "norm_attn": norm_attn, "w_query": w_query, "w_key": w_key, "w_value": w_value, "q_gain": q_gain, "k_gain": k_gain, "w_out": w_out, "norm_moe": norm_moe, "w_router": w_router, "w_gate": w_gate, "w_up": w_up, "w_down": w_down, "seq_lengths": seq_lengths, "routes": routes, "out_grad": out_grad}


@jax.custom_vjp
def low(v):
    return lax.optimization_barrier(v.astype(jnp.bfloat16)).astype(jnp.float32)

@jax.custom_vjp
def low_back(v):
    return v

def low_keep(v):
    return (low(v), None)

def low_pass(kept, grad):
    return (grad,)

def back_keep(v):
    return (v, None)

def back_low(kept, grad):
    return (low(grad),)
low.defvjp(low_keep, low_pass)
low_back.defvjp(back_keep, back_low)
eps_norm = 1e-06
rope_base = 1000000.0
highest = lax.Precision.HIGHEST

def rms_scale(values, norm_gain):
    return values * lax.rsqrt(lax.optimization_barrier(jnp.mean(values * values, axis=-1, keepdims=True)) + eps_norm) * norm_gain

def head_prep(values, norm_gain, cosine_table, sine_table):
    normed = rms_scale(values, norm_gain)
    half_dim = values.shape[-1] // 2
    turned = jnp.concatenate([-normed[..., half_dim:], normed[..., :half_dim]], axis=-1)
    return normed * cosine_table[:, None, :] + turned * sine_table[:, None, :]

def rope_tables(positions, head_dim):
    half_dim = head_dim // 2
    inverse = rope_base ** (-(jnp.arange(half_dim, dtype=jnp.float32) * 2.0 / head_dim))
    angles = positions.astype(jnp.float32)[:, None] * inverse[None, :]
    angles = jnp.concatenate([angles, angles], axis=1)
    return (jnp.cos(angles), jnp.sin(angles))

def group_layout(lengths, slot_count):
    seq_count = lengths.shape[0]
    seq_ends = jnp.cumsum(lengths, dtype=jnp.int32)
    starts = seq_ends - lengths
    slot_ids = jnp.arange(slot_count, dtype=jnp.int32)
    segment = lax.optimization_barrier(jnp.sum((slot_ids[:, None] >= seq_ends[None, :]).astype(jnp.int32), axis=1, dtype=jnp.int32))
    inside = segment < seq_count
    seq_ids = jnp.arange(seq_count, dtype=jnp.int32)
    own_start = lax.optimization_barrier(jnp.sum(jnp.where(seq_ids[None, :] == segment[:, None], starts[None, :], 0), axis=1, dtype=jnp.int32))
    positions = jnp.where(inside, slot_ids - own_start, 0)
    segment = jnp.where(inside, segment, seq_count + slot_ids)
    return (segment, positions)

def layout_one(lengths):
    return group_layout(lengths, GROUP_TOK)

def rope_one(positions):
    return rope_tables(positions, HEAD_DIM)

def attend_block(query_block, segment_block, position_block, key_heads, values_kv, segment, positions):
    rows_here = query_block.shape[0]
    per_group = HEADS // KV_HEADS
    grouped = query_block.reshape(rows_here, KV_HEADS, per_group, HEAD_DIM)
    logits_block = jnp.einsum('qkgd,tkd->kgqt', grouped, key_heads, precision=highest) * HEAD_DIM ** (-0.5)
    logits_block = low_back(logits_block)
    allowed = (segment_block[:, None] == segment[None, :]) & (positions[None, :] <= position_block[:, None])
    weights = jnp.where(allowed[None, None], jnp.exp(logits_block), 0.0)
    probabilities = low(weights / lax.optimization_barrier(jnp.sum(weights, axis=-1, keepdims=True)))
    heads_out = jnp.einsum('kgqt,tkd->qkgd', probabilities, values_kv, precision=highest)
    return heads_out.reshape(rows_here, HEADS * HEAD_DIM)

def reference(layer_input, norm_attn, w_query, w_key, w_value, q_gain, k_gain, w_out, norm_moe, w_router, w_gate, w_up, w_down, seq_lengths, routes, out_grad):
    segments, positions = jax.vmap(layout_one)(seq_lengths)
    cosine_tables, sine_tables = jax.vmap(rope_one)(positions)
    block_rows = min(512, GROUP_TOK)
    block_count = GROUP_TOK // block_rows
    picked = routes.reshape(-1, TOK_DEV * TOPK)
    source_blocks = picked.shape[0]
    onehot = (picked[:, :, None] == jnp.arange(EXPERTS, dtype=jnp.int32)[None, None, :]).astype(jnp.int32)
    slot_rank = lax.optimization_barrier(jnp.sum(jnp.cumsum(onehot, axis=1, dtype=jnp.int32) * onehot, axis=2, dtype=jnp.int32)) - 1
    block_ids = jnp.arange(source_blocks, dtype=jnp.int32)[:, None]
    slot_index = (picked * (source_blocks * CAP) + block_ids * CAP + slot_rank).reshape(-1)
    assign_count = TOKENS * TOPK
    slot_owner = jnp.full((EXPERTS * source_blocks * CAP,), assign_count, jnp.int32).at[slot_index].set(jnp.arange(assign_count, dtype=jnp.int32))
    owner_row = (slot_owner // TOPK).reshape(EXPERTS, source_blocks * CAP)

    def forward(input_rows, gain_attn, query_w, key_w, value_w, query_gain, key_gain, out_w, gain_moe, router_w, gate_w, up_w, down_w):
        normed = low(rms_scale(input_rows, gain_attn))

        def group_attention(inputs):
            group_rows, segment, position, cosine_table, sine_table = inputs
            query_pre = low_back(jnp.dot(group_rows, query_w, precision=highest)).reshape(GROUP_TOK, HEADS, HEAD_DIM)
            key_pre = jnp.dot(group_rows, key_w, precision=highest).reshape(GROUP_TOK, KV_HEADS, HEAD_DIM)
            value_pre = jnp.dot(group_rows, value_w, precision=highest).reshape(GROUP_TOK, KV_HEADS, HEAD_DIM)
            queries = low(head_prep(query_pre, query_gain, cosine_table, sine_table))
            key_heads = low(head_prep(key_pre, key_gain, cosine_table, sine_table))
            values_kv = low(value_pre)

            def one_block(block_inputs):
                return attend_block(block_inputs[0], block_inputs[1], block_inputs[2], key_heads, values_kv, segment, position)
            heads_out = lax.map(jax.checkpoint(one_block), (queries.reshape(block_count, block_rows, HEADS, HEAD_DIM), segment.reshape(block_count, block_rows), position.reshape(block_count, block_rows)))
            heads_low = low_back(low(heads_out.reshape(GROUP_TOK, HEADS * HEAD_DIM)))
            return low_back(jnp.dot(heads_low, out_w, precision=highest))
        attn_rows = lax.map(jax.checkpoint(group_attention), (normed.reshape(GROUPS, GROUP_TOK, D), segments, positions, cosine_tables, sine_tables))
        mixed_rows = input_rows + attn_rows.reshape(TOKENS, D)
        moe_input = low(rms_scale(mixed_rows, gain_moe))
        router_logits = jnp.dot(moe_input, router_w, precision=highest)
        chosen = jnp.take_along_axis(router_logits, routes, axis=1)
        chosen = chosen - lax.optimization_barrier(jnp.max(chosen, axis=1, keepdims=True))
        raised = jnp.exp(chosen)
        gate_values = raised / lax.optimization_barrier(jnp.sum(raised, axis=1, keepdims=True))
        padded_input = jnp.concatenate([moe_input, jnp.zeros((1, D), moe_input.dtype)], axis=0)

        def expert(inputs):
            owner_rows, gate_matrix, up_matrix, down_matrix = inputs
            slot_rows = low_back(padded_input[owner_rows])
            gate_pre = low_back(jnp.dot(slot_rows, gate_matrix, precision=highest))
            up_pre = low_back(jnp.dot(slot_rows, up_matrix, precision=highest))
            hidden = low(jax.nn.silu(gate_pre) * up_pre)
            return low_back(low(jnp.dot(hidden, down_matrix, precision=highest)))
        expert_out = lax.map(jax.checkpoint(expert), (owner_row, gate_w, up_w, down_w))
        assigned = expert_out.reshape(-1, D)[slot_index].reshape(TOKENS, TOPK, D)
        return mixed_rows + lax.optimization_barrier(jnp.sum(gate_values[:, :, None] * assigned, axis=1))
    float_args = (layer_input.astype(jnp.float32), norm_attn, w_query.astype(jnp.float32), w_key.astype(jnp.float32), w_value.astype(jnp.float32), q_gain, k_gain, w_out.astype(jnp.float32), norm_moe, w_router.astype(jnp.float32), w_gate.astype(jnp.float32), w_up.astype(jnp.float32), w_down.astype(jnp.float32))
    out_rows, pullback = jax.vjp(forward, *float_args)
    gradients = pullback(out_grad.astype(jnp.float32))
    return (out_rows.astype(jnp.bfloat16), gradients[0].astype(jnp.bfloat16), gradients[1], gradients[2], gradients[3], gradients[4], gradients[5], gradients[6], gradients[7], gradients[8], gradients[9], gradients[10], gradients[11], gradients[12])
```

```python
import jax
import jax.numpy as jnp
from jax import lax
from jax.sharding import PartitionSpec as P

eps_norm = 1e-06
rope_base = 1000000.0
highest = lax.Precision.HIGHEST
chunk_count = 2


def rms_scale(values, norm_gain):
    return (
        values * lax.rsqrt(jnp.mean(values * values, axis=-1, keepdims=True) + eps_norm) * norm_gain
    )


def head_prep(values, norm_gain, cosine_table, sine_table):
    normed = rms_scale(values, norm_gain)
    half_dim = values.shape[-1] // 2
    turned = jnp.concatenate([-normed[..., half_dim:], normed[..., :half_dim]], axis=-1)
    return normed * cosine_table[:, None, :] + turned * sine_table[:, None, :]


def rope_tables(positions, head_dim):
    half_dim = head_dim // 2
    inverse = rope_base ** (-(jnp.arange(half_dim, dtype=jnp.float32) * 2.0 / head_dim))
    angles = positions.astype(jnp.float32)[:, None] * inverse[None, :]
    angles = jnp.concatenate([angles, angles], axis=1)
    return (jnp.cos(angles), jnp.sin(angles))


def group_layout(lengths, slot_count):
    seq_count = lengths.shape[0]
    seq_ends = jnp.cumsum(lengths, dtype=jnp.int32)
    starts = seq_ends - lengths
    slot_ids = jnp.arange(slot_count, dtype=jnp.int32)
    segment = jnp.sum(
        (slot_ids[:, None] >= seq_ends[None, :]).astype(jnp.int32), axis=1, dtype=jnp.int32
    )
    inside = segment < seq_count
    seq_ids = jnp.arange(seq_count, dtype=jnp.int32)
    own_start = jnp.sum(
        jnp.where(seq_ids[None, :] == segment[:, None], starts[None, :], 0), axis=1, dtype=jnp.int32
    )
    positions = jnp.where(inside, slot_ids - own_start, 0)
    segment = jnp.where(inside, segment, seq_count + slot_ids)
    return (segment, positions)


def times_transposed(left, right):
    return lax.dot_general(
        left, right, (((1,), (1,)), ((), ())), preferred_element_type=jnp.float32
    )


def transposed_times(left, right):
    return lax.dot_general(
        left, right, (((0,), (0,)), ((), ())), preferred_element_type=jnp.float32
    )


plane_axes = ("row", "col")


def move_plane(parts):
    return lax.all_to_all(parts, plane_axes, split_axis=0, concat_axis=0, tiled=True)


def plane_shift(block, step):
    planes = lax.axis_size("expert")
    return lax.ppermute(block, "expert", [(i, (i + step) % planes) for i in range(planes)])


def gather_planes(block):
    planes = lax.axis_size("expert")
    return jnp.concatenate([block] + [plane_shift(block, k) for k in range(1, planes)], axis=0)


def sum_everywhere(values):
    plane_size = lax.axis_size(plane_axes)
    planes = lax.axis_size("expert")
    shares = jnp.sum(move_plane(values.reshape(plane_size, -1, 128)), axis=0)
    shares = lax.all_to_all(
        jnp.broadcast_to(shares[None], (planes,) + shares.shape), "expert", 0, 0, tiled=True
    )
    shares = jnp.sum(shares, axis=0)
    return move_plane(jnp.broadcast_to(shares[None], (plane_size,) + shares.shape)).reshape(-1)


def sum_small(values):
    plane_size = lax.axis_size(plane_axes)
    planes = lax.axis_size("expert")
    values = values.reshape(-1, 128)
    values = jnp.sum(
        move_plane(jnp.broadcast_to(values[None], (plane_size,) + values.shape)), axis=0
    )
    return jnp.sum(
        lax.all_to_all(
            jnp.broadcast_to(values[None], (planes,) + values.shape), "expert", 0, 0, tiled=True
        ),
        axis=0,
    ).reshape(-1)


def rotate(block, axis, step):
    size = lax.axis_size(axis)
    return lax.ppermute(block, axis, [(i, (i + step) % size) for i in range(size)])


def scatter_plane(product):
    col = lax.axis_index("col")
    cols = lax.axis_size("col")
    row = lax.axis_index("row")
    rows = lax.axis_size("row")
    moved = [rotate(product((col + k) % cols).astype(jnp.bfloat16), "col", k) for k in range(1, cols)]
    total = product(col)
    for part in moved:
        total = total + part.astype(jnp.float32)
    low = total.astype(jnp.bfloat16)

    def piece(k):
        return lax.dynamic_index_in_dim(low, (row + k) % rows, 0, keepdims=False)

    arrived = [rotate(piece(k), "row", k) for k in range(1, rows)]
    result = piece(0).astype(jnp.float32)
    for part in arrived:
        result = result + part.astype(jnp.float32)
    return result


def return_planes(parts):
    total = parts[0].astype(jnp.float32)
    for k in range(1, parts.shape[0]):
        total = total + plane_shift(parts[k], -k).astype(jnp.float32)
    return total


def local(
    layer_input,
    norm_attn,
    w_query,
    w_key,
    w_value,
    q_gain,
    k_gain,
    w_out,
    norm_moe,
    w_router,
    w_gate,
    w_up,
    w_down,
    seq_lengths,
    routes,
    out_grad,
):
    tok_dev = layer_input.shape[0]
    model_width = layer_input.shape[1]
    group_tok = tok_dev * lax.axis_size(("row", "col"))
    head_dim = q_gain.shape[0]
    local_heads = w_query.shape[1] // head_dim
    softmax_scale = head_dim ** (-0.5)
    experts = w_router.shape[1]
    top_count = routes.shape[1]
    capacity = tok_dev * top_count * 17 // (16 * experts)
    planes = lax.axis_size("expert")
    plane_size = lax.axis_size(plane_axes)
    plane_index = lax.axis_index("expert")
    plane_cap = planes * capacity
    chosen_here = jnp.any(
        routes[:, :, None] == jnp.arange(experts, dtype=jnp.int32)[None, None, :], axis=1
    )
    plane_routes = gather_planes(routes.T[None])
    plane_experts = plane_index * plane_size + jnp.arange(plane_size, dtype=jnp.int32)
    chosen_plane = jnp.any(
        plane_routes[None] == plane_experts[:, None, None, None], axis=2
    )
    token_ids = jnp.arange(tok_dev, dtype=jnp.int32)
    earlier = (token_ids[:, None] < token_ids[None, :]).astype(jnp.bfloat16)
    slot_rank = jnp.dot(
        chosen_plane.astype(jnp.bfloat16).reshape(plane_size * planes, tok_dev),
        earlier,
        preferred_element_type=jnp.float32,
    ).astype(jnp.int32).reshape(plane_size, planes, tok_dev)
    plane_slot = jnp.where(
        chosen_plane,
        slot_rank + (jnp.arange(planes, dtype=jnp.int32) * capacity)[None, :, None],
        -1,
    ).reshape(plane_size, 1, planes * tok_dev)
    dispatch = (
        plane_slot == jnp.arange(plane_cap, dtype=jnp.int32)[None, :, None]
    ).astype(jnp.bfloat16)
    chosen_all = jnp.any(
        plane_routes[:, :, :, None] == jnp.arange(experts, dtype=jnp.int32), axis=1
    ).reshape(planes * tok_dev, experts).astype(jnp.bfloat16)

    def send_slots(rows_all):
        return move_plane(
            jnp.dot(
                dispatch.reshape(plane_size * plane_cap, -1),
                rows_all,
                preferred_element_type=jnp.float32,
            )
            .astype(jnp.bfloat16)
            .reshape(plane_size, plane_cap, rows_all.shape[1])
        ).reshape(plane_size * plane_cap, rows_all.shape[1])

    slot_chosen = send_slots(chosen_all) > 0.5
    chunk_width = model_width // chunk_count
    chunks = [slice(i * chunk_width, (i + 1) * chunk_width) for i in range(chunk_count)]
    grad_slots = jnp.concatenate(
        [send_slots(gather_planes(out_grad[:, cut])) for cut in chunks], axis=1
    )

    def gates_of(all_logits, chosen):
        top = jnp.max(jnp.where(chosen, all_logits, -3e38), axis=1, keepdims=True)
        raised = jnp.where(chosen, jnp.exp(jnp.where(chosen, all_logits - top, 0.0)), 0.0)
        return raised / jnp.maximum(jnp.sum(raised, axis=1, keepdims=True), 1e-30)

    input_rows = layer_input.astype(jnp.float32)
    normed_one, norm_one_back = jax.vjp(rms_scale, input_rows, norm_attn)
    normed_low = normed_one.astype(jnp.bfloat16)
    group_rows = lax.all_gather(normed_low, ("row", "col"), axis=0, tiled=True)
    segment, positions = group_layout(seq_lengths[0], group_tok)
    cosine_table, sine_table = rope_tables(positions, head_dim)
    query_pre = jnp.dot(group_rows, w_query, preferred_element_type=jnp.float32).reshape(
        group_tok, local_heads, head_dim
    )
    key_pre = jnp.dot(group_rows, w_key, preferred_element_type=jnp.float32)
    value_low = jnp.dot(group_rows, w_value, preferred_element_type=jnp.float32).astype(
        jnp.bfloat16
    )

    def query_prep(values, norm_gain):
        return head_prep(values, norm_gain, cosine_table, sine_table)

    def key_prep(values, norm_gain):
        return head_prep(values[:, None, :], norm_gain, cosine_table, sine_table)[:, 0, :]

    query_full, query_back = jax.vjp(query_prep, query_pre, q_gain)
    key_full, key_back = jax.vjp(key_prep, key_pre, k_gain)
    query_low = query_full.astype(jnp.bfloat16)
    key_low = key_full.astype(jnp.bfloat16)
    block_rows = min(512, group_tok)
    block_count = group_tok // block_rows
    query_blocks = query_low.reshape(block_count, block_rows, local_heads, head_dim)
    segment_blocks = segment.reshape(block_count, block_rows)
    position_blocks = positions.reshape(block_count, block_rows)

    def scores(query_block, segment_block, position_block):
        logits_block = (
            jnp.einsum("qhd,kd->hqk", query_block, key_low, preferred_element_type=jnp.float32)
            * softmax_scale
        )
        allowed = (segment_block[:, None] == segment[None, :]) & (
            positions[None, :] <= position_block[:, None]
        )
        return (logits_block, allowed[None, :, :])

    def attend(inputs):
        query_block, segment_block, position_block = inputs
        logits_block, allowed = scores(query_block, segment_block, position_block)
        weights = jnp.where(allowed, jnp.exp(logits_block), 0.0)
        totals = jnp.sum(weights, axis=-1)
        probabilities = (weights / totals[..., None]).astype(jnp.bfloat16)
        heads_out = jnp.einsum(
            "hqk,kd->qhd", probabilities, value_low, preferred_element_type=jnp.float32
        )
        return (heads_out.astype(jnp.bfloat16), jnp.log(totals))

    head_blocks, log_totals = lax.map(attend, (query_blocks, segment_blocks, position_blocks))
    heads_low = head_blocks.reshape(group_tok, local_heads * head_dim)
    attn_rows = lax.psum_scatter(
        jnp.dot(heads_low, w_out, preferred_element_type=jnp.float32).astype(jnp.bfloat16),
        ("row", "col"),
        scatter_dimension=0,
        tiled=True,
    ).astype(jnp.float32)
    mixed_rows = input_rows + attn_rows
    normed_two, norm_two_back = jax.vjp(rms_scale, mixed_rows, norm_moe)
    moe_input = normed_two.astype(jnp.bfloat16)
    router_logits = jnp.dot(moe_input, w_router, preferred_element_type=jnp.float32)
    source_gates = gates_of(router_logits, chosen_here)

    slot_chunks = [send_slots(gather_planes(moe_input[:, cut])) for cut in chunks]
    moe_slots = jnp.concatenate(slot_chunks, axis=1)
    gate_matrix = w_gate[0]
    up_matrix = w_up[0]
    down_matrix = w_down[0]

    def slots_times(weights):
        return sum(
            jnp.dot(part, weights[cut], preferred_element_type=jnp.float32)
            for part, cut in zip(slot_chunks, chunks)
        )

    slot_logits = slots_times(w_router)
    own_expert = plane_index * plane_size + lax.axis_index(plane_axes)
    own_column = jnp.arange(experts, dtype=jnp.int32)[None, :] == own_expert
    slot_gates = jnp.sum(
        jnp.where(own_column, gates_of(slot_logits, slot_chosen), 0.0), axis=1, keepdims=True
    )
    gate_pre = slots_times(gate_matrix)
    up_pre = slots_times(up_matrix)
    hidden_low = (jax.nn.silu(gate_pre) * up_pre).astype(jnp.bfloat16)
    expert_out = (
        jnp.dot(hidden_low, down_matrix, preferred_element_type=jnp.float32)
        .astype(jnp.bfloat16)
        .astype(jnp.float32)
    )
    slot_grads_full = grad_slots.astype(jnp.float32)
    slot_dots = jnp.sum(expert_out * slot_grads_full, axis=1)
    weighted_out = (expert_out * slot_gates).astype(jnp.bfloat16)
    grad_out_slots = (slot_grads_full * slot_gates).astype(jnp.bfloat16)

    def combine(slot_values):
        width = slot_values.shape[1]
        returned = move_plane(slot_values.reshape(plane_size, plane_cap, width))
        summed = lax.dot_general(
            dispatch.reshape(plane_size * plane_cap, -1),
            returned.reshape(plane_size * plane_cap, width),
            (((0,), (0,)), ((), ())),
            preferred_element_type=jnp.float32,
        ).astype(jnp.bfloat16)
        return return_planes(summed.reshape(planes, tok_dev, width))

    returned_dots = move_plane(slot_dots.reshape(plane_size, 1, plane_cap)).reshape(
        plane_size, plane_cap, 1
    )
    token_dots = jnp.sum(dispatch.astype(jnp.float32) * returned_dots, axis=1).reshape(
        plane_size, planes, tok_dev
    )
    dot_parts = jnp.stack(
        [token_dots[:, 0]] + [plane_shift(token_dots[:, k], -k) for k in range(1, planes)], axis=0
    )
    dot_parts = lax.dynamic_slice_in_dim(
        jnp.concatenate([dot_parts, dot_parts], axis=0), planes - plane_index, planes, axis=0
    )
    grad_gates = dot_parts.reshape(experts, tok_dev).T
    grad_rows = out_grad.astype(jnp.float32)
    grad_logits = source_gates * (
        grad_gates - jnp.sum(source_gates * grad_gates, axis=1, keepdims=True)
    )
    grad_hidden = times_transposed(grad_out_slots, down_matrix)
    sigmoid_gate = jax.nn.sigmoid(gate_pre)
    grad_gate_pre = (
        grad_hidden * up_pre * sigmoid_gate * (1.0 + gate_pre * (1.0 - sigmoid_gate))
    ).astype(jnp.bfloat16)
    grad_up_pre = (grad_hidden * jax.nn.silu(gate_pre)).astype(jnp.bfloat16)
    grad_moe_input = jnp.concatenate(
        [
            combine(
                (
                    times_transposed(grad_gate_pre, gate_matrix[cut])
                    + times_transposed(grad_up_pre, up_matrix[cut])
                ).astype(jnp.bfloat16)
            )
            for cut in chunks
        ],
        axis=1,
    )
    grad_down = transposed_times(hidden_low, grad_out_slots)
    grad_gate = transposed_times(moe_slots, grad_gate_pre)
    grad_up = transposed_times(moe_slots, grad_up_pre)
    grad_router = lax.dot_general(
        grad_logits,
        moe_input.astype(jnp.float32),
        (((0,), (0,)), ((), ())),
        precision=highest,
        preferred_element_type=jnp.float32,
    )
    grad_moe_input = grad_moe_input + jnp.einsum(
        "te,de->td", grad_logits, w_router, precision=highest, preferred_element_type=jnp.float32
    )
    grad_mixed_norm, grad_norm_moe = norm_two_back(grad_moe_input)
    grad_mixed = grad_rows + grad_mixed_norm
    grad_attn_low = grad_mixed.astype(jnp.bfloat16)
    grad_group = lax.all_gather(grad_attn_low, ("row", "col"), axis=0, tiled=True)
    weighted_out, grad_group = lax.optimization_barrier((weighted_out, grad_group))
    out_rows = (mixed_rows + combine(weighted_out)).astype(jnp.bfloat16)
    grad_out_proj = lax.psum(
        transposed_times(heads_low, grad_group).astype(jnp.bfloat16), "expert"
    ).astype(jnp.float32)
    router_sums = sum_everywhere(
        jnp.concatenate([grad_router.reshape(-1), grad_norm_moe])
    )
    grad_router = router_sums[: experts * model_width].reshape(experts, model_width).T
    grad_norm_moe = router_sums[experts * model_width :]
    grad_heads = (
        times_transposed(grad_group, w_out)
        .astype(jnp.bfloat16)
        .reshape(block_count, block_rows, local_heads, head_dim)
    )

    def attend_back(totals, inputs):
        grad_key_acc, grad_value_acc = totals
        query_block, segment_block, position_block, log_block, grad_block = inputs
        logits_block, allowed = scores(query_block, segment_block, position_block)
        probabilities = jnp.where(allowed, jnp.exp(logits_block - log_block[..., None]), 0.0)
        probs_low = probabilities.astype(jnp.bfloat16)
        grad_probs = jnp.einsum(
            "qhd,kd->hqk", grad_block, value_low, preferred_element_type=jnp.float32
        )
        centre = jnp.sum(probabilities * grad_probs, axis=-1, keepdims=True)
        grad_scores = (probabilities * (grad_probs - centre)).astype(jnp.bfloat16)
        grad_query_block = (
            jnp.einsum("hqk,kd->qhd", grad_scores, key_low, preferred_element_type=jnp.float32)
            * softmax_scale
        )
        grad_key_acc = (
            grad_key_acc
            + jnp.einsum(
                "hqk,qhd->kd", grad_scores, query_block, preferred_element_type=jnp.float32
            )
            * softmax_scale
        )
        grad_value_acc = grad_value_acc + jnp.einsum(
            "hqk,qhd->kd", probs_low, grad_block, preferred_element_type=jnp.float32
        )
        return ((grad_key_acc, grad_value_acc), grad_query_block)

    zero_rows = jnp.zeros((group_tok, head_dim), jnp.float32)
    (grad_key_post, grad_value_pre), grad_query_blocks = lax.scan(
        attend_back,
        (zero_rows, zero_rows),
        (query_blocks, segment_blocks, position_blocks, log_totals, grad_heads),
    )
    grad_query_post = grad_query_blocks.reshape(group_tok, local_heads, head_dim)
    grad_query_pre, grad_q_gain = query_back(grad_query_post)
    grad_key_pre, grad_k_gain = key_back(grad_key_post)
    grad_query_low = grad_query_pre.reshape(group_tok, local_heads * head_dim).astype(jnp.bfloat16)
    grad_query = transposed_times(group_rows, grad_query_low)
    grad_kv = jnp.concatenate([grad_key_pre, grad_value_pre], axis=1).astype(jnp.bfloat16)
    grad_key_value = transposed_times(group_rows, grad_kv)
    key_value_w = jnp.concatenate([w_key, w_value], axis=1)
    norm_terms = (
        jnp.sum(grad_query * w_query.astype(jnp.float32), axis=1)
        + jnp.sum(grad_key_value * key_value_w.astype(jnp.float32), axis=1)
    ) / norm_attn
    cols = lax.axis_size("col")
    col = lax.axis_index("col")
    kv_low = grad_key_value.astype(jnp.bfloat16).reshape(cols, model_width // cols, 2 * head_dim)
    kv_part = lax.dynamic_index_in_dim(kv_low, col, 0, keepdims=False).astype(jnp.float32)
    for k in range(1, cols):
        kv_part = kv_part + rotate(
            lax.dynamic_index_in_dim(kv_low, (col + k) % cols, 0, keepdims=False), "col", k
        ).astype(jnp.float32)
    query_low_grad, kv_part, grad_out_proj = lax.optimization_barrier(
        (grad_query.astype(jnp.bfloat16), kv_part.astype(jnp.bfloat16), grad_out_proj)
    )
    grad_query, kv_part = lax.psum((query_low_grad, kv_part), "expert")
    grad_query = grad_query.astype(jnp.float32)
    kv_parts = jnp.stack([kv_part] + [rotate(kv_part, "col", k) for k in range(1, cols)], axis=0)
    kv_parts = lax.dynamic_slice_in_dim(
        jnp.concatenate([kv_parts[::-1], kv_parts[::-1]], axis=0), cols - 1 - col, cols, axis=0
    )
    kv_full = kv_parts.reshape(model_width, 2 * head_dim).astype(jnp.float32)
    grad_key = kv_full[:, :head_dim]
    grad_value = kv_full[:, head_dim:]
    small_sums = sum_small(jnp.concatenate([norm_terms, grad_q_gain, grad_k_gain]))
    grad_norm_attn = small_sums[:model_width]
    grad_q_gain = small_sums[model_width : model_width + head_dim]
    grad_k_gain = small_sums[model_width + head_dim :]
    left_parts = jnp.concatenate([grad_query_low, grad_kv], axis=1).reshape(
        -1, cols, tok_dev, grad_query_low.shape[1] + 2 * head_dim
    )
    right_all = jnp.concatenate([w_query, key_value_w], axis=1)

    def grad_normed_rows(place):
        left = lax.dynamic_index_in_dim(left_parts, place, 1, keepdims=False)
        return lax.dot_general(
            left, right_all, (((2,), (1,)), ((), ())), preferred_element_type=jnp.float32
        )

    grad_normed = scatter_plane(grad_normed_rows)
    grad_input_norm = norm_one_back(grad_normed)[0]
    grad_x = (grad_mixed + grad_input_norm).astype(jnp.bfloat16)
    return (
        out_rows,
        grad_x,
        grad_norm_attn,
        grad_query,
        grad_key,
        grad_value,
        grad_q_gain,
        grad_k_gain,
        grad_out_proj,
        grad_norm_moe,
        grad_router,
        grad_gate[None],
        grad_up[None],
        grad_down[None],
    )


def solution(mesh):
    placed = (
        P(("expert", "row", "col"), None),
        P(),
        P(None, ("row", "col")),
        P(None, "row"),
        P(None, "row"),
        P(),
        P(),
        P(("row", "col"), None),
        P(),
        P(),
        P(("expert", "row", "col"), None, None),
        P(("expert", "row", "col"), None, None),
        P(("expert", "row", "col"), None, None),
        P("expert", None),
        P(("expert", "row", "col"), None),
        P(("expert", "row", "col"), None),
    )
    return jax.shard_map(
        local,
        mesh=mesh,
        in_specs=placed,
        out_specs=(
            P(("expert", "row", "col"), None),
            P(("expert", "row", "col"), None),
            P(),
            P(None, ("row", "col")),
            P(None, "row"),
            P(None, "row"),
            P(),
            P(),
            P(("row", "col"), None),
            P(),
            P(),
            P(("expert", "row", "col"), None, None),
            P(("expert", "row", "col"), None, None),
            P(("expert", "row", "col"), None, None),
        ),
        check_vma=False,
    )
```

```python
import functools

import jax
import jax.numpy as jnp
from jax import lax
from jax.experimental import pallas as pl
from jax.experimental.pallas import tpu as pltpu
from jax.sharding import PartitionSpec as P

eps_norm = 1e-06
rope_base = 1000000.0
highest = lax.Precision.HIGHEST
chunk_count = 2
block_slots = 256
expert_steps = 4
expert_vmem = 48 * 1024 * 1024
kernel_vmem = 40 * 1024 * 1024


def rms_scale(values, norm_gain):
    return (
        values * lax.rsqrt(jnp.mean(values * values, axis=-1, keepdims=True) + eps_norm) * norm_gain
    )


def rope_tables(positions, head_dim):
    half_dim = head_dim // 2
    inverse = rope_base ** (-(jnp.arange(half_dim, dtype=jnp.float32) * 2.0 / head_dim))
    angles = positions.astype(jnp.float32)[:, None] * inverse[None, :]
    cosine = jnp.cos(angles)
    sine = jnp.sin(angles)
    return (jnp.concatenate([cosine, cosine], axis=1), jnp.concatenate([-sine, sine], axis=1))


def slot_positions(ends, slot_count):
    slot_ids = jnp.arange(slot_count, dtype=jnp.int32)
    starts = row_starts(slot_ids, [ends[k] for k in range(ends.shape[0])])
    return slot_ids - starts


def row_starts(row_ids, ends):
    starts = jnp.zeros_like(row_ids)
    for end in ends:
        starts = jnp.where(row_ids >= end, end, starts)
    return jnp.where(row_ids >= ends[-1], row_ids, starts)


def lanes_dot(left, right):
    return lax.dot_general(
        left, right, (((1,), (1,)), ((), ())), preferred_element_type=jnp.float32
    )


def turn_halves(values):
    return pltpu.roll(values, values.shape[-1] // 2, axis=1)


def attend_kernel(
    ends_ref,
    rows_ref,
    query_w_ref,
    kv_w_ref,
    out_w_ref,
    query_gain_ref,
    key_gain_ref,
    cosine_ref,
    sine_ref,
    partial_ref,
    query_ref,
    key_ref,
    value_ref,
    heads_ref,
    log_ref,
    scale_ref,
    keys,
    values,
    total,
    sums,
    *,
    head_dim,
):
    step = pl.program_id(0)
    block = rows_ref.shape[0]
    heads = query_w_ref.shape[1] // head_dim
    ends = [ends_ref[k] for k in range(ends_ref.shape[0])]
    softmax_scale = head_dim ** (-0.5)
    rows = rows_ref[...]
    query_pre = jnp.dot(rows, query_w_ref[...], preferred_element_type=jnp.float32)
    kv_pre = jnp.dot(rows, kv_w_ref[...], preferred_element_type=jnp.float32)
    cosine = cosine_ref[...]
    sine = sine_ref[...]
    lanes = lax.broadcasted_iota(jnp.int32, (block, head_dim), 1)
    scales = jnp.zeros((block, head_dim), jnp.float32)

    def prep(vectors, gain):
        scale = lax.rsqrt(jnp.mean(vectors * vectors, axis=-1, keepdims=True) + eps_norm)
        gained = vectors * scale * gain
        return (gained * cosine + turn_halves(gained) * sine).astype(jnp.bfloat16), scale

    stacked = []
    for h in range(heads):
        cut = slice(h * head_dim, (h + 1) * head_dim)
        low, scale = prep(query_pre[:, cut], query_gain_ref[...])
        query_ref[:, cut] = low
        stacked.append(low)
        scales = jnp.where(lanes == h, scale, scales)
    key_low, scale = prep(kv_pre[:, :head_dim], key_gain_ref[...])
    scale_ref[...] = jnp.where(lanes == heads, scale, scales)
    value_low = kv_pre[:, head_dim:].astype(jnp.bfloat16)
    key_ref[...] = key_low
    value_ref[...] = value_low
    own = pl.ds(pl.multiple_of(step * block, block), block)
    keys[own, :] = key_low
    values[own, :head_dim] = value_low
    values[own, head_dim:] = jnp.ones((block, head_dim), jnp.bfloat16)
    queries = jnp.concatenate(stacked, axis=0)
    row_ids = step * block + lax.broadcasted_iota(jnp.int32, (block, 1), 0)
    starts = row_starts(row_ids, ends)
    total[...] = jnp.zeros_like(total)
    sums[...] = jnp.zeros_like(sums)
    ones = jnp.ones((8, block), jnp.bfloat16)

    def one_block(j, carry):
        there = pl.ds(pl.multiple_of(j * block, block), block)
        scores = lanes_dot(queries, keys[there, :]) * softmax_scale
        column_ids = j * block + lax.broadcasted_iota(jnp.int32, (block, block), 1)
        allowed = (column_ids <= row_ids) & (column_ids >= starts)
        weights = jnp.concatenate(
            [
                jnp.where(allowed, jnp.exp(scores[h * block : (h + 1) * block]), 0.0).astype(
                    jnp.bfloat16
                )
                for h in range(heads)
            ],
            axis=0,
        )
        total[...] += jnp.dot(weights, values[there, :], preferred_element_type=jnp.float32)
        sums[...] += lanes_dot(ones, weights)
        return carry

    first = row_starts(step * block, ends) // block
    lax.fori_loop(first, step + 1, one_block, 0)
    log_ref[0] = jnp.log(sums[...])
    outs = (total[:, :head_dim] / total[:, head_dim:]).astype(jnp.bfloat16)
    for h in range(heads):
        heads_ref[:, h * head_dim : (h + 1) * head_dim] = outs[h * block : (h + 1) * block]
    partial_ref[...] = jnp.dot(
        heads_ref[...], out_w_ref[...], preferred_element_type=jnp.float32
    ).astype(jnp.bfloat16)


def attend_rows(ends, rows, w_query, w_kv, w_out, q_gain, k_gain, cosine, sine):
    slots, width = rows.shape
    head_dim = q_gain.shape[0]
    head_width = w_query.shape[1]
    heads = head_width // head_dim
    block = min(block_slots, slots)
    count = slots // block

    def tile(columns):
        return pl.BlockSpec((block, columns), lambda i: (i, 0))

    def whole(array):
        return pl.BlockSpec(array.shape, lambda i: (0, 0))

    shape = pltpu.HBM
    q_gain = q_gain[None]
    k_gain = k_gain[None]
    return pl.pallas_call(
        functools.partial(attend_kernel, head_dim=head_dim),
        grid=(count,),
        in_specs=[
            pl.BlockSpec(memory_space=pltpu.SMEM),
            tile(width),
            whole(w_query),
            whole(w_kv),
            whole(w_out),
            whole(q_gain),
            whole(k_gain),
            tile(head_dim),
            tile(head_dim),
        ],
        out_specs=[
            tile(width),
            tile(head_width),
            tile(head_dim),
            tile(head_dim),
            tile(head_width),
            pl.BlockSpec((1, 8, heads * block), lambda i: (i, 0, 0)),
            tile(head_dim),
        ],
        out_shape=[
            shape((slots, width), jnp.bfloat16),
            shape((slots, head_width), jnp.bfloat16),
            shape((slots, head_dim), jnp.bfloat16),
            shape((slots, head_dim), jnp.bfloat16),
            shape((slots, head_width), jnp.bfloat16),
            shape((count, 8, heads * block), jnp.float32),
            shape((slots, head_dim), jnp.float32),
        ],
        scratch_shapes=[
            pltpu.VMEM((slots, head_dim), jnp.bfloat16),
            pltpu.VMEM((slots, 2 * head_dim), jnp.bfloat16),
            pltpu.VMEM((heads * block, 2 * head_dim), jnp.float32),
            pltpu.VMEM((8, heads * block), jnp.float32),
        ],
        compiler_params=pltpu.CompilerParams(vmem_limit_bytes=kernel_vmem),
        cost_estimate=pl.CostEstimate(
            flops=2 * slots * width * (2 * head_width + 2 * head_dim)
            + 3 * slots * slots * head_width,
            bytes_accessed=4 * slots * width + 4 * width * head_width,
            transcendentals=slots * slots * heads // 2,
        ),
        name="attend_rows",
    )(ends, rows, w_query, w_kv, w_out, q_gain, k_gain, cosine, sine)


def attend_back_kernel(
    ends_ref,
    grad_ref,
    out_w_ref,
    query_ref,
    heads_ref,
    key_ref,
    value_ref,
    log_ref,
    scale_ref,
    query_gain_ref,
    key_gain_ref,
    cosine_ref,
    sine_ref,
    grad_query_ref,
    grad_kv_ref,
    grad_query_gain_ref,
    grad_key_gain_ref,
    grad_keys,
    grad_values,
    grad_queries,
    *,
    head_dim,
):
    step = pl.program_id(0)
    block = query_ref.shape[0]
    heads = query_ref.shape[1] // head_dim
    ends = [ends_ref[k] for k in range(ends_ref.shape[0])]
    softmax_scale = head_dim ** (-0.5)

    @pl.when(step == 0)
    def _():
        grad_keys[...] = jnp.zeros_like(grad_keys)
        grad_values[...] = jnp.zeros_like(grad_values)
        grad_query_gain_ref[...] = jnp.zeros_like(grad_query_gain_ref)

    grad_heads = lanes_dot(grad_ref[...], out_w_ref[...]).astype(jnp.bfloat16)
    query = query_ref[...]
    out = heads_ref[...]
    cuts = [slice(h * head_dim, (h + 1) * head_dim) for h in range(heads)]
    queries = jnp.concatenate([query[:, cut] for cut in cuts], axis=0)
    grads = jnp.concatenate([grad_heads[:, cut] for cut in cuts], axis=0)
    outs = jnp.concatenate([out[:, cut] for cut in cuts], axis=0)
    products = grads.astype(jnp.float32) * outs.astype(jnp.float32)
    high = products.astype(jnp.bfloat16)
    rest = (products - high.astype(jnp.float32)).astype(jnp.bfloat16)
    ones = jnp.ones((8, head_dim), jnp.bfloat16)
    centre = (lanes_dot(ones, high) + lanes_dot(ones, rest))[:1]
    logs = log_ref[0, :1, :]
    column_ids = step * block + lax.broadcasted_iota(jnp.int32, (1, block), 1)
    starts = row_starts(column_ids, ends)
    grad_queries[...] = jnp.zeros_like(grad_queries)

    def one_block(j, carry):
        there = pl.ds(pl.multiple_of(j * block, block), block)
        key = key_ref[there, :]
        value = value_ref[there, :]
        scores = lanes_dot(key, queries) * softmax_scale - logs
        grad_probs = lanes_dot(value, grads) - centre
        row_ids = j * block + lax.broadcasted_iota(jnp.int32, (block, block), 0)
        allowed = (row_ids <= column_ids) & (row_ids >= starts)
        probs = jnp.concatenate(
            [
                jnp.where(allowed, jnp.exp(scores[:, h * block : (h + 1) * block]), 0.0)
                for h in range(heads)
            ],
            axis=1,
        )
        probs_low = probs.astype(jnp.bfloat16)
        grad_scores = (probs * grad_probs).astype(jnp.bfloat16)
        grad_values[there, :] += jnp.dot(probs_low, grads, preferred_element_type=jnp.float32)
        grad_keys[there, :] += jnp.dot(grad_scores, queries, preferred_element_type=jnp.float32)
        grad_queries[...] += lax.dot_general(
            grad_scores, key, (((0,), (0,)), ((), ())), preferred_element_type=jnp.float32
        )
        return carry

    first = row_starts(step * block, ends) // block
    lax.fori_loop(first, step + 1, one_block, 0)

    def prep_back(grad, low, gain, cosine, sine, scale):
        grad = grad * softmax_scale
        low = low.astype(jnp.float32)
        grad_gained = grad * cosine - turn_halves(grad) * sine
        normed = (low * cosine - turn_halves(low) * sine) / gain
        grad_gain = jnp.sum(grad_gained * normed, axis=0, keepdims=True)
        grad_normed = grad_gained * gain
        mean = jnp.mean(grad_normed * normed, axis=-1, keepdims=True)
        return scale * (grad_normed - normed * mean), grad_gain

    own = pl.ds(pl.multiple_of(step * block, block), block)
    cosine = cosine_ref[own, :]
    sine = sine_ref[own, :]
    scales = scale_ref[own, :]
    for h, cut in enumerate(cuts):
        grad_pre, grad_gain = prep_back(
            grad_queries[h * block : (h + 1) * block, :],
            query[:, cut],
            query_gain_ref[...],
            cosine,
            sine,
            scales[:, h : h + 1],
        )
        grad_query_ref[:, cut] = grad_pre.astype(jnp.bfloat16)
        grad_query_gain_ref[...] += grad_gain

    @pl.when(step == pl.num_programs(0) - 1)
    def _():
        grad_pre, grad_gain = prep_back(
            grad_keys[...],
            key_ref[...],
            key_gain_ref[...],
            cosine_ref[...],
            sine_ref[...],
            scale_ref[:, heads : heads + 1],
        )
        grad_kv_ref[:, :head_dim] = grad_pre.astype(jnp.bfloat16)
        grad_kv_ref[:, head_dim:] = grad_values[...].astype(jnp.bfloat16)
        grad_key_gain_ref[...] = grad_gain


def attend_rows_back(
    ends, grad, w_out, query, heads_low, key, value, logs, scales, q_gain, k_gain, cosine, sine
):
    slots, width = grad.shape
    head_dim = q_gain.shape[0]
    head_width = query.shape[1]
    heads = head_width // head_dim
    block = min(block_slots, slots)
    count = slots // block

    def tile(columns):
        return pl.BlockSpec((block, columns), lambda i: (i, 0))

    def whole(array):
        return pl.BlockSpec(array.shape, lambda i: (0, 0))

    shape = pltpu.HBM
    q_gain = q_gain[None]
    k_gain = k_gain[None]
    return pl.pallas_call(
        functools.partial(attend_back_kernel, head_dim=head_dim),
        grid=(count,),
        in_specs=[
            pl.BlockSpec(memory_space=pltpu.SMEM),
            tile(width),
            whole(w_out),
            tile(head_width),
            tile(head_width),
            whole(key),
            whole(value),
            pl.BlockSpec((1, 8, heads * block), lambda i: (i, 0, 0)),
            whole(scales),
            whole(q_gain),
            whole(k_gain),
            whole(cosine),
            whole(sine),
        ],
        out_specs=[
            tile(head_width),
            pl.BlockSpec((slots, 2 * head_dim), lambda i: (0, 0)),
            pl.BlockSpec((1, head_dim), lambda i: (0, 0)),
            pl.BlockSpec((1, head_dim), lambda i: (0, 0)),
        ],
        out_shape=[
            shape((slots, head_width), jnp.bfloat16),
            shape((slots, 2 * head_dim), jnp.bfloat16),
            shape((1, head_dim), jnp.float32),
            shape((1, head_dim), jnp.float32),
        ],
        scratch_shapes=[
            pltpu.VMEM((slots, head_dim), jnp.float32),
            pltpu.VMEM((slots, head_dim), jnp.float32),
            pltpu.VMEM((heads * block, head_dim), jnp.float32),
        ],
        compiler_params=pltpu.CompilerParams(vmem_limit_bytes=kernel_vmem),
        cost_estimate=pl.CostEstimate(
            flops=2 * slots * width * head_width + 6 * slots * slots * head_width,
            bytes_accessed=2 * slots * width + 2 * width * head_width,
            transcendentals=slots * slots * heads // 2,
        ),
        name="attend_rows_back",
    )(ends, grad, w_out, query, heads_low, key, value, logs, scales, q_gain, k_gain, cosine, sine)


def transposed_times(left, right):
    return lax.dot_general(
        left, right, (((0,), (0,)), ((), ())), preferred_element_type=jnp.float32
    )


plane_axes = ("row", "col")


def move_plane(parts):
    return lax.all_to_all(parts, plane_axes, split_axis=0, concat_axis=0, tiled=True)


def rotate(block, axis, step):
    size = lax.axis_size(axis)
    return lax.ppermute(block, axis, [(i, (i + step) % size) for i in range(size)])


def gather_planes(block):
    planes = lax.axis_size("expert")
    return jnp.stack([block] + [rotate(block, "expert", k) for k in range(1, planes)], axis=0)


def return_planes(parts):
    return [parts[0]] + [rotate(parts[k], "expert", -k) for k in range(1, parts.shape[0])]


def together(*values):
    return lax.optimization_barrier(values)


def move_all(parts):
    return lax.all_to_all(
        parts, ("expert",) + plane_axes, split_axis=0, concat_axis=0, tiled=True
    )


def sum_all(values):
    devices = lax.axis_size(("expert",) + plane_axes)
    padded = jnp.pad(values, (0, -values.shape[0] % (devices * 128)))
    total = jnp.sum(move_all(padded.reshape(devices, -1, 128)), axis=0)
    return move_all(jnp.broadcast_to(total[None], (devices,) + total.shape)).reshape(-1)


def line_step(value, step, hop):
    planes = lax.axis_size("expert")
    if hop > 0:
        pairs = [(i, i + 1) for i in range(*step)]
    else:
        pairs = [(planes - 1 - i, planes - 2 - i) for i in range(*step)]
    return lax.ppermute(value, "expert", pairs)


def sum_planes(product):
    planes = lax.axis_size("expert")
    plane = lax.axis_index("expert")
    shares = product.reshape(planes, -1, product.shape[1])

    def share(k):
        return lax.dynamic_index_in_dim(shares, (plane + k) % planes, 0, keepdims=False)

    arrived = [rotate(share(k), "expert", k) for k in range(1, planes)]
    total = share(0).astype(jnp.float32)
    for part in arrived:
        total = total + part.astype(jnp.float32)
    return total.astype(product.dtype)


def spread_planes(total):
    planes = lax.axis_size("expert")
    arrived = []
    for hop in (1, -1):
        message = total
        for k in range(1, planes):
            message = line_step(message, (k - 1, planes - 1), hop)
            arrived.append((k, hop, message))
    arrived.sort(key=lambda entry: -entry[0])
    return [message for _, _, message in arrived] + [total]


def in_plane_order(parts):
    planes = lax.axis_size("expert")
    plane = lax.axis_index("expert")
    rows = parts[0].shape[0]
    result = jnp.zeros((planes * rows, parts[0].shape[1]), jnp.float32)
    places = [plane - hop * k for k in range(planes - 1, 0, -1) for hop in (1, -1)] + [plane]
    for place, part in zip(places, parts):
        result = lax.dynamic_update_slice_in_dim(
            result, part.astype(jnp.float32), jnp.clip(place, 0, planes - 1) * rows, axis=0
        )
    return result


def scatter_cols(product):
    col = lax.axis_index("col")
    cols = lax.axis_size("col")
    moved = [rotate(product((col + k) % cols).astype(jnp.bfloat16), "col", k) for k in range(1, cols)]
    total = product(col)
    for part in moved:
        total = total + part.astype(jnp.float32)
    return total.astype(jnp.bfloat16)


def scatter_rows(parts):
    row = lax.axis_index("row")
    rows = lax.axis_size("row")

    def piece(k):
        return lax.dynamic_index_in_dim(parts, (row + k) % rows, 0, keepdims=False)

    arrived = [rotate(piece(k), "row", k) for k in range(1, rows)]
    result = piece(0).astype(jnp.float32)
    for part in arrived:
        result = result + part.astype(jnp.float32)
    return result


def expert_kernel(ids_ref, router_ref, gate_ref, up_ref, down_ref, *refs, count, experts):
    rows_refs = refs[:count]
    grads_refs = refs[count : 2 * count]
    sends = refs[2 * count : 3 * count]
    weighted = refs[3 * count : 4 * count]
    rows_out, grads_out, hidden_out, grad_gate_out, grad_up_out = refs[4 * count :]
    width = rows_refs[1].shape[1]
    cuts = [slice(i * width, (i + 1) * width) for i in range(count)]
    rows = [ref[...] for ref in rows_refs]
    chosen = grads_refs[0][:, width:].astype(jnp.float32) > 0.5
    lanes = lax.broadcasted_iota(jnp.int32, chosen.shape, 1)

    def times(weights_ref):
        return sum(
            jnp.dot(part, weights_ref[cut, :], preferred_element_type=jnp.float32)
            for part, cut in zip(rows, cuts)
        )

    logits = times(router_ref)
    top = jnp.max(jnp.where(chosen, logits, -3e38), axis=1, keepdims=True)
    raised = jnp.where(chosen, jnp.exp(jnp.where(chosen, logits - top, 0.0)), 0.0)
    own = jnp.sum(jnp.where(lanes == ids_ref[0], raised, 0.0), axis=1, keepdims=True)
    gates = own / jnp.maximum(jnp.sum(raised, axis=1, keepdims=True), 1e-30)
    gate_pre = times(gate_ref)
    up_pre = times(up_ref)
    sigmoid = 1.0 / (1.0 + jnp.exp(-gate_pre))
    silu = gate_pre * sigmoid
    hidden = (silu * up_pre).astype(jnp.bfloat16)
    hidden_out[...] = hidden
    dots = jnp.zeros(gates.shape, jnp.float32)
    grad_hidden = jnp.zeros(gate_pre.shape, jnp.float32)
    for i, cut in enumerate(cuts):
        out = jnp.dot(hidden, down_ref[:, cut], preferred_element_type=jnp.float32)
        out = out.astype(jnp.bfloat16).astype(jnp.float32)
        grads = grads_refs[i][:, :width].astype(jnp.float32)
        dots = dots + jnp.sum(out * grads, axis=1, keepdims=True)
        weighted[i][...] = (out * gates).astype(jnp.bfloat16)
        grads_low = (grads * gates).astype(jnp.bfloat16)
        grads_out[:, cut] = grads_low
        rows_out[:, cut] = rows[i]
        grad_hidden = grad_hidden + lanes_dot(grads_low, down_ref[:, cut])
    grad_gate = (grad_hidden * up_pre * sigmoid * (1.0 + gate_pre * (1.0 - sigmoid))).astype(
        jnp.bfloat16
    )
    grad_up = (grad_hidden * silu).astype(jnp.bfloat16)
    grad_gate_out[...] = grad_gate
    grad_up_out[...] = grad_up
    for i, cut in enumerate(cuts):
        sends[i][:, :width] = (
            lanes_dot(grad_gate, gate_ref[cut, :]) + lanes_dot(grad_up, up_ref[cut, :])
        ).astype(jnp.bfloat16)
    dots_high = dots.astype(jnp.bfloat16).astype(jnp.float32)
    side = jnp.where(lanes == ids_ref[1], dots_high, 0.0) + jnp.where(
        lanes == ids_ref[1] + experts, dots - dots_high, 0.0
    )
    sends[0][:, width:] = side.astype(jnp.bfloat16)


def expert_rows(ids, w_router, w_gate, w_up, w_down, rows, grads, plane_size):
    count = len(rows)
    slots, width = rows[0].shape
    model_width, hidden = w_gate.shape
    side = grads[0].shape[1] - width
    block = slots // expert_steps

    def tile(columns):
        return pl.BlockSpec((block, columns), lambda i: (i, 0))

    def whole(array):
        return pl.BlockSpec(array.shape, lambda i: (0, 0), pipeline_mode=pl.Buffered(1))

    def shape(columns):
        return pltpu.HBM((slots, columns), jnp.bfloat16)

    sides = [width + side] + [width] * (count - 1)
    outs = sides + [width] * count + [model_width, model_width, hidden, hidden, hidden]
    flops = 2 * slots * model_width * hidden * 6
    return pl.pallas_call(
        functools.partial(expert_kernel, count=count, experts=plane_size),
        grid=(expert_steps,),
        in_specs=[pl.BlockSpec(memory_space=pltpu.SMEM)]
        + [whole(array) for array in (w_router, w_gate, w_up, w_down)]
        + [tile(width)] * count
        + [tile(columns) for columns in sides],
        out_specs=[tile(columns) for columns in outs],
        out_shape=[shape(columns) for columns in outs],
        compiler_params=pltpu.CompilerParams(vmem_limit_bytes=expert_vmem),
        cost_estimate=pl.CostEstimate(
            flops=flops, bytes_accessed=6 * model_width * hidden, transcendentals=slots * hidden
        ),
        name="expert_rows",
    )(ids, w_router, w_gate, w_up, w_down, *rows, *grads)


def local(
    layer_input,
    norm_attn,
    w_query,
    w_key,
    w_value,
    q_gain,
    k_gain,
    w_out,
    norm_moe,
    w_router,
    w_gate,
    w_up,
    w_down,
    seq_lengths,
    routes,
    out_grad,
):
    tok_dev = layer_input.shape[0]
    model_width = layer_input.shape[1]
    group_tok = tok_dev * lax.axis_size(("row", "col"))
    head_dim = q_gain.shape[0]
    experts = w_router.shape[1]
    top_count = routes.shape[1]
    capacity = tok_dev * top_count * 17 // (16 * experts)
    planes = lax.axis_size("expert")
    plane_size = lax.axis_size(plane_axes)
    plane_index = lax.axis_index("expert")
    plane_cap = planes * capacity
    chosen_here = jnp.any(
        routes[:, :, None] == jnp.arange(experts, dtype=jnp.int32)[None, None, :], axis=1
    )
    plane_routes = gather_planes(routes.T)
    plane_experts = plane_index * plane_size + jnp.arange(plane_size, dtype=jnp.int32)
    chosen_plane = jnp.any(
        plane_routes[None] == plane_experts[:, None, None, None], axis=2
    )
    token_ids = jnp.arange(tok_dev, dtype=jnp.int32)
    earlier = (token_ids[:, None] < token_ids[None, :]).astype(jnp.bfloat16)
    slot_rank = jnp.dot(
        chosen_plane.astype(jnp.bfloat16).reshape(plane_size * planes, tok_dev),
        earlier,
        preferred_element_type=jnp.float32,
    ).astype(jnp.int32).reshape(plane_size, planes, tok_dev)
    plane_slot = jnp.where(
        chosen_plane,
        slot_rank + (jnp.arange(planes, dtype=jnp.int32) * capacity)[None, :, None],
        -1,
    ).reshape(plane_size, 1, planes * tok_dev)
    dispatch = (
        plane_slot == jnp.arange(plane_cap, dtype=jnp.int32)[None, :, None]
    ).astype(jnp.bfloat16)
    chosen_all = jnp.any(
        plane_routes[:, :, :, None] == jnp.arange(experts, dtype=jnp.int32), axis=1
    ).reshape(planes * tok_dev, experts).astype(jnp.bfloat16)

    def gather_rows(block):
        return gather_planes(block).reshape(planes * tok_dev, block.shape[1])

    def select_slots(rows_all):
        return jnp.dot(
            dispatch.reshape(plane_size * plane_cap, -1),
            rows_all,
            preferred_element_type=jnp.float32,
        ).astype(jnp.bfloat16)

    def to_plane(slot_values):
        width = slot_values.shape[1]
        moved = move_plane(slot_values.reshape(plane_size, plane_cap, width))
        return moved.reshape(plane_size * plane_cap, width)

    chunk_width = model_width // chunk_count
    chunks = [slice(i * chunk_width, (i + 1) * chunk_width) for i in range(chunk_count)]
    side_width = 128
    grad_planes = [gather_rows(out_grad[:, cut]) for cut in chunks]
    grad_planes[0] = jnp.concatenate(
        [grad_planes[0], jnp.pad(chosen_all, ((0, 0), (0, side_width - experts)))], axis=1
    )
    slot_sends = [select_slots(part) for part in grad_planes]
    def gates_of(all_logits, chosen):
        top = jnp.max(jnp.where(chosen, all_logits, -3e38), axis=1, keepdims=True)
        raised = jnp.where(chosen, jnp.exp(jnp.where(chosen, all_logits - top, 0.0)), 0.0)
        return raised / jnp.maximum(jnp.sum(raised, axis=1, keepdims=True), 1e-30)

    input_rows = layer_input.astype(jnp.float32)
    normed_one, norm_one_back = jax.vjp(rms_scale, input_rows, norm_attn)
    normed_low = normed_one.astype(jnp.bfloat16)
    group_rows = lax.all_gather(normed_low, ("row", "col"), axis=0, tiled=True)
    ends = jnp.cumsum(seq_lengths[0], dtype=jnp.int32)
    cosine_table, sine_table = rope_tables(slot_positions(ends, group_tok), head_dim)
    key_value_w = jnp.concatenate([w_key, w_value], axis=1)
    group_rows, slot_sends[0], cosine_table, sine_table, key_value_w = together(
        group_rows, slot_sends[0], cosine_table, sine_table, key_value_w
    )
    grad_slot_chunks = [to_plane(slot_sends[0])]
    attn_partial, query_low, key_low, value_low, heads_low, log_totals, head_scales = attend_rows(
        ends, group_rows, w_query, key_value_w, w_out, q_gain, k_gain, cosine_table, sine_table
    )
    attn_partial, grad_slot_chunks[0] = together(attn_partial, grad_slot_chunks[0])
    col_parts = attn_partial.reshape(-1, lax.axis_size("col"), tok_dev, model_width)
    attn_rows = scatter_rows(
        scatter_cols(lambda place: lax.dynamic_index_in_dim(col_parts, place, 1, keepdims=False))
    )
    attn_rows, *late_sends = together(attn_rows, *slot_sends[1:])
    grad_slot_chunks += [to_plane(part) for part in late_sends]
    attn_rows = attn_rows.astype(jnp.float32)
    mixed_rows = input_rows + attn_rows
    normed_two, norm_two_back = jax.vjp(rms_scale, mixed_rows, norm_moe)
    moe_input = normed_two.astype(jnp.bfloat16)
    router_logits = jnp.dot(moe_input, w_router, preferred_element_type=jnp.float32)
    source_gates = gates_of(router_logits, chosen_here)

    moe_planes = [gather_rows(moe_input[:, cut]) for cut in chunks]
    moe_sends = [select_slots(part) for part in moe_planes]
    moe_sends[0], *grad_slot_chunks[1:] = together(moe_sends[0], *grad_slot_chunks[1:])
    slot_chunks = [to_plane(part) for part in moe_sends]
    place = lax.axis_index(plane_axes)
    ids = jnp.stack([plane_index * plane_size + place, place]).astype(jnp.int32)
    expert_outs = expert_rows(
        ids,
        jnp.pad(w_router, ((0, 0), (0, side_width - experts))),
        w_gate[0],
        w_up[0],
        w_down[0],
        slot_chunks,
        grad_slot_chunks,
        plane_size,
    )
    grad_sends = expert_outs[:chunk_count]
    out_sends = expert_outs[chunk_count : 2 * chunk_count]
    moe_slots, grad_out_slots, hidden_low, grad_gate_pre, grad_up_pre = expert_outs[
        2 * chunk_count :
    ]

    def to_source(returned):
        summed = lax.dot_general(
            dispatch.reshape(plane_size * plane_cap, -1),
            returned,
            (((0,), (0,)), ((), ())),
            preferred_element_type=jnp.float32,
        ).astype(jnp.bfloat16)
        return return_planes(summed.reshape(planes, tok_dev, returned.shape[1]))

    def add_parts(parts):
        return sum(part.astype(jnp.float32) for part in parts)

    grad_rows = out_grad.astype(jnp.float32)
    grad_down = transposed_times(hidden_low, grad_out_slots)
    grad_gate = transposed_times(moe_slots, grad_gate_pre)
    grad_up = transposed_times(moe_slots, grad_up_pre)
    grad_returns = [to_plane(part) for part in grad_sends]
    grad_returns[0], grad_down = together(grad_returns[0], grad_down)
    grad_returns[-1], grad_gate, *out_sends = together(grad_returns[-1], grad_gate, *out_sends)
    out_returns = [to_plane(out_sends[0])]
    grad_parts = [to_source(part) for part in grad_returns]
    grad_parts[-1][-1], grad_up = together(grad_parts[-1][-1], grad_up)
    side_parts = jnp.stack(
        [part[:, chunk_width:].astype(jnp.float32) for part in grad_parts[0]], axis=0
    )
    dot_parts = side_parts[:, :, :plane_size] + side_parts[:, :, plane_size : 2 * plane_size]
    dot_parts = lax.dynamic_slice_in_dim(
        jnp.concatenate([dot_parts, dot_parts], axis=0), planes - plane_index, planes, axis=0
    )
    grad_gates = jnp.swapaxes(dot_parts, 0, 1).reshape(tok_dev, experts)
    grad_logits = source_gates * (
        grad_gates - jnp.sum(source_gates * grad_gates, axis=1, keepdims=True)
    )
    grad_parts[0] = [part[:, :chunk_width] for part in grad_parts[0]]
    grad_moe_input = jnp.concatenate([add_parts(parts) for parts in grad_parts], axis=1)
    grad_router = lax.dot_general(
        grad_logits,
        moe_input.astype(jnp.float32),
        (((0,), (0,)), ((), ())),
        precision=highest,
        preferred_element_type=jnp.float32,
    )
    grad_moe_input = grad_moe_input + jnp.einsum(
        "te,de->td", grad_logits, w_router, precision=highest, preferred_element_type=jnp.float32
    )
    grad_mixed_norm, grad_norm_moe = norm_two_back(grad_moe_input)
    grad_mixed = grad_rows + grad_mixed_norm
    grad_attn_low = grad_mixed.astype(jnp.bfloat16)
    grad_attn_low, out_returns[0] = together(grad_attn_low, out_returns[0])
    grad_group = lax.all_gather(grad_attn_low, ("row", "col"), axis=0, tiled=True)
    out_first = add_parts(to_source(out_returns[0]))
    grad_group, out_first, *out_late = together(grad_group, out_first, *out_sends[1:])
    out_returns += [to_plane(part) for part in out_late]
    grad_out_proj = transposed_times(heads_low, grad_group).astype(jnp.bfloat16)
    grad_out_proj, grad_group = together(grad_out_proj, grad_group)
    out_share = sum_planes(grad_out_proj)
    grad_query_low, grad_kv, grad_q_gain, grad_k_gain = attend_rows_back(
        ends,
        grad_group,
        w_out,
        query_low,
        heads_low,
        key_low,
        value_low,
        log_totals,
        head_scales,
        q_gain,
        k_gain,
        cosine_table,
        sine_table,
    )
    grad_query_low, grad_kv, out_share = together(grad_query_low, grad_kv, out_share)
    grad_query = transposed_times(group_rows, grad_query_low)
    grad_key_value = transposed_times(group_rows, grad_kv)
    norm_terms = (
        jnp.sum(grad_query * w_query.astype(jnp.float32), axis=1)
        + jnp.sum(grad_key_value * key_value_w.astype(jnp.float32), axis=1)
    ) / norm_attn
    cols = lax.axis_size("col")
    col = lax.axis_index("col")
    kv_low = grad_key_value.astype(jnp.bfloat16).reshape(cols, -1, 2 * head_dim)
    kv_part = lax.dynamic_index_in_dim(kv_low, col, 0, keepdims=False).astype(jnp.float32)
    for k in range(1, cols):
        kv_part = kv_part + rotate(
            lax.dynamic_index_in_dim(kv_low, (col + k) % cols, 0, keepdims=False), "col", k
        ).astype(jnp.float32)
    query_kv = jnp.concatenate(
        [
            grad_query.astype(jnp.bfloat16),
            kv_part.astype(jnp.bfloat16).reshape(-1, grad_query.shape[1]),
        ],
        axis=0,
    )
    query_kv = lax.psum(query_kv, "expert")
    left_parts = jnp.concatenate([grad_query_low, grad_kv], axis=1).reshape(
        -1, cols, tok_dev, grad_query_low.shape[1] + 2 * head_dim
    )
    right_all = jnp.concatenate([w_query, key_value_w], axis=1)

    def grad_normed_rows(place):
        left = lax.dynamic_index_in_dim(left_parts, place, 1, keepdims=False)
        return lax.dot_general(
            left, right_all, (((2,), (1,)), ((), ())), preferred_element_type=jnp.float32
        )

    left_parts, *out_returns[1:] = together(left_parts, *out_returns[1:])
    out_shares = spread_planes(out_share)
    out_parts = [out_first] + [add_parts(to_source(part)) for part in out_returns[1:]]
    col_sums = scatter_cols(grad_normed_rows)
    summed_values = jnp.concatenate(
        [grad_router.reshape(-1), grad_norm_moe, norm_terms, grad_q_gain[0], grad_k_gain[0]]
    )
    col_sums, summed_values = together(col_sums, summed_values)
    sums = sum_all(summed_values)
    grad_normed = scatter_rows(col_sums)
    grad_normed, sums, query_kv, *out_parts = together(grad_normed, sums, query_kv, *out_parts)
    out_rows = (mixed_rows + jnp.concatenate(out_parts, axis=1)).astype(jnp.bfloat16)
    grad_out_proj = in_plane_order(out_shares)
    places = (0, experts * model_width, model_width, model_width, head_dim, head_dim)
    ends_at = [sum(places[: k + 1]) for k in range(len(places))]
    grad_router, grad_norm_moe, grad_norm_attn, grad_q_gain, grad_k_gain = [
        sums[low:high] for low, high in zip(ends_at[:-1], ends_at[1:])
    ]
    grad_router = grad_router.reshape(experts, model_width).T
    grad_query = query_kv[:model_width].astype(jnp.float32)
    kv_part = query_kv[model_width:].reshape(-1, 2 * head_dim)
    kv_parts = jnp.stack([kv_part] + [rotate(kv_part, "col", k) for k in range(1, cols)], axis=0)
    kv_parts = lax.dynamic_slice_in_dim(
        jnp.concatenate([kv_parts[::-1], kv_parts[::-1]], axis=0), cols - 1 - col, cols, axis=0
    )
    kv_full = kv_parts.reshape(model_width, 2 * head_dim).astype(jnp.float32)
    grad_key = kv_full[:, :head_dim]
    grad_value = kv_full[:, head_dim:]
    grad_input_norm = norm_one_back(grad_normed)[0]
    grad_x = (grad_mixed + grad_input_norm).astype(jnp.bfloat16)
    return (
        out_rows,
        grad_x,
        grad_norm_attn,
        grad_query,
        grad_key,
        grad_value,
        grad_q_gain,
        grad_k_gain,
        grad_out_proj,
        grad_norm_moe,
        grad_router,
        grad_gate[None],
        grad_up[None],
        grad_down[None],
    )


def solution(mesh):
    placed = (
        P(("expert", "row", "col"), None),
        P(),
        P(None, ("row", "col")),
        P(None, "row"),
        P(None, "row"),
        P(),
        P(),
        P(("row", "col"), None),
        P(),
        P(),
        P(("expert", "row", "col"), None, None),
        P(("expert", "row", "col"), None, None),
        P(("expert", "row", "col"), None, None),
        P("expert", None),
        P(("expert", "row", "col"), None),
        P(("expert", "row", "col"), None),
    )
    return jax.shard_map(
        local,
        mesh=mesh,
        in_specs=placed,
        out_specs=(
            P(("expert", "row", "col"), None),
            P(("expert", "row", "col"), None),
            P(),
            P(None, ("row", "col")),
            P(None, "row"),
            P(None, "row"),
            P(),
            P(),
            P(("row", "col"), None),
            P(),
            P(),
            P(("expert", "row", "col"), None, None),
            P(("expert", "row", "col"), None, None),
            P(("expert", "row", "col"), None, None),
        ),
        check_vma=False,
    )
```

```python
import functools

import jax
import jax.numpy as jnp
from jax import lax
from jax.experimental import pallas as pl
from jax.experimental.pallas import tpu as pltpu
from jax.sharding import PartitionSpec as P

eps_norm = 1e-06
rope_base = 1000000.0
highest = lax.Precision.HIGHEST
chunk_count = 2
expert_steps = 2
expert_vmem = 56 * 1024 * 1024
kernel_vmem = 40 * 1024 * 1024


def rms_scale(values, norm_gain):
    return (
        values * lax.rsqrt(jnp.mean(values * values, axis=-1, keepdims=True) + eps_norm) * norm_gain
    )


def rope_tables(positions, head_dim):
    half_dim = head_dim // 2
    inverse = rope_base ** (-(jnp.arange(half_dim, dtype=jnp.float32) * 2.0 / head_dim))
    angles = positions.astype(jnp.float32)[:, None] * inverse[None, :]
    cosine = jnp.cos(angles)
    sine = jnp.sin(angles)
    return (jnp.concatenate([cosine, cosine], axis=1), jnp.concatenate([-sine, sine], axis=1))


def slot_positions(ends, slot_count):
    slot_ids = jnp.arange(slot_count, dtype=jnp.int32)
    starts = row_starts(slot_ids, [ends[k] for k in range(ends.shape[0])])
    return slot_ids - starts


def row_starts(row_ids, ends):
    starts = jnp.zeros_like(row_ids)
    for end in ends:
        starts = jnp.where(row_ids >= end, end, starts)
    return jnp.where(row_ids >= ends[-1], row_ids, starts)


def lanes_dot(left, right):
    return lax.dot_general(
        left, right, (((1,), (1,)), ((), ())), preferred_element_type=jnp.float32
    )


def turn_halves(values):
    return pltpu.roll(values, values.shape[-1] // 2, axis=1)


def keep(array):
    return pltpu.with_memory_space_constraint(array, pltpu.HBM)


def attend_kernel(
    ends_ref,
    place_ref,
    rows_ref,
    query_w_ref,
    kv_w_ref,
    out_w_ref,
    query_gain_ref,
    key_gain_ref,
    cosine_ref,
    sine_ref,
    kept_ref,
    sent_ref,
    query_ref,
    key_ref,
    value_ref,
    heads_ref,
    log_ref,
    scale_ref,
    keys,
    values,
    total,
    sums,
    partial,
    *,
    head_dim,
):
    step = pl.program_id(0)
    block = rows_ref.shape[0]
    heads = query_w_ref.shape[1] // head_dim
    ends = [ends_ref[k] for k in range(ends_ref.shape[0])]
    softmax_scale = head_dim ** (-0.5)
    rows = rows_ref[...]
    query_pre = jnp.dot(rows, query_w_ref[...], preferred_element_type=jnp.float32)
    kv_pre = jnp.dot(rows, kv_w_ref[...], preferred_element_type=jnp.float32)
    cosine = cosine_ref[...]
    sine = sine_ref[...]
    lanes = lax.broadcasted_iota(jnp.int32, (block, head_dim), 1)
    scales = jnp.zeros((block, head_dim), jnp.float32)

    def prep(vectors, gain):
        scale = lax.rsqrt(jnp.mean(vectors * vectors, axis=-1, keepdims=True) + eps_norm)
        gained = vectors * scale * gain
        return (gained * cosine + turn_halves(gained) * sine).astype(jnp.bfloat16), scale

    stacked = []
    for h in range(heads):
        cut = slice(h * head_dim, (h + 1) * head_dim)
        low, scale = prep(query_pre[:, cut], query_gain_ref[...])
        query_ref[:, cut] = low
        stacked.append(low)
        scales = jnp.where(lanes == h, scale, scales)
    key_low, scale = prep(kv_pre[:, :head_dim], key_gain_ref[...])
    scale_ref[...] = jnp.where(lanes == heads, scale, scales)
    value_low = kv_pre[:, head_dim:].astype(jnp.bfloat16)
    key_ref[...] = key_low
    value_ref[...] = value_low
    own = pl.ds(pl.multiple_of(step * block, block), block)
    keys[own, :] = key_low
    values[own, :head_dim] = value_low
    values[own, head_dim:] = jnp.ones((block, head_dim), jnp.bfloat16)
    queries = jnp.concatenate(stacked, axis=0)
    row_ids = step * block + lax.broadcasted_iota(jnp.int32, (block, 1), 0)
    starts = row_starts(row_ids, ends)
    total[...] = jnp.zeros_like(total)
    sums[...] = jnp.zeros_like(sums)
    ones = jnp.ones((8, block), jnp.bfloat16)

    def one_block(j, carry):
        there = pl.ds(pl.multiple_of(j * block, block), block)
        scores = lanes_dot(queries, keys[there, :]) * softmax_scale
        column_ids = j * block + lax.broadcasted_iota(jnp.int32, (block, block), 1)
        allowed = (column_ids <= row_ids) & (column_ids >= starts)
        weights = jnp.concatenate(
            [
                jnp.where(allowed, jnp.exp(scores[h * block : (h + 1) * block]), 0.0).astype(
                    jnp.bfloat16
                )
                for h in range(heads)
            ],
            axis=0,
        )
        total[...] += jnp.dot(weights, values[there, :], preferred_element_type=jnp.float32)
        sums[...] += lanes_dot(ones, weights)
        return carry

    first = row_starts(step * block, ends) // block
    lax.fori_loop(first, step + 1, one_block, 0)
    log_ref[0] = jnp.log(sums[...])
    outs = (total[:, :head_dim] / total[:, head_dim:]).astype(jnp.bfloat16)
    for h in range(heads):
        heads_ref[:, h * head_dim : (h + 1) * head_dim] = outs[h * block : (h + 1) * block]
    partial[...] = jnp.dot(
        heads_ref[...], out_w_ref[...], preferred_element_type=jnp.float32
    ).astype(jnp.bfloat16)
    share = kept_ref.shape[0]
    kept = pl.multiple_of(place_ref[0] * share, share)
    sent = pl.multiple_of((1 - place_ref[0]) * share, share)
    kept_ref[...] = partial[pl.ds(kept, share), :]
    sent_ref[...] = partial[pl.ds(sent, share), :]


def attend_rows(ends, place, rows, w_query, w_kv, w_out, q_gain, k_gain, cosine, sine, block):
    slots, width = rows.shape
    head_dim = q_gain.shape[0]
    head_width = w_query.shape[1]
    heads = head_width // head_dim
    count = slots // block

    def tile(columns):
        return pl.BlockSpec((block, columns), lambda i: (i, 0))

    def whole(array):
        return pl.BlockSpec(array.shape, lambda i: (0, 0))

    def half(columns):
        return pl.BlockSpec((block // 2, columns), lambda i: (i, 0))

    shape = pltpu.HBM
    q_gain = q_gain[None]
    k_gain = k_gain[None]
    return pl.pallas_call(
        functools.partial(attend_kernel, head_dim=head_dim),
        grid=(count,),
        in_specs=[
            pl.BlockSpec(memory_space=pltpu.SMEM),
            pl.BlockSpec(memory_space=pltpu.SMEM),
            tile(width),
            whole(w_query),
            whole(w_kv),
            whole(w_out),
            whole(q_gain),
            whole(k_gain),
            tile(head_dim),
            tile(head_dim),
        ],
        out_specs=[
            half(width),
            half(width),
            tile(head_width),
            tile(head_dim),
            tile(head_dim),
            tile(head_width),
            pl.BlockSpec((1, 8, heads * block), lambda i: (i, 0, 0)),
            tile(head_dim),
        ],
        out_shape=[
            shape((slots // 2, width), jnp.bfloat16),
            shape((slots // 2, width), jnp.bfloat16),
            shape((slots, head_width), jnp.bfloat16),
            shape((slots, head_dim), jnp.bfloat16),
            shape((slots, head_dim), jnp.bfloat16),
            shape((slots, head_width), jnp.bfloat16),
            shape((count, 8, heads * block), jnp.float32),
            shape((slots, head_dim), jnp.float32),
        ],
        scratch_shapes=[
            pltpu.VMEM((slots, head_dim), jnp.bfloat16),
            pltpu.VMEM((slots, 2 * head_dim), jnp.bfloat16),
            pltpu.VMEM((heads * block, 2 * head_dim), jnp.float32),
            pltpu.VMEM((8, heads * block), jnp.float32),
            pltpu.VMEM((block, width), jnp.bfloat16),
        ],
        compiler_params=pltpu.CompilerParams(vmem_limit_bytes=kernel_vmem),
        cost_estimate=pl.CostEstimate(
            flops=2 * slots * width * (2 * head_width + 2 * head_dim)
            + 3 * slots * slots * head_width,
            bytes_accessed=4 * slots * width + 4 * width * head_width,
            transcendentals=slots * slots * heads // 2,
        ),
        name="attend_rows",
    )(
        ends,
        place,
        keep(rows),
        keep(w_query),
        keep(w_kv),
        keep(w_out),
        q_gain,
        k_gain,
        keep(cosine),
        keep(sine),
    )


def attend_back_kernel(
    ends_ref,
    grad_ref,
    out_w_ref,
    query_ref,
    heads_ref,
    key_ref,
    value_ref,
    log_ref,
    scale_ref,
    query_gain_ref,
    key_gain_ref,
    cosine_ref,
    sine_ref,
    grad_query_ref,
    grad_kv_ref,
    grad_query_gain_ref,
    grad_key_gain_ref,
    grad_keys,
    grad_values,
    grad_queries,
    *,
    head_dim,
):
    step = pl.program_id(0)
    block = query_ref.shape[0]
    heads = query_ref.shape[1] // head_dim
    ends = [ends_ref[k] for k in range(ends_ref.shape[0])]
    softmax_scale = head_dim ** (-0.5)

    @pl.when(step == 0)
    def _():
        grad_keys[...] = jnp.zeros_like(grad_keys)
        grad_values[...] = jnp.zeros_like(grad_values)
        grad_query_gain_ref[...] = jnp.zeros_like(grad_query_gain_ref)

    grad_heads = lanes_dot(grad_ref[...], out_w_ref[...]).astype(jnp.bfloat16)
    query = query_ref[...]
    out = heads_ref[...]
    cuts = [slice(h * head_dim, (h + 1) * head_dim) for h in range(heads)]
    queries = jnp.concatenate([query[:, cut] for cut in cuts], axis=0)
    grads = jnp.concatenate([grad_heads[:, cut] for cut in cuts], axis=0)
    outs = jnp.concatenate([out[:, cut] for cut in cuts], axis=0)
    products = grads.astype(jnp.float32) * outs.astype(jnp.float32)
    high = products.astype(jnp.bfloat16)
    rest = (products - high.astype(jnp.float32)).astype(jnp.bfloat16)
    ones = jnp.ones((8, head_dim), jnp.bfloat16)
    centre = (lanes_dot(ones, high) + lanes_dot(ones, rest))[:1]
    logs = log_ref[0, :1, :]
    column_ids = step * block + lax.broadcasted_iota(jnp.int32, (1, block), 1)
    starts = row_starts(column_ids, ends)
    grad_queries[...] = jnp.zeros_like(grad_queries)

    def one_block(j, carry):
        there = pl.ds(pl.multiple_of(j * block, block), block)
        key = key_ref[there, :]
        value = value_ref[there, :]
        scores = lanes_dot(key, queries) * softmax_scale - logs
        grad_probs = lanes_dot(value, grads) - centre
        row_ids = j * block + lax.broadcasted_iota(jnp.int32, (block, block), 0)
        allowed = (row_ids <= column_ids) & (row_ids >= starts)
        probs = jnp.concatenate(
            [
                jnp.where(allowed, jnp.exp(scores[:, h * block : (h + 1) * block]), 0.0)
                for h in range(heads)
            ],
            axis=1,
        )
        probs_low = probs.astype(jnp.bfloat16)
        grad_scores = (probs * grad_probs).astype(jnp.bfloat16)
        grad_values[there, :] += jnp.dot(probs_low, grads, preferred_element_type=jnp.float32)
        grad_keys[there, :] += jnp.dot(grad_scores, queries, preferred_element_type=jnp.float32)
        grad_queries[...] += lax.dot_general(
            grad_scores, key, (((0,), (0,)), ((), ())), preferred_element_type=jnp.float32
        )
        return carry

    first = row_starts(step * block, ends) // block
    lax.fori_loop(first, step + 1, one_block, 0)

    def prep_back(grad, low, gain, cosine, sine, scale):
        grad = grad * softmax_scale
        low = low.astype(jnp.float32)
        grad_gained = grad * cosine - turn_halves(grad) * sine
        normed = (low * cosine - turn_halves(low) * sine) / gain
        grad_gain = jnp.sum(grad_gained * normed, axis=0, keepdims=True)
        grad_normed = grad_gained * gain
        mean = jnp.mean(grad_normed * normed, axis=-1, keepdims=True)
        return scale * (grad_normed - normed * mean), grad_gain

    own = pl.ds(pl.multiple_of(step * block, block), block)
    cosine = cosine_ref[own, :]
    sine = sine_ref[own, :]
    scales = scale_ref[own, :]
    for h, cut in enumerate(cuts):
        grad_pre, grad_gain = prep_back(
            grad_queries[h * block : (h + 1) * block, :],
            query[:, cut],
            query_gain_ref[...],
            cosine,
            sine,
            scales[:, h : h + 1],
        )
        grad_query_ref[:, cut] = grad_pre.astype(jnp.bfloat16)
        grad_query_gain_ref[...] += grad_gain

    @pl.when(step == pl.num_programs(0) - 1)
    def _():
        grad_pre, grad_gain = prep_back(
            grad_keys[...],
            key_ref[...],
            key_gain_ref[...],
            cosine_ref[...],
            sine_ref[...],
            scale_ref[:, heads : heads + 1],
        )
        grad_kv_ref[:, :head_dim] = grad_pre.astype(jnp.bfloat16)
        grad_kv_ref[:, head_dim:] = grad_values[...].astype(jnp.bfloat16)
        grad_key_gain_ref[...] = grad_gain


def attend_rows_back(
    ends, grad, w_out, query, heads_low, key, value, logs, scales, q_gain, k_gain, cosine, sine, block
):
    slots, width = grad.shape
    head_dim = q_gain.shape[0]
    head_width = query.shape[1]
    heads = head_width // head_dim
    count = slots // block

    def tile(columns):
        return pl.BlockSpec((block, columns), lambda i: (i, 0))

    def whole(array):
        return pl.BlockSpec(array.shape, lambda i: (0, 0))

    shape = pltpu.HBM
    q_gain = q_gain[None]
    k_gain = k_gain[None]
    return pl.pallas_call(
        functools.partial(attend_back_kernel, head_dim=head_dim),
        grid=(count,),
        in_specs=[
            pl.BlockSpec(memory_space=pltpu.SMEM),
            tile(width),
            whole(w_out),
            tile(head_width),
            tile(head_width),
            whole(key),
            whole(value),
            pl.BlockSpec((1, 8, heads * block), lambda i: (i, 0, 0)),
            whole(scales),
            whole(q_gain),
            whole(k_gain),
            whole(cosine),
            whole(sine),
        ],
        out_specs=[
            tile(head_width),
            pl.BlockSpec((slots, 2 * head_dim), lambda i: (0, 0)),
            pl.BlockSpec((1, head_dim), lambda i: (0, 0)),
            pl.BlockSpec((1, head_dim), lambda i: (0, 0)),
        ],
        out_shape=[
            shape((slots, head_width), jnp.bfloat16),
            shape((slots, 2 * head_dim), jnp.bfloat16),
            shape((1, head_dim), jnp.float32),
            shape((1, head_dim), jnp.float32),
        ],
        scratch_shapes=[
            pltpu.VMEM((slots, head_dim), jnp.float32),
            pltpu.VMEM((slots, head_dim), jnp.float32),
            pltpu.VMEM((heads * block, head_dim), jnp.float32),
        ],
        compiler_params=pltpu.CompilerParams(vmem_limit_bytes=kernel_vmem),
        cost_estimate=pl.CostEstimate(
            flops=2 * slots * width * head_width + 6 * slots * slots * head_width,
            bytes_accessed=2 * slots * width + 2 * width * head_width,
            transcendentals=slots * slots * heads // 2,
        ),
        name="attend_rows_back",
    )(
        ends,
        keep(grad),
        keep(w_out),
        keep(query),
        keep(heads_low),
        keep(key),
        keep(value),
        keep(logs),
        keep(scales),
        q_gain,
        k_gain,
        keep(cosine),
        keep(sine),
    )


def transposed_times(left, right):
    return lax.dot_general(
        left, right, (((0,), (0,)), ((), ())), preferred_element_type=jnp.float32
    )


plane_axes = ("row", "col")


def move_plane(parts):
    return lax.all_to_all(parts, plane_axes, split_axis=0, concat_axis=0, tiled=True)


def rotate(block, axis, step):
    size = lax.axis_size(axis)
    return lax.ppermute(block, axis, [(i, (i + step) % size) for i in range(size)])


def gather_planes(block):
    planes = lax.axis_size("expert")
    return jnp.stack([block] + [rotate(block, "expert", k) for k in range(1, planes)], axis=0)


def return_planes(parts):
    return [parts[0]] + [rotate(parts[k], "expert", -k) for k in range(1, parts.shape[0])]


def together(*values):
    return lax.optimization_barrier(values)


def move_all(parts):
    return lax.all_to_all(
        parts, ("expert",) + plane_axes, split_axis=0, concat_axis=0, tiled=True
    )


def sum_all(values):
    devices = lax.axis_size(("expert",) + plane_axes)
    padded = jnp.pad(values, (0, -values.shape[0] % (devices * 128)))
    total = jnp.sum(move_all(padded.reshape(devices, -1, 128)), axis=0)
    return move_all(jnp.broadcast_to(total[None], (devices,) + total.shape)).reshape(-1)


def line_step(value, step, hop):
    planes = lax.axis_size("expert")
    if hop > 0:
        pairs = [(i, i + 1) for i in range(*step)]
    else:
        pairs = [(planes - 1 - i, planes - 2 - i) for i in range(*step)]
    return lax.ppermute(value, "expert", pairs)


def send_planes(product):
    planes = lax.axis_size("expert")
    plane = lax.axis_index("expert")
    shares = product.reshape(planes, -1, product.shape[1])

    def share(k):
        return lax.dynamic_index_in_dim(shares, (plane + k) % planes, 0, keepdims=False)

    return [share(0)] + [rotate(share(k), "expert", k) for k in range(1, planes)]


def spread_planes(total):
    planes = lax.axis_size("expert")
    arrived = []
    for hop in (1, -1):
        message = total
        for k in range(1, planes):
            message = line_step(message, (k - 1, planes - 1), hop)
            arrived.append((k, hop, message))
    arrived.sort(key=lambda entry: -entry[0])
    return [message for _, _, message in arrived] + [total]


def in_plane_order(parts):
    planes = lax.axis_size("expert")
    plane = lax.axis_index("expert")
    rows = parts[0].shape[0]
    result = jnp.zeros((planes * rows, parts[0].shape[1]), jnp.float32)
    places = [plane - hop * k for k in range(planes - 1, 0, -1) for hop in (1, -1)] + [plane]
    for place, part in zip(places, parts):
        result = lax.dynamic_update_slice_in_dim(
            result, part.astype(jnp.float32), jnp.clip(place, 0, planes - 1) * rows, axis=0
        )
    return result


def scatter_cols(product):
    col = lax.axis_index("col")
    cols = lax.axis_size("col")
    moved = [rotate(product((col + k) % cols).astype(jnp.bfloat16), "col", k) for k in range(1, cols)]
    total = product(col)
    for part in moved:
        total = total + part.astype(jnp.float32)
    return total.astype(jnp.bfloat16)


def scatter_rows(parts):
    row = lax.axis_index("row")
    rows = lax.axis_size("row")

    def piece(k):
        return lax.dynamic_index_in_dim(parts, (row + k) % rows, 0, keepdims=False)

    arrived = [rotate(piece(k), "row", k) for k in range(1, rows)]
    result = piece(0).astype(jnp.float32)
    for part in arrived:
        result = result + part.astype(jnp.float32)
    return result


def expert_kernel(ids_ref, router_ref, gate_ref, up_ref, down_ref, *refs, count, experts):
    rows_refs = refs[:count]
    grads_refs = refs[count : 2 * count]
    sends = refs[2 * count : 3 * count]
    weighted = refs[3 * count : 4 * count]
    rows_out, grads_out, hidden_out, grad_gate_out, grad_up_out = refs[4 * count :]
    width = rows_refs[1].shape[1]
    cuts = [slice(i * width, (i + 1) * width) for i in range(count)]
    rows = [ref[...] for ref in rows_refs]
    chosen = grads_refs[0][:, width:].astype(jnp.float32) > 0.5
    lanes = lax.broadcasted_iota(jnp.int32, chosen.shape, 1)

    def times(weights_ref):
        return sum(
            jnp.dot(part, weights_ref[cut, :], preferred_element_type=jnp.float32)
            for part, cut in zip(rows, cuts)
        )

    logits = times(router_ref)
    top = jnp.max(jnp.where(chosen, logits, -3e38), axis=1, keepdims=True)
    raised = jnp.where(chosen, jnp.exp(jnp.where(chosen, logits - top, 0.0)), 0.0)
    own = jnp.sum(jnp.where(lanes == ids_ref[0], raised, 0.0), axis=1, keepdims=True)
    gates = own / jnp.maximum(jnp.sum(raised, axis=1, keepdims=True), 1e-30)
    gate_pre = times(gate_ref)
    up_pre = times(up_ref)
    sigmoid = 1.0 / (1.0 + jnp.exp(-gate_pre))
    silu = gate_pre * sigmoid
    hidden = (silu * up_pre).astype(jnp.bfloat16)
    hidden_out[...] = hidden
    dots = jnp.zeros(gates.shape, jnp.float32)
    grad_hidden = jnp.zeros(gate_pre.shape, jnp.float32)
    for i, cut in enumerate(cuts):
        out = jnp.dot(hidden, down_ref[:, cut], preferred_element_type=jnp.float32)
        out = out.astype(jnp.bfloat16).astype(jnp.float32)
        grads = grads_refs[i][:, :width].astype(jnp.float32)
        dots = dots + jnp.sum(out * grads, axis=1, keepdims=True)
        weighted[i][...] = (out * gates).astype(jnp.bfloat16)
        grads_low = (grads * gates).astype(jnp.bfloat16)
        grads_out[:, cut] = grads_low
        rows_out[:, cut] = rows[i]
        grad_hidden = grad_hidden + lanes_dot(grads_low, down_ref[:, cut])
    grad_gate = (grad_hidden * up_pre * sigmoid * (1.0 + gate_pre * (1.0 - sigmoid))).astype(
        jnp.bfloat16
    )
    grad_up = (grad_hidden * silu).astype(jnp.bfloat16)
    grad_gate_out[...] = grad_gate
    grad_up_out[...] = grad_up
    for i, cut in enumerate(cuts):
        sends[i][:, :width] = (
            lanes_dot(grad_gate, gate_ref[cut, :]) + lanes_dot(grad_up, up_ref[cut, :])
        ).astype(jnp.bfloat16)
    dots_high = dots.astype(jnp.bfloat16).astype(jnp.float32)
    side = jnp.where(lanes == ids_ref[1], dots_high, 0.0) + jnp.where(
        lanes == ids_ref[1] + experts, dots - dots_high, 0.0
    )
    sends[0][:, width:] = side.astype(jnp.bfloat16)


def expert_rows(ids, w_router, w_gate, w_up, w_down, rows, grads, plane_size):
    count = len(rows)
    slots, width = rows[0].shape
    model_width, hidden = w_gate.shape
    side = grads[0].shape[1] - width
    block = slots // expert_steps

    def tile(columns):
        return pl.BlockSpec((block, columns), lambda i: (i, 0))

    def whole(array):
        return pl.BlockSpec(array.shape, lambda i: (0, 0), pipeline_mode=pl.Buffered(1))

    def shape(columns):
        return pltpu.HBM((slots, columns), jnp.bfloat16)

    sides = [width + side] + [width] * (count - 1)
    outs = sides + [width] * count + [model_width, model_width, hidden, hidden, hidden]
    flops = 2 * slots * model_width * hidden * 6
    return pl.pallas_call(
        functools.partial(expert_kernel, count=count, experts=plane_size),
        grid=(expert_steps,),
        in_specs=[pl.BlockSpec(memory_space=pltpu.SMEM)]
        + [whole(array) for array in (w_router, w_gate, w_up, w_down)]
        + [tile(width)] * count
        + [tile(columns) for columns in sides],
        out_specs=[tile(columns) for columns in outs],
        out_shape=[shape(columns) for columns in outs],
        compiler_params=pltpu.CompilerParams(vmem_limit_bytes=expert_vmem),
        cost_estimate=pl.CostEstimate(
            flops=flops, bytes_accessed=6 * model_width * hidden, transcendentals=slots * hidden
        ),
        name="expert_rows",
    )(ids, w_router, w_gate, w_up, w_down, *rows, *grads)


def local(
    layer_input,
    norm_attn,
    w_query,
    w_key,
    w_value,
    q_gain,
    k_gain,
    w_out,
    norm_moe,
    w_router,
    w_gate,
    w_up,
    w_down,
    seq_lengths,
    routes,
    out_grad,
):
    tok_dev = layer_input.shape[0]
    model_width = layer_input.shape[1]
    group_tok = tok_dev * lax.axis_size(("row", "col"))
    head_dim = q_gain.shape[0]
    experts = w_router.shape[1]
    top_count = routes.shape[1]
    capacity = tok_dev * top_count * 17 // (16 * experts)
    planes = lax.axis_size("expert")
    plane_size = lax.axis_size(plane_axes)
    plane_index = lax.axis_index("expert")
    plane_cap = planes * capacity
    chosen_here = jnp.any(
        routes[:, :, None] == jnp.arange(experts, dtype=jnp.int32)[None, None, :], axis=1
    )
    plane_routes = gather_planes(routes.T)
    plane_experts = plane_index * plane_size + jnp.arange(plane_size, dtype=jnp.int32)
    chosen_plane = jnp.any(
        plane_routes[None] == plane_experts[:, None, None, None], axis=2
    )
    token_ids = jnp.arange(tok_dev, dtype=jnp.int32)
    earlier = (token_ids[:, None] < token_ids[None, :]).astype(jnp.bfloat16)
    slot_rank = jnp.dot(
        chosen_plane.astype(jnp.bfloat16).reshape(plane_size * planes, tok_dev),
        earlier,
        preferred_element_type=jnp.float32,
    ).astype(jnp.int32).reshape(plane_size, planes, tok_dev)
    plane_slot = jnp.where(
        chosen_plane,
        slot_rank + (jnp.arange(planes, dtype=jnp.int32) * capacity)[None, :, None],
        -1,
    ).reshape(plane_size, 1, planes * tok_dev)
    dispatch = (
        plane_slot == jnp.arange(plane_cap, dtype=jnp.int32)[None, :, None]
    ).astype(jnp.bfloat16)
    chosen_all = jnp.any(
        plane_routes[:, :, :, None] == jnp.arange(experts, dtype=jnp.int32), axis=1
    ).reshape(planes * tok_dev, experts).astype(jnp.bfloat16)

    def gather_rows(block):
        return gather_planes(block).reshape(planes * tok_dev, block.shape[1])

    def select_slots(rows_all):
        return jnp.dot(
            dispatch.reshape(plane_size * plane_cap, -1),
            rows_all,
            preferred_element_type=jnp.float32,
        ).astype(jnp.bfloat16)

    def to_plane(slot_values):
        width = slot_values.shape[1]
        moved = move_plane(slot_values.reshape(plane_size, plane_cap, width))
        return moved.reshape(plane_size * plane_cap, width)

    chunk_width = model_width // chunk_count
    chunks = [slice(i * chunk_width, (i + 1) * chunk_width) for i in range(chunk_count)]
    side_width = 128
    grad_planes = [gather_rows(out_grad[:, cut]) for cut in chunks]
    grad_planes[0] = jnp.concatenate(
        [grad_planes[0], jnp.pad(chosen_all, ((0, 0), (0, side_width - experts)))], axis=1
    )
    slot_sends = [select_slots(part) for part in grad_planes]
    def gates_of(all_logits, chosen):
        top = jnp.max(jnp.where(chosen, all_logits, -3e38), axis=1, keepdims=True)
        raised = jnp.where(chosen, jnp.exp(jnp.where(chosen, all_logits - top, 0.0)), 0.0)
        return raised / jnp.maximum(jnp.sum(raised, axis=1, keepdims=True), 1e-30)

    input_rows = layer_input.astype(jnp.float32)
    normed_one, norm_one_back = jax.vjp(rms_scale, input_rows, norm_attn)
    normed_low = normed_one.astype(jnp.bfloat16)
    group_rows = lax.all_gather(normed_low, ("row", "col"), axis=0, tiled=True)
    ends = jnp.cumsum(seq_lengths[0], dtype=jnp.int32)
    cosine_table, sine_table = rope_tables(slot_positions(ends, group_tok), head_dim)
    key_value_w = jnp.concatenate([w_key, w_value], axis=1)
    cosine_table, sine_table, key_value_w, slot_sends[0] = together(
        cosine_table, sine_table, key_value_w, slot_sends[0]
    )
    grad_slot_chunks = [to_plane(slot_sends[0])]
    col = lax.axis_index("col")
    kept, sent, query_low, key_low, value_low, heads_low, log_totals, head_scales = attend_rows(
        ends, col.astype(jnp.int32)[None], group_rows, w_query, key_value_w, w_out, q_gain, k_gain, cosine_table, sine_table,
        2 * tok_dev,
    )
    sent, kept, grad_slot_chunks[0] = together(sent, kept, grad_slot_chunks[0])
    col_sums = kept.astype(jnp.float32) + rotate(sent, "col", 1).astype(jnp.float32)
    attn_rows = scatter_rows(col_sums.astype(jnp.bfloat16).reshape(-1, tok_dev, model_width))
    attn_rows, *late_sends = together(attn_rows, *slot_sends[1:])
    grad_slot_chunks += [to_plane(part) for part in late_sends]
    attn_rows = attn_rows.astype(jnp.float32)
    mixed_rows = input_rows + attn_rows
    normed_two, norm_two_back = jax.vjp(rms_scale, mixed_rows, norm_moe)
    moe_input = normed_two.astype(jnp.bfloat16)
    router_logits = jnp.dot(moe_input, w_router, preferred_element_type=jnp.float32)
    source_gates = gates_of(router_logits, chosen_here)

    moe_planes = [gather_rows(moe_input[:, cut]) for cut in chunks]
    moe_sends = [select_slots(part) for part in moe_planes]
    moe_sends[0], *grad_slot_chunks[1:] = together(moe_sends[0], *grad_slot_chunks[1:])
    slot_chunks = [to_plane(part) for part in moe_sends]
    place = lax.axis_index(plane_axes)
    ids = jnp.stack([plane_index * plane_size + place, place]).astype(jnp.int32)
    expert_outs = expert_rows(
        ids,
        jnp.pad(w_router, ((0, 0), (0, side_width - experts))),
        w_gate[0],
        w_up[0],
        w_down[0],
        slot_chunks,
        grad_slot_chunks,
        plane_size,
    )
    grad_sends = expert_outs[:chunk_count]
    out_sends = expert_outs[chunk_count : 2 * chunk_count]
    moe_slots, grad_out_slots, hidden_low, grad_gate_pre, grad_up_pre = expert_outs[
        2 * chunk_count :
    ]

    def to_source(returned):
        summed = lax.dot_general(
            dispatch.reshape(plane_size * plane_cap, -1),
            returned,
            (((0,), (0,)), ((), ())),
            preferred_element_type=jnp.float32,
        ).astype(jnp.bfloat16)
        return return_planes(summed.reshape(planes, tok_dev, returned.shape[1]))

    def add_parts(parts):
        return sum(part.astype(jnp.float32) for part in parts)

    grad_rows = out_grad.astype(jnp.float32)
    grad_down = transposed_times(hidden_low, grad_out_slots)
    grad_gate = transposed_times(moe_slots, grad_gate_pre)
    grad_up = transposed_times(moe_slots, grad_up_pre)
    grad_returns = [to_plane(part) for part in grad_sends]
    grad_returns[0], grad_down = together(grad_returns[0], grad_down)
    grad_returns[-1], grad_gate, *out_sends = together(grad_returns[-1], grad_gate, *out_sends)
    out_returns = [to_plane(out_sends[0])]
    grad_parts = [to_source(part) for part in grad_returns]
    grad_parts[-1][-1], grad_up = together(grad_parts[-1][-1], grad_up)
    side_parts = jnp.stack(
        [part[:, chunk_width:].astype(jnp.float32) for part in grad_parts[0]], axis=0
    )
    dot_parts = side_parts[:, :, :plane_size] + side_parts[:, :, plane_size : 2 * plane_size]
    dot_parts = lax.dynamic_slice_in_dim(
        jnp.concatenate([dot_parts, dot_parts], axis=0), planes - plane_index, planes, axis=0
    )
    grad_gates = jnp.swapaxes(dot_parts, 0, 1).reshape(tok_dev, experts)
    grad_logits = source_gates * (
        grad_gates - jnp.sum(source_gates * grad_gates, axis=1, keepdims=True)
    )
    grad_parts[0] = [part[:, :chunk_width] for part in grad_parts[0]]
    grad_moe_input = jnp.concatenate([add_parts(parts) for parts in grad_parts], axis=1)
    grad_router = lax.dot_general(
        grad_logits,
        moe_input.astype(jnp.float32),
        (((0,), (0,)), ((), ())),
        precision=highest,
        preferred_element_type=jnp.float32,
    )
    grad_moe_input = grad_moe_input + jnp.einsum(
        "te,de->td", grad_logits, w_router, precision=highest, preferred_element_type=jnp.float32
    )
    grad_mixed_norm, grad_norm_moe = norm_two_back(grad_moe_input)
    grad_mixed = grad_rows + grad_mixed_norm
    grad_attn_low = grad_mixed.astype(jnp.bfloat16)
    grad_attn_low, out_returns[0] = together(grad_attn_low, out_returns[0])
    grad_group = lax.all_gather(grad_attn_low, ("row", "col"), axis=0, tiled=True)
    out_first = add_parts(to_source(out_returns[0]))
    grad_group, out_first, *out_late = together(grad_group, out_first, *out_sends[1:])
    out_returns += [to_plane(part) for part in out_late]
    grad_out_proj = transposed_times(heads_low, grad_group).astype(jnp.bfloat16)
    grad_out_proj, grad_group = together(grad_out_proj, grad_group)
    out_terms = send_planes(grad_out_proj)
    grad_query_low, grad_kv, grad_q_gain, grad_k_gain = attend_rows_back(
        ends,
        grad_group,
        w_out,
        query_low,
        heads_low,
        key_low,
        value_low,
        log_totals,
        head_scales,
        q_gain,
        k_gain,
        cosine_table,
        sine_table,
        2 * tok_dev,
    )
    grad_query_low, grad_kv, out_terms[1], out_terms[-1] = together(
        grad_query_low, grad_kv, out_terms[1], out_terms[-1]
    )
    grad_query = transposed_times(group_rows, grad_query_low)
    grad_key_value = transposed_times(group_rows, grad_kv)
    norm_terms = (
        jnp.sum(grad_query * w_query.astype(jnp.float32), axis=1)
        + jnp.sum(grad_key_value * key_value_w.astype(jnp.float32), axis=1)
    ) / norm_attn
    cols = lax.axis_size("col")
    col = lax.axis_index("col")
    kv_low = grad_key_value.astype(jnp.bfloat16).reshape(cols, -1, 2 * head_dim)
    kv_part = lax.dynamic_index_in_dim(kv_low, col, 0, keepdims=False).astype(jnp.float32)
    for k in range(1, cols):
        kv_part = kv_part + rotate(
            lax.dynamic_index_in_dim(kv_low, (col + k) % cols, 0, keepdims=False), "col", k
        ).astype(jnp.float32)
    lane_parts = grad_query.shape[1] // (2 * head_dim)
    query_kv = jnp.concatenate(
        [
            grad_query.astype(jnp.bfloat16),
            *[
                jnp.concatenate(jnp.split(kv_part.astype(jnp.bfloat16), lane_parts), axis=1)
            ],
        ],
        axis=0,
    )
    query_kv = lax.psum(query_kv, "expert")
    left_parts = jnp.concatenate([grad_query_low, grad_kv], axis=1).reshape(
        -1, cols, tok_dev, grad_query_low.shape[1] + 2 * head_dim
    )
    right_all = jnp.concatenate([w_query, key_value_w], axis=1)

    def grad_normed_rows(place):
        left = lax.dynamic_index_in_dim(left_parts, place, 1, keepdims=False)
        return lax.dot_general(
            left, right_all, (((2,), (1,)), ((), ())), preferred_element_type=jnp.float32
        )

    out_share = add_parts(out_terms).astype(jnp.bfloat16)
    left_parts, out_share, *out_returns[1:] = together(left_parts, out_share, *out_returns[1:])
    out_shares = spread_planes(out_share)
    out_parts = [out_first] + [add_parts(to_source(part)) for part in out_returns[1:]]
    col_sums = scatter_cols(grad_normed_rows)
    summed_values = jnp.concatenate(
        [grad_router.reshape(-1), grad_norm_moe, norm_terms, grad_q_gain[0], grad_k_gain[0]]
    )
    col_sums, summed_values = together(col_sums, summed_values)
    sums = sum_all(summed_values)
    grad_normed = scatter_rows(col_sums)
    grad_normed, sums, query_kv, *out_parts = together(grad_normed, sums, query_kv, *out_parts)
    out_rows = (mixed_rows + jnp.concatenate(out_parts, axis=1)).astype(jnp.bfloat16)
    grad_out_proj = in_plane_order(out_shares)
    places = (0, experts * model_width, model_width, model_width, head_dim, head_dim)
    ends_at = [sum(places[: k + 1]) for k in range(len(places))]
    grad_router, grad_norm_moe, grad_norm_attn, grad_q_gain, grad_k_gain = [
        sums[low:high] for low, high in zip(ends_at[:-1], ends_at[1:])
    ]
    grad_router = grad_router.reshape(experts, model_width).T
    grad_query = query_kv[:model_width].astype(jnp.float32)
    kv_part = query_kv[model_width:]
    kv_parts = [kv_part] + [rotate(kv_part, "col", k) for k in range(1, cols)]
    kv_blocks = []
    for place in range(cols):
        block = kv_parts[0]
        for k in range(1, cols):
            block = jnp.where((col - k) % cols == place, kv_parts[k], block)
        kv_blocks += jnp.split(block.astype(jnp.float32), lane_parts, axis=1)
    grad_key = jnp.concatenate([block[:, :head_dim] for block in kv_blocks], axis=0)
    grad_value = jnp.concatenate([block[:, head_dim:] for block in kv_blocks], axis=0)
    grad_input_norm = norm_one_back(grad_normed)[0]
    grad_x = (grad_mixed + grad_input_norm).astype(jnp.bfloat16)
    return (
        out_rows,
        grad_x,
        grad_norm_attn,
        grad_query,
        grad_key,
        grad_value,
        grad_q_gain,
        grad_k_gain,
        grad_out_proj,
        grad_norm_moe,
        grad_router,
        grad_gate[None],
        grad_up[None],
        grad_down[None],
    )


def solution(mesh):
    placed = (
        P(("expert", "row", "col"), None),
        P(),
        P(None, ("row", "col")),
        P(None, "row"),
        P(None, "row"),
        P(),
        P(),
        P(("row", "col"), None),
        P(),
        P(),
        P(("expert", "row", "col"), None, None),
        P(("expert", "row", "col"), None, None),
        P(("expert", "row", "col"), None, None),
        P("expert", None),
        P(("expert", "row", "col"), None),
        P(("expert", "row", "col"), None),
    )
    return jax.shard_map(
        local,
        mesh=mesh,
        in_specs=placed,
        out_specs=(
            P(("expert", "row", "col"), None),
            P(("expert", "row", "col"), None),
            P(),
            P(None, ("row", "col")),
            P(None, "row"),
            P(None, "row"),
            P(),
            P(),
            P(("row", "col"), None),
            P(),
            P(),
            P(("expert", "row", "col"), None, None),
            P(("expert", "row", "col"), None, None),
            P(("expert", "row", "col"), None, None),
        ),
        check_vma=False,
    )
```

```python
import functools

import jax
import jax.numpy as jnp
from jax import lax
from jax.experimental import pallas as pl
from jax.experimental.pallas import tpu as pltpu
from jax.sharding import PartitionSpec as P

eps_norm = 1e-06
rope_base = 1000000.0
highest = lax.Precision.HIGHEST
chunk_count = 2
grads_first = 7
weighted_first = 9
expert_steps = 2
expert_vmem = 56 * 1024 * 1024
kernel_vmem = 40 * 1024 * 1024


def rms_scale(values, norm_gain):
    return (
        values * lax.rsqrt(jnp.mean(values * values, axis=-1, keepdims=True) + eps_norm) * norm_gain
    )


def rope_tables(positions, head_dim):
    half_dim = head_dim // 2
    inverse = rope_base ** (-(jnp.arange(half_dim, dtype=jnp.float32) * 2.0 / head_dim))
    angles = positions.astype(jnp.float32)[:, None] * inverse[None, :]
    cosine = jnp.cos(angles)
    sine = jnp.sin(angles)
    return (jnp.concatenate([cosine, cosine], axis=1), jnp.concatenate([-sine, sine], axis=1))


def slot_positions(ends, slot_count):
    slot_ids = jnp.arange(slot_count, dtype=jnp.int32)
    starts = row_starts(slot_ids, [ends[k] for k in range(ends.shape[0])])
    return slot_ids - starts


def row_starts(row_ids, ends):
    starts = jnp.zeros_like(row_ids)
    for end in ends:
        starts = jnp.where(row_ids >= end, end, starts)
    return jnp.where(row_ids >= ends[-1], row_ids, starts)


def lanes_dot(left, right):
    return lax.dot_general(
        left, right, (((1,), (1,)), ((), ())), preferred_element_type=jnp.float32
    )


def turn_halves(values):
    return pltpu.roll(values, values.shape[-1] // 2, axis=1)


def keep(array):
    return pltpu.with_memory_space_constraint(array, pltpu.HBM)


def attend_kernel(
    ends_ref,
    place_ref,
    rows_ref,
    query_w_ref,
    kv_w_ref,
    out_w_ref,
    query_gain_ref,
    key_gain_ref,
    cosine_ref,
    sine_ref,
    kept_ref,
    sent_ref,
    query_ref,
    key_ref,
    value_ref,
    heads_ref,
    log_ref,
    scale_ref,
    keys,
    values,
    total,
    sums,
    partial,
    *,
    head_dim,
):
    step = pl.program_id(0)
    block = rows_ref.shape[0]
    heads = query_w_ref.shape[1] // head_dim
    ends = [ends_ref[k] for k in range(ends_ref.shape[0])]
    softmax_scale = head_dim ** (-0.5)
    rows = rows_ref[...]
    query_pre = jnp.dot(rows, query_w_ref[...], preferred_element_type=jnp.float32)
    kv_pre = jnp.dot(rows, kv_w_ref[...], preferred_element_type=jnp.float32)
    cosine = cosine_ref[...]
    sine = sine_ref[...]
    lanes = lax.broadcasted_iota(jnp.int32, (block, head_dim), 1)
    scales = jnp.zeros((block, head_dim), jnp.float32)

    def prep(vectors, gain):
        scale = lax.rsqrt(jnp.mean(vectors * vectors, axis=-1, keepdims=True) + eps_norm)
        gained = vectors * scale * gain
        return (gained * cosine + turn_halves(gained) * sine).astype(jnp.bfloat16), scale

    stacked = []
    for h in range(heads):
        cut = slice(h * head_dim, (h + 1) * head_dim)
        low, scale = prep(query_pre[:, cut], query_gain_ref[...])
        query_ref[:, cut] = low
        stacked.append(low)
        scales = jnp.where(lanes == h, scale, scales)
    key_low, scale = prep(kv_pre[:, :head_dim], key_gain_ref[...])
    scale_ref[...] = jnp.where(lanes == heads, scale, scales)
    value_low = kv_pre[:, head_dim:].astype(jnp.bfloat16)
    key_ref[...] = key_low
    value_ref[...] = value_low
    own = pl.ds(pl.multiple_of(step * block, block), block)
    keys[own, :] = key_low
    values[own, :head_dim] = value_low
    values[own, head_dim:] = jnp.ones((block, head_dim), jnp.bfloat16)
    queries = jnp.concatenate(stacked, axis=0)
    row_ids = step * block + lax.broadcasted_iota(jnp.int32, (block, 1), 0)
    starts = row_starts(row_ids, ends)
    total[...] = jnp.zeros_like(total)
    sums[...] = jnp.zeros_like(sums)
    ones = jnp.ones((8, block), jnp.bfloat16)

    def one_block(j, carry):
        there = pl.ds(pl.multiple_of(j * block, block), block)
        scores = lanes_dot(queries, keys[there, :]) * softmax_scale
        column_ids = j * block + lax.broadcasted_iota(jnp.int32, (block, block), 1)
        allowed = (column_ids <= row_ids) & (column_ids >= starts)
        weights = jnp.concatenate(
            [
                jnp.where(allowed, jnp.exp(scores[h * block : (h + 1) * block]), 0.0).astype(
                    jnp.bfloat16
                )
                for h in range(heads)
            ],
            axis=0,
        )
        total[...] += jnp.dot(weights, values[there, :], preferred_element_type=jnp.float32)
        sums[...] += lanes_dot(ones, weights)
        return carry

    first = row_starts(step * block, ends) // block
    lax.fori_loop(first, step + 1, one_block, 0)
    log_ref[0] = jnp.log(sums[...])
    outs = (total[:, :head_dim] / total[:, head_dim:]).astype(jnp.bfloat16)
    for h in range(heads):
        heads_ref[:, h * head_dim : (h + 1) * head_dim] = outs[h * block : (h + 1) * block]
    partial[...] = jnp.dot(
        heads_ref[...], out_w_ref[...], preferred_element_type=jnp.float32
    ).astype(jnp.bfloat16)
    share = kept_ref.shape[0]
    kept = pl.multiple_of(place_ref[0] * share, share)
    sent = pl.multiple_of((1 - place_ref[0]) * share, share)
    kept_ref[...] = partial[pl.ds(kept, share), :]
    sent_ref[...] = partial[pl.ds(sent, share), :]


def attend_rows(ends, place, rows, w_query, w_kv, w_out, q_gain, k_gain, cosine, sine, block):
    slots, width = rows.shape
    head_dim = q_gain.shape[0]
    head_width = w_query.shape[1]
    heads = head_width // head_dim
    count = slots // block

    def tile(columns):
        return pl.BlockSpec((block, columns), lambda i: (i, 0))

    def whole(array):
        return pl.BlockSpec(array.shape, lambda i: (0, 0))

    def half(columns):
        return pl.BlockSpec((block // 2, columns), lambda i: (i, 0))

    shape = pltpu.HBM
    q_gain = q_gain[None]
    k_gain = k_gain[None]
    return pl.pallas_call(
        functools.partial(attend_kernel, head_dim=head_dim),
        grid=(count,),
        in_specs=[
            pl.BlockSpec(memory_space=pltpu.SMEM),
            pl.BlockSpec(memory_space=pltpu.SMEM),
            tile(width),
            whole(w_query),
            whole(w_kv),
            whole(w_out),
            whole(q_gain),
            whole(k_gain),
            tile(head_dim),
            tile(head_dim),
        ],
        out_specs=[
            half(width),
            half(width),
            tile(head_width),
            tile(head_dim),
            tile(head_dim),
            tile(head_width),
            pl.BlockSpec((1, 8, heads * block), lambda i: (i, 0, 0)),
            tile(head_dim),
        ],
        out_shape=[
            shape((slots // 2, width), jnp.bfloat16),
            shape((slots // 2, width), jnp.bfloat16),
            shape((slots, head_width), jnp.bfloat16),
            shape((slots, head_dim), jnp.bfloat16),
            shape((slots, head_dim), jnp.bfloat16),
            shape((slots, head_width), jnp.bfloat16),
            shape((count, 8, heads * block), jnp.float32),
            shape((slots, head_dim), jnp.float32),
        ],
        scratch_shapes=[
            pltpu.VMEM((slots, head_dim), jnp.bfloat16),
            pltpu.VMEM((slots, 2 * head_dim), jnp.bfloat16),
            pltpu.VMEM((heads * block, 2 * head_dim), jnp.float32),
            pltpu.VMEM((8, heads * block), jnp.float32),
            pltpu.VMEM((block, width), jnp.bfloat16),
        ],
        compiler_params=pltpu.CompilerParams(vmem_limit_bytes=kernel_vmem),
        cost_estimate=pl.CostEstimate(
            flops=2 * slots * width * (2 * head_width + 2 * head_dim)
            + 3 * slots * slots * head_width,
            bytes_accessed=4 * slots * width + 4 * width * head_width,
            transcendentals=slots * slots * heads // 2,
        ),
        name="attend_rows",
    )(
        ends,
        place,
        keep(rows),
        keep(w_query),
        keep(w_kv),
        keep(w_out),
        q_gain,
        k_gain,
        keep(cosine),
        keep(sine),
    )


def attend_back_kernel(
    ends_ref,
    grad_ref,
    out_w_ref,
    query_ref,
    heads_ref,
    key_ref,
    value_ref,
    log_ref,
    scale_ref,
    query_gain_ref,
    key_gain_ref,
    cosine_ref,
    sine_ref,
    grad_query_ref,
    grad_kv_ref,
    grad_query_gain_ref,
    grad_key_gain_ref,
    grad_keys,
    grad_values,
    grad_queries,
    *,
    head_dim,
):
    step = pl.program_id(0)
    block = query_ref.shape[0]
    heads = query_ref.shape[1] // head_dim
    ends = [ends_ref[k] for k in range(ends_ref.shape[0])]
    softmax_scale = head_dim ** (-0.5)

    @pl.when(step == 0)
    def _():
        grad_keys[...] = jnp.zeros_like(grad_keys)
        grad_values[...] = jnp.zeros_like(grad_values)
        grad_query_gain_ref[...] = jnp.zeros_like(grad_query_gain_ref)

    grad_heads = lanes_dot(grad_ref[...], out_w_ref[...]).astype(jnp.bfloat16)
    query = query_ref[...]
    out = heads_ref[...]
    cuts = [slice(h * head_dim, (h + 1) * head_dim) for h in range(heads)]
    queries = jnp.concatenate([query[:, cut] for cut in cuts], axis=0)
    grads = jnp.concatenate([grad_heads[:, cut] for cut in cuts], axis=0)
    outs = jnp.concatenate([out[:, cut] for cut in cuts], axis=0)
    products = grads.astype(jnp.float32) * outs.astype(jnp.float32)
    high = products.astype(jnp.bfloat16)
    rest = (products - high.astype(jnp.float32)).astype(jnp.bfloat16)
    ones = jnp.ones((8, head_dim), jnp.bfloat16)
    centre = (lanes_dot(ones, high) + lanes_dot(ones, rest))[:1]
    logs = log_ref[0, :1, :]
    column_ids = step * block + lax.broadcasted_iota(jnp.int32, (1, block), 1)
    starts = row_starts(column_ids, ends)
    grad_queries[...] = jnp.zeros_like(grad_queries)

    def one_block(j, carry):
        there = pl.ds(pl.multiple_of(j * block, block), block)
        key = key_ref[there, :]
        value = value_ref[there, :]
        scores = lanes_dot(key, queries) * softmax_scale - logs
        grad_probs = lanes_dot(value, grads) - centre
        row_ids = j * block + lax.broadcasted_iota(jnp.int32, (block, block), 0)
        allowed = (row_ids <= column_ids) & (row_ids >= starts)
        probs = jnp.concatenate(
            [
                jnp.where(allowed, jnp.exp(scores[:, h * block : (h + 1) * block]), 0.0)
                for h in range(heads)
            ],
            axis=1,
        )
        probs_low = probs.astype(jnp.bfloat16)
        grad_scores = (probs * grad_probs).astype(jnp.bfloat16)
        grad_values[there, :] += jnp.dot(probs_low, grads, preferred_element_type=jnp.float32)
        grad_keys[there, :] += jnp.dot(grad_scores, queries, preferred_element_type=jnp.float32)
        grad_queries[...] += lax.dot_general(
            grad_scores, key, (((0,), (0,)), ((), ())), preferred_element_type=jnp.float32
        )
        return carry

    first = row_starts(step * block, ends) // block
    lax.fori_loop(first, step + 1, one_block, 0)

    def prep_back(grad, low, gain, cosine, sine, scale):
        grad = grad * softmax_scale
        low = low.astype(jnp.float32)
        grad_gained = grad * cosine - turn_halves(grad) * sine
        normed = (low * cosine - turn_halves(low) * sine) / gain
        grad_gain = jnp.sum(grad_gained * normed, axis=0, keepdims=True)
        grad_normed = grad_gained * gain
        mean = jnp.mean(grad_normed * normed, axis=-1, keepdims=True)
        return scale * (grad_normed - normed * mean), grad_gain

    own = pl.ds(pl.multiple_of(step * block, block), block)
    cosine = cosine_ref[own, :]
    sine = sine_ref[own, :]
    scales = scale_ref[own, :]
    for h, cut in enumerate(cuts):
        grad_pre, grad_gain = prep_back(
            grad_queries[h * block : (h + 1) * block, :],
            query[:, cut],
            query_gain_ref[...],
            cosine,
            sine,
            scales[:, h : h + 1],
        )
        grad_query_ref[:, cut] = grad_pre.astype(jnp.bfloat16)
        grad_query_gain_ref[...] += grad_gain

    @pl.when(step == pl.num_programs(0) - 1)
    def _():
        grad_pre, grad_gain = prep_back(
            grad_keys[...],
            key_ref[...],
            key_gain_ref[...],
            cosine_ref[...],
            sine_ref[...],
            scale_ref[:, heads : heads + 1],
        )
        grad_kv_ref[:, :head_dim] = grad_pre.astype(jnp.bfloat16)
        grad_kv_ref[:, head_dim:] = grad_values[...].astype(jnp.bfloat16)
        grad_key_gain_ref[...] = grad_gain


def attend_rows_back(
    ends, grad, w_out, query, heads_low, key, value, logs, scales, q_gain, k_gain, cosine, sine, block
):
    slots, width = grad.shape
    head_dim = q_gain.shape[0]
    head_width = query.shape[1]
    heads = head_width // head_dim
    count = slots // block

    def tile(columns):
        return pl.BlockSpec((block, columns), lambda i: (i, 0))

    def whole(array):
        return pl.BlockSpec(array.shape, lambda i: (0, 0))

    shape = pltpu.HBM
    q_gain = q_gain[None]
    k_gain = k_gain[None]
    return pl.pallas_call(
        functools.partial(attend_back_kernel, head_dim=head_dim),
        grid=(count,),
        in_specs=[
            pl.BlockSpec(memory_space=pltpu.SMEM),
            tile(width),
            whole(w_out),
            tile(head_width),
            tile(head_width),
            whole(key),
            whole(value),
            pl.BlockSpec((1, 8, heads * block), lambda i: (i, 0, 0)),
            whole(scales),
            whole(q_gain),
            whole(k_gain),
            whole(cosine),
            whole(sine),
        ],
        out_specs=[
            tile(head_width),
            pl.BlockSpec((slots, 2 * head_dim), lambda i: (0, 0)),
            pl.BlockSpec((1, head_dim), lambda i: (0, 0)),
            pl.BlockSpec((1, head_dim), lambda i: (0, 0)),
        ],
        out_shape=[
            shape((slots, head_width), jnp.bfloat16),
            shape((slots, 2 * head_dim), jnp.bfloat16),
            shape((1, head_dim), jnp.float32),
            shape((1, head_dim), jnp.float32),
        ],
        scratch_shapes=[
            pltpu.VMEM((slots, head_dim), jnp.float32),
            pltpu.VMEM((slots, head_dim), jnp.float32),
            pltpu.VMEM((heads * block, head_dim), jnp.float32),
        ],
        compiler_params=pltpu.CompilerParams(vmem_limit_bytes=kernel_vmem),
        cost_estimate=pl.CostEstimate(
            flops=2 * slots * width * head_width + 6 * slots * slots * head_width,
            bytes_accessed=2 * slots * width + 2 * width * head_width,
            transcendentals=slots * slots * heads // 2,
        ),
        name="attend_rows_back",
    )(
        ends,
        keep(grad),
        keep(w_out),
        keep(query),
        keep(heads_low),
        keep(key),
        keep(value),
        keep(logs),
        keep(scales),
        q_gain,
        k_gain,
        keep(cosine),
        keep(sine),
    )


def transposed_times(left, right):
    return lax.dot_general(
        left, right, (((0,), (0,)), ((), ())), preferred_element_type=jnp.float32
    )


plane_axes = ("row", "col")


def move_plane(parts):
    return lax.all_to_all(parts, plane_axes, split_axis=0, concat_axis=0, tiled=True)


def rotate(block, axis, step):
    size = lax.axis_size(axis)
    return lax.ppermute(block, axis, [(i, (i + step) % size) for i in range(size)])


def gather_planes(block):
    planes = lax.axis_size("expert")
    return jnp.stack([block] + [rotate(block, "expert", k) for k in range(1, planes)], axis=0)


def return_planes(parts):
    return [parts[0]] + [rotate(parts[k], "expert", -k) for k in range(1, parts.shape[0])]


def parts_of(width, sixteenths):
    return [width * sixteenths // 16, width - width * sixteenths // 16]


def together(*values):
    return lax.optimization_barrier(values)


def move_all(parts):
    return lax.all_to_all(
        parts, ("expert",) + plane_axes, split_axis=0, concat_axis=0, tiled=True
    )


def sum_all(values):
    devices = lax.axis_size(("expert",) + plane_axes)
    padded = jnp.pad(values, (0, -values.shape[0] % (devices * 128)))
    total = jnp.sum(move_all(padded.reshape(devices, -1, 128)), axis=0)
    return move_all(jnp.broadcast_to(total[None], (devices,) + total.shape)).reshape(-1)


def line_step(value, step, hop):
    planes = lax.axis_size("expert")
    if hop > 0:
        pairs = [(i, i + 1) for i in range(*step)]
    else:
        pairs = [(planes - 1 - i, planes - 2 - i) for i in range(*step)]
    return lax.ppermute(value, "expert", pairs)


def send_planes(product):
    planes = lax.axis_size("expert")
    plane = lax.axis_index("expert")
    shares = product.reshape(planes, -1, product.shape[1])

    def share(k):
        return lax.dynamic_index_in_dim(shares, (plane + k) % planes, 0, keepdims=False)

    return [share(0)] + [rotate(share(k), "expert", k) for k in range(1, planes)]


def spread_planes(total):
    planes = lax.axis_size("expert")
    arrived = []
    for hop in (1, -1):
        message = total
        for k in range(1, planes):
            message = line_step(message, (k - 1, planes - 1), hop)
            arrived.append((k, hop, message))
    arrived.sort(key=lambda entry: -entry[0])
    return [message for _, _, message in arrived] + [total]


def in_plane_order(parts):
    planes = lax.axis_size("expert")
    plane = lax.axis_index("expert")
    rows = parts[0].shape[0]
    result = jnp.zeros((planes * rows, parts[0].shape[1]), jnp.float32)
    places = [plane - hop * k for k in range(planes - 1, 0, -1) for hop in (1, -1)] + [plane]
    for place, part in zip(places, parts):
        result = lax.dynamic_update_slice_in_dim(
            result, part.astype(jnp.float32), jnp.clip(place, 0, planes - 1) * rows, axis=0
        )
    return result


def scatter_cols(product):
    col = lax.axis_index("col")
    cols = lax.axis_size("col")
    moved = [rotate(product((col + k) % cols).astype(jnp.bfloat16), "col", k) for k in range(1, cols)]
    total = product(col)
    for part in moved:
        total = total + part.astype(jnp.float32)
    return total.astype(jnp.bfloat16)


def scatter_rows(parts):
    row = lax.axis_index("row")
    rows = lax.axis_size("row")

    def piece(k):
        return lax.dynamic_index_in_dim(parts, (row + k) % rows, 0, keepdims=False)

    arrived = [rotate(piece(k), "row", k) for k in range(1, rows)]
    result = piece(0).astype(jnp.float32)
    for part in arrived:
        result = result + part.astype(jnp.float32)
    return result


def split_columns(refs, widths, low, high):
    base = 0
    for ref, width in zip(refs, widths):
        first, last = max(low, base), min(high, base + width)
        if first < last:
            yield ref, slice(first - base, last - base), slice(first - low, last - low)
        base += width


def expert_kernel(
    ids_ref,
    router_ref,
    gate_ref,
    up_ref,
    down_ref,
    *refs,
    count,
    grads_widths,
    weighted_widths,
    experts,
):
    rows_refs, refs = refs[:count], refs[count:]
    grads_refs, refs = refs[: len(grads_widths)], refs[len(grads_widths) :]
    sends, refs = refs[:count], refs[count:]
    weighted, refs = refs[: len(weighted_widths)], refs[len(weighted_widths) :]
    rows_out, grads_out, hidden_out, grad_gate_out, grad_up_out = refs
    width = rows_refs[0].shape[1]
    cuts = [slice(i * width, (i + 1) * width) for i in range(count)]
    rows = [ref[...] for ref in rows_refs]
    chosen = grads_refs[0][:, grads_widths[0] :].astype(jnp.float32) > 0.5
    lanes = lax.broadcasted_iota(jnp.int32, chosen.shape, 1)

    def times(weights_ref):
        return sum(
            jnp.dot(part, weights_ref[cut, :], preferred_element_type=jnp.float32)
            for part, cut in zip(rows, cuts)
        )

    logits = times(router_ref)
    top = jnp.max(jnp.where(chosen, logits, -3e38), axis=1, keepdims=True)
    raised = jnp.where(chosen, jnp.exp(jnp.where(chosen, logits - top, 0.0)), 0.0)
    own = jnp.sum(jnp.where(lanes == ids_ref[0], raised, 0.0), axis=1, keepdims=True)
    gates = own / jnp.maximum(jnp.sum(raised, axis=1, keepdims=True), 1e-30)
    gate_pre = times(gate_ref)
    up_pre = times(up_ref)
    sigmoid = 1.0 / (1.0 + jnp.exp(-gate_pre))
    silu = gate_pre * sigmoid
    hidden = (silu * up_pre).astype(jnp.bfloat16)
    hidden_out[...] = hidden
    dots = jnp.zeros(gates.shape, jnp.float32)
    grad_hidden = jnp.zeros(gate_pre.shape, jnp.float32)
    for i, cut in enumerate(cuts):
        out = jnp.dot(hidden, down_ref[:, cut], preferred_element_type=jnp.float32)
        out = out.astype(jnp.bfloat16).astype(jnp.float32)
        grads = jnp.concatenate(
            [
                ref[:, part].astype(jnp.float32)
                for ref, part, _ in split_columns(grads_refs, grads_widths, cut.start, cut.stop)
            ],
            axis=1,
        )
        dots = dots + jnp.sum(out * grads, axis=1, keepdims=True)
        gated = (out * gates).astype(jnp.bfloat16)
        for ref, part, own in split_columns(weighted, weighted_widths, cut.start, cut.stop):
            ref[:, part] = gated[:, own]
        grads_low = (grads * gates).astype(jnp.bfloat16)
        grads_out[:, cut] = grads_low
        rows_out[:, cut] = rows[i]
        grad_hidden = grad_hidden + lanes_dot(grads_low, down_ref[:, cut])
    grad_gate = (grad_hidden * up_pre * sigmoid * (1.0 + gate_pre * (1.0 - sigmoid))).astype(
        jnp.bfloat16
    )
    grad_up = (grad_hidden * silu).astype(jnp.bfloat16)
    grad_gate_out[...] = grad_gate
    grad_up_out[...] = grad_up
    for i, cut in enumerate(cuts):
        sends[i][:, :width] = (
            lanes_dot(grad_gate, gate_ref[cut, :]) + lanes_dot(grad_up, up_ref[cut, :])
        ).astype(jnp.bfloat16)
    dots_high = dots.astype(jnp.bfloat16).astype(jnp.float32)
    side = jnp.where(lanes == ids_ref[1], dots_high, 0.0) + jnp.where(
        lanes == ids_ref[1] + experts, dots - dots_high, 0.0
    )
    sends[0][:, width:] = side.astype(jnp.bfloat16)


def expert_rows(
    ids, w_router, w_gate, w_up, w_down, rows, grads, grads_widths, weighted_widths, plane_size
):
    count = len(rows)
    slots, width = rows[0].shape
    model_width, hidden = w_gate.shape
    side = grads[0].shape[1] - grads_widths[0]
    block = slots // expert_steps

    def tile(columns):
        return pl.BlockSpec((block, columns), lambda i: (i, 0))

    def whole(array):
        return pl.BlockSpec(array.shape, lambda i: (0, 0), pipeline_mode=pl.Buffered(1))

    def shape(columns):
        return pltpu.HBM((slots, columns), jnp.bfloat16)

    sides = [width + side] + [width] * (count - 1)
    outs = sides + list(weighted_widths) + [model_width, model_width, hidden, hidden, hidden]
    flops = 2 * slots * model_width * hidden * 6
    return pl.pallas_call(
        functools.partial(
            expert_kernel,
            count=count,
            grads_widths=tuple(grads_widths),
            weighted_widths=tuple(weighted_widths),
            experts=plane_size,
        ),
        grid=(expert_steps,),
        in_specs=[pl.BlockSpec(memory_space=pltpu.SMEM)]
        + [whole(array) for array in (w_router, w_gate, w_up, w_down)]
        + [tile(width)] * count
        + [tile(array.shape[1]) for array in grads],
        out_specs=[tile(columns) for columns in outs],
        out_shape=[shape(columns) for columns in outs],
        compiler_params=pltpu.CompilerParams(vmem_limit_bytes=expert_vmem),
        cost_estimate=pl.CostEstimate(
            flops=flops, bytes_accessed=6 * model_width * hidden, transcendentals=slots * hidden
        ),
        name="expert_rows",
    )(ids, w_router, w_gate, w_up, w_down, *rows, *grads)


def local(
    layer_input,
    norm_attn,
    w_query,
    w_key,
    w_value,
    q_gain,
    k_gain,
    w_out,
    norm_moe,
    w_router,
    w_gate,
    w_up,
    w_down,
    seq_lengths,
    routes,
    out_grad,
):
    tok_dev = layer_input.shape[0]
    model_width = layer_input.shape[1]
    group_tok = tok_dev * lax.axis_size(("row", "col"))
    head_dim = q_gain.shape[0]
    experts = w_router.shape[1]
    top_count = routes.shape[1]
    capacity = tok_dev * top_count * 17 // (16 * experts)
    planes = lax.axis_size("expert")
    plane_size = lax.axis_size(plane_axes)
    plane_index = lax.axis_index("expert")
    plane_cap = planes * capacity
    chosen_here = jnp.any(
        routes[:, :, None] == jnp.arange(experts, dtype=jnp.int32)[None, None, :], axis=1
    )
    plane_routes = gather_planes(routes.T)
    plane_experts = plane_index * plane_size + jnp.arange(plane_size, dtype=jnp.int32)
    chosen_plane = jnp.any(
        plane_routes[None] == plane_experts[:, None, None, None], axis=2
    )
    token_ids = jnp.arange(tok_dev, dtype=jnp.int32)
    earlier = (token_ids[:, None] < token_ids[None, :]).astype(jnp.bfloat16)
    slot_rank = jnp.dot(
        chosen_plane.astype(jnp.bfloat16).reshape(plane_size * planes, tok_dev),
        earlier,
        preferred_element_type=jnp.float32,
    ).astype(jnp.int32).reshape(plane_size, planes, tok_dev)
    plane_slot = jnp.where(
        chosen_plane,
        slot_rank + (jnp.arange(planes, dtype=jnp.int32) * capacity)[None, :, None],
        -1,
    ).reshape(plane_size, 1, planes * tok_dev)
    dispatch = (
        plane_slot == jnp.arange(plane_cap, dtype=jnp.int32)[None, :, None]
    ).astype(jnp.bfloat16)
    chosen_all = jnp.any(
        plane_routes[:, :, :, None] == jnp.arange(experts, dtype=jnp.int32), axis=1
    ).reshape(planes * tok_dev, experts).astype(jnp.bfloat16)

    def gather_rows(block):
        return gather_planes(block).reshape(planes * tok_dev, block.shape[1])

    def select_slots(rows_all):
        return jnp.dot(
            dispatch.reshape(plane_size * plane_cap, -1),
            rows_all,
            preferred_element_type=jnp.float32,
        ).astype(jnp.bfloat16)

    def to_plane(slot_values):
        width = slot_values.shape[1]
        moved = move_plane(slot_values.reshape(plane_size, plane_cap, width))
        return moved.reshape(plane_size * plane_cap, width)

    chunk_width = model_width // chunk_count
    chunks = [slice(i * chunk_width, (i + 1) * chunk_width) for i in range(chunk_count)]
    side_width = 128
    grads_widths = parts_of(model_width, grads_first)
    weighted_widths = parts_of(model_width, weighted_first)
    grad_planes = [gather_rows(part) for part in jnp.split(out_grad, [grads_widths[0]], axis=1)]
    grad_planes[0] = jnp.concatenate(
        [grad_planes[0], jnp.pad(chosen_all, ((0, 0), (0, side_width - experts)))], axis=1
    )
    slot_sends = [select_slots(part) for part in grad_planes]
    def gates_of(all_logits, chosen):
        top = jnp.max(jnp.where(chosen, all_logits, -3e38), axis=1, keepdims=True)
        raised = jnp.where(chosen, jnp.exp(jnp.where(chosen, all_logits - top, 0.0)), 0.0)
        return raised / jnp.maximum(jnp.sum(raised, axis=1, keepdims=True), 1e-30)

    input_rows = layer_input.astype(jnp.float32)
    normed_one, norm_one_back = jax.vjp(rms_scale, input_rows, norm_attn)
    normed_low = normed_one.astype(jnp.bfloat16)
    group_rows = lax.all_gather(normed_low, ("row", "col"), axis=0, tiled=True)
    ends = jnp.cumsum(seq_lengths[0], dtype=jnp.int32)
    cosine_table, sine_table = rope_tables(slot_positions(ends, group_tok), head_dim)
    key_value_w = jnp.concatenate([w_key, w_value], axis=1)
    cosine_table, sine_table, key_value_w, slot_sends[0] = together(
        cosine_table, sine_table, key_value_w, slot_sends[0]
    )
    grad_slot_chunks = [to_plane(slot_sends[0])]
    col = lax.axis_index("col")
    kept, sent, query_low, key_low, value_low, heads_low, log_totals, head_scales = attend_rows(
        ends, col.astype(jnp.int32)[None], group_rows, w_query, key_value_w, w_out, q_gain, k_gain, cosine_table, sine_table,
        2 * tok_dev,
    )
    sent, kept, grad_slot_chunks[0] = together(sent, kept, grad_slot_chunks[0])
    col_sums = kept.astype(jnp.float32) + rotate(sent, "col", 1).astype(jnp.float32)
    attn_rows = scatter_rows(col_sums.astype(jnp.bfloat16).reshape(-1, tok_dev, model_width))
    attn_rows, *late_sends = together(attn_rows, *slot_sends[1:])
    grad_slot_chunks += [to_plane(part) for part in late_sends]
    attn_rows = attn_rows.astype(jnp.float32)
    mixed_rows = input_rows + attn_rows
    normed_two, norm_two_back = jax.vjp(rms_scale, mixed_rows, norm_moe)
    moe_input = normed_two.astype(jnp.bfloat16)
    router_logits = jnp.dot(moe_input, w_router, preferred_element_type=jnp.float32)
    source_gates = gates_of(router_logits, chosen_here)

    moe_planes = [gather_rows(moe_input[:, cut]) for cut in chunks]
    moe_sends = [select_slots(part) for part in moe_planes]
    moe_sends[0], *grad_slot_chunks[1:] = together(moe_sends[0], *grad_slot_chunks[1:])
    slot_chunks = [to_plane(part) for part in moe_sends]
    place = lax.axis_index(plane_axes)
    ids = jnp.stack([plane_index * plane_size + place, place]).astype(jnp.int32)
    expert_outs = expert_rows(
        ids,
        jnp.pad(w_router, ((0, 0), (0, side_width - experts))),
        w_gate[0],
        w_up[0],
        w_down[0],
        slot_chunks,
        grad_slot_chunks,
        grads_widths,
        weighted_widths,
        plane_size,
    )
    grad_sends = expert_outs[:chunk_count]
    out_sends = expert_outs[chunk_count : chunk_count + len(weighted_widths)]
    moe_slots, grad_out_slots, hidden_low, grad_gate_pre, grad_up_pre = expert_outs[
        chunk_count + len(weighted_widths) :
    ]

    def to_source(returned):
        summed = lax.dot_general(
            dispatch.reshape(plane_size * plane_cap, -1),
            returned,
            (((0,), (0,)), ((), ())),
            preferred_element_type=jnp.float32,
        ).astype(jnp.bfloat16)
        return return_planes(summed.reshape(planes, tok_dev, returned.shape[1]))

    def add_parts(parts):
        return sum(part.astype(jnp.float32) for part in parts)

    grad_rows = out_grad.astype(jnp.float32)
    grad_down = transposed_times(hidden_low, grad_out_slots)
    grad_gate = transposed_times(moe_slots, grad_gate_pre)
    grad_up = transposed_times(moe_slots, grad_up_pre)
    grad_returns = [to_plane(part) for part in grad_sends]
    grad_returns[0], grad_down = together(grad_returns[0], grad_down)
    grad_returns[-1], grad_gate, *out_sends = together(grad_returns[-1], grad_gate, *out_sends)
    out_returns = [to_plane(out_sends[0])]
    grad_parts = [to_source(part) for part in grad_returns]
    grad_parts[-1][-1], grad_up = together(grad_parts[-1][-1], grad_up)
    side_parts = jnp.stack(
        [part[:, chunk_width:].astype(jnp.float32) for part in grad_parts[0]], axis=0
    )
    dot_parts = side_parts[:, :, :plane_size] + side_parts[:, :, plane_size : 2 * plane_size]
    dot_parts = lax.dynamic_slice_in_dim(
        jnp.concatenate([dot_parts, dot_parts], axis=0), planes - plane_index, planes, axis=0
    )
    grad_gates = jnp.swapaxes(dot_parts, 0, 1).reshape(tok_dev, experts)
    grad_logits = source_gates * (
        grad_gates - jnp.sum(source_gates * grad_gates, axis=1, keepdims=True)
    )
    grad_parts[0] = [part[:, :chunk_width] for part in grad_parts[0]]
    grad_moe_input = jnp.concatenate([add_parts(parts) for parts in grad_parts], axis=1)
    grad_router = lax.dot_general(
        grad_logits,
        moe_input.astype(jnp.float32),
        (((0,), (0,)), ((), ())),
        precision=highest,
        preferred_element_type=jnp.float32,
    )
    grad_moe_input = grad_moe_input + jnp.einsum(
        "te,de->td", grad_logits, w_router, precision=highest, preferred_element_type=jnp.float32
    )
    grad_mixed_norm, grad_norm_moe = norm_two_back(grad_moe_input)
    grad_mixed = grad_rows + grad_mixed_norm
    grad_attn_low = grad_mixed.astype(jnp.bfloat16)
    grad_attn_low, out_returns[0] = together(grad_attn_low, out_returns[0])
    grad_group = lax.all_gather(grad_attn_low, ("row", "col"), axis=0, tiled=True)
    out_first = add_parts(to_source(out_returns[0]))
    grad_group, out_first, *out_late = together(grad_group, out_first, *out_sends[1:])
    out_returns += [to_plane(part) for part in out_late]
    grad_out_proj = transposed_times(heads_low, grad_group).astype(jnp.bfloat16)
    grad_out_proj, grad_group = together(grad_out_proj, grad_group)
    out_terms = send_planes(grad_out_proj)
    grad_query_low, grad_kv, grad_q_gain, grad_k_gain = attend_rows_back(
        ends,
        grad_group,
        w_out,
        query_low,
        heads_low,
        key_low,
        value_low,
        log_totals,
        head_scales,
        q_gain,
        k_gain,
        cosine_table,
        sine_table,
        2 * tok_dev,
    )
    grad_query_low, grad_kv, out_terms[1], out_terms[-1] = together(
        grad_query_low, grad_kv, out_terms[1], out_terms[-1]
    )
    grad_query = transposed_times(group_rows, grad_query_low)
    grad_key_value = transposed_times(group_rows, grad_kv)
    norm_terms = (
        jnp.sum(grad_query * w_query.astype(jnp.float32), axis=1)
        + jnp.sum(grad_key_value * key_value_w.astype(jnp.float32), axis=1)
    ) / norm_attn
    cols = lax.axis_size("col")
    col = lax.axis_index("col")
    kv_low = grad_key_value.astype(jnp.bfloat16).reshape(cols, -1, 2 * head_dim)
    kv_part = lax.dynamic_index_in_dim(kv_low, col, 0, keepdims=False).astype(jnp.float32)
    for k in range(1, cols):
        kv_part = kv_part + rotate(
            lax.dynamic_index_in_dim(kv_low, (col + k) % cols, 0, keepdims=False), "col", k
        ).astype(jnp.float32)
    lane_parts = grad_query.shape[1] // (2 * head_dim)
    query_kv = jnp.concatenate(
        [
            grad_query.astype(jnp.bfloat16),
            *[
                jnp.concatenate(jnp.split(kv_part.astype(jnp.bfloat16), lane_parts), axis=1)
            ],
        ],
        axis=0,
    )
    query_kv = lax.psum(query_kv, "expert")
    left_parts = jnp.concatenate([grad_query_low, grad_kv], axis=1).reshape(
        -1, cols, tok_dev, grad_query_low.shape[1] + 2 * head_dim
    )
    right_all = jnp.concatenate([w_query, key_value_w], axis=1)

    def grad_normed_rows(place):
        left = lax.dynamic_index_in_dim(left_parts, place, 1, keepdims=False)
        return lax.dot_general(
            left, right_all, (((2,), (1,)), ((), ())), preferred_element_type=jnp.float32
        )

    out_share = add_parts(out_terms).astype(jnp.bfloat16)
    summed_values = jnp.concatenate(
        [grad_router.reshape(-1), grad_norm_moe, norm_terms, grad_q_gain[0], grad_k_gain[0]]
    )
    left_parts, out_share, summed_values = together(left_parts, out_share, summed_values)
    sums = sum_all(summed_values)
    out_shares = spread_planes(out_share)
    col_sums = scatter_cols(grad_normed_rows)
    col_sums, *out_returns[1:] = together(col_sums, *out_returns[1:])
    out_parts = [out_first] + [add_parts(to_source(part)) for part in out_returns[1:]]
    grad_normed = scatter_rows(col_sums)
    grad_normed, sums, query_kv, *out_parts = together(grad_normed, sums, query_kv, *out_parts)
    out_rows = (mixed_rows + jnp.concatenate(out_parts, axis=1)).astype(jnp.bfloat16)
    grad_out_proj = in_plane_order(out_shares)
    places = (0, experts * model_width, model_width, model_width, head_dim, head_dim)
    ends_at = [sum(places[: k + 1]) for k in range(len(places))]
    grad_router, grad_norm_moe, grad_norm_attn, grad_q_gain, grad_k_gain = [
        sums[low:high] for low, high in zip(ends_at[:-1], ends_at[1:])
    ]
    grad_router = grad_router.reshape(experts, model_width).T
    grad_query = query_kv[:model_width].astype(jnp.float32)
    kv_part = query_kv[model_width:]
    kv_parts = [kv_part] + [rotate(kv_part, "col", k) for k in range(1, cols)]
    kv_blocks = []
    for place in range(cols):
        block = kv_parts[0]
        for k in range(1, cols):
            block = jnp.where((col - k) % cols == place, kv_parts[k], block)
        kv_blocks += jnp.split(block.astype(jnp.float32), lane_parts, axis=1)
    grad_key = jnp.concatenate([block[:, :head_dim] for block in kv_blocks], axis=0)
    grad_value = jnp.concatenate([block[:, head_dim:] for block in kv_blocks], axis=0)
    grad_input_norm = norm_one_back(grad_normed)[0]
    grad_x = (grad_mixed + grad_input_norm).astype(jnp.bfloat16)
    return (
        out_rows,
        grad_x,
        grad_norm_attn,
        grad_query,
        grad_key,
        grad_value,
        grad_q_gain,
        grad_k_gain,
        grad_out_proj,
        grad_norm_moe,
        grad_router,
        grad_gate[None],
        grad_up[None],
        grad_down[None],
    )


def solution(mesh):
    placed = (
        P(("expert", "row", "col"), None),
        P(),
        P(None, ("row", "col")),
        P(None, "row"),
        P(None, "row"),
        P(),
        P(),
        P(("row", "col"), None),
        P(),
        P(),
        P(("expert", "row", "col"), None, None),
        P(("expert", "row", "col"), None, None),
        P(("expert", "row", "col"), None, None),
        P("expert", None),
        P(("expert", "row", "col"), None),
        P(("expert", "row", "col"), None),
    )
    return jax.shard_map(
        local,
        mesh=mesh,
        in_specs=placed,
        out_specs=(
            P(("expert", "row", "col"), None),
            P(("expert", "row", "col"), None),
            P(),
            P(None, ("row", "col")),
            P(None, "row"),
            P(None, "row"),
            P(),
            P(),
            P(("row", "col"), None),
            P(),
            P(),
            P(("expert", "row", "col"), None, None),
            P(("expert", "row", "col"), None, None),
            P(("expert", "row", "col"), None, None),
        ),
        check_vma=False,
    )
```

```python
import functools

import jax
import jax.numpy as jnp
from jax import lax
from jax.experimental import pallas as pl
from jax.experimental.pallas import tpu as pltpu
from jax.sharding import PartitionSpec as P

eps_norm = 1e-06
rope_base = 1000000.0
highest = lax.Precision.HIGHEST
chunk_count = 2
grads_first = 7
weighted_first = 12
expert_steps = 2
expert_vmem = 56 * 1024 * 1024
kernel_vmem = 40 * 1024 * 1024


def rms_scale(values, norm_gain):
    return (
        values * lax.rsqrt(jnp.mean(values * values, axis=-1, keepdims=True) + eps_norm) * norm_gain
    )


def rope_tables(positions, head_dim):
    half_dim = head_dim // 2
    inverse = rope_base ** (-(jnp.arange(half_dim, dtype=jnp.float32) * 2.0 / head_dim))
    angles = positions.astype(jnp.float32)[:, None] * inverse[None, :]
    cosine = jnp.cos(angles)
    sine = jnp.sin(angles)
    return (jnp.concatenate([cosine, cosine], axis=1), jnp.concatenate([-sine, sine], axis=1))


def slot_positions(ends, slot_count):
    slot_ids = jnp.arange(slot_count, dtype=jnp.int32)
    starts = row_starts(slot_ids, [ends[k] for k in range(ends.shape[0])])
    return slot_ids - starts


def row_starts(row_ids, ends):
    starts = jnp.zeros_like(row_ids)
    for end in ends:
        starts = jnp.where(row_ids >= end, end, starts)
    return jnp.where(row_ids >= ends[-1], row_ids, starts)


def lanes_dot(left, right):
    return lax.dot_general(
        left, right, (((1,), (1,)), ((), ())), preferred_element_type=jnp.float32
    )


def turn_halves(values):
    return pltpu.roll(values, values.shape[-1] // 2, axis=1)


def keep(array):
    return pltpu.with_memory_space_constraint(array, pltpu.HBM)


def attend_kernel(
    ends_ref,
    place_ref,
    rows_ref,
    query_w_ref,
    kv_w_ref,
    out_w_ref,
    query_gain_ref,
    key_gain_ref,
    cosine_ref,
    sine_ref,
    kept_ref,
    sent_ref,
    query_ref,
    key_ref,
    value_ref,
    heads_ref,
    log_ref,
    scale_ref,
    keys,
    values,
    total,
    sums,
    partial,
    *,
    head_dim,
):
    step = pl.program_id(0)
    block = rows_ref.shape[0]
    heads = query_w_ref.shape[1] // head_dim
    ends = [ends_ref[k] for k in range(ends_ref.shape[0])]
    softmax_scale = head_dim ** (-0.5)
    rows = rows_ref[...]
    query_pre = jnp.dot(rows, query_w_ref[...], preferred_element_type=jnp.float32)
    kv_pre = jnp.dot(rows, kv_w_ref[...], preferred_element_type=jnp.float32)
    cosine = cosine_ref[...]
    sine = sine_ref[...]
    lanes = lax.broadcasted_iota(jnp.int32, (block, head_dim), 1)
    scales = jnp.zeros((block, head_dim), jnp.float32)

    def prep(vectors, gain):
        scale = lax.rsqrt(jnp.mean(vectors * vectors, axis=-1, keepdims=True) + eps_norm)
        gained = vectors * scale * gain
        return (gained * cosine + turn_halves(gained) * sine).astype(jnp.bfloat16), scale

    stacked = []
    for h in range(heads):
        cut = slice(h * head_dim, (h + 1) * head_dim)
        low, scale = prep(query_pre[:, cut], query_gain_ref[...])
        query_ref[:, cut] = low
        stacked.append(low)
        scales = jnp.where(lanes == h, scale, scales)
    key_low, scale = prep(kv_pre[:, :head_dim], key_gain_ref[...])
    scale_ref[...] = jnp.where(lanes == heads, scale, scales)
    value_low = kv_pre[:, head_dim:].astype(jnp.bfloat16)
    key_ref[...] = key_low
    value_ref[...] = value_low
    own = pl.ds(pl.multiple_of(step * block, block), block)
    keys[own, :] = key_low
    values[own, :head_dim] = value_low
    values[own, head_dim:] = jnp.ones((block, head_dim), jnp.bfloat16)
    queries = jnp.concatenate(stacked, axis=0)
    row_ids = step * block + lax.broadcasted_iota(jnp.int32, (block, 1), 0)
    starts = row_starts(row_ids, ends)
    total[...] = jnp.zeros_like(total)
    sums[...] = jnp.zeros_like(sums)
    ones = jnp.ones((8, block), jnp.bfloat16)

    def one_block(j, carry):
        there = pl.ds(pl.multiple_of(j * block, block), block)
        scores = lanes_dot(queries, keys[there, :]) * softmax_scale
        column_ids = j * block + lax.broadcasted_iota(jnp.int32, (block, block), 1)
        allowed = (column_ids <= row_ids) & (column_ids >= starts)
        weights = jnp.concatenate(
            [
                jnp.where(allowed, jnp.exp(scores[h * block : (h + 1) * block]), 0.0).astype(
                    jnp.bfloat16
                )
                for h in range(heads)
            ],
            axis=0,
        )
        total[...] += jnp.dot(weights, values[there, :], preferred_element_type=jnp.float32)
        sums[...] += lanes_dot(ones, weights)
        return carry

    first = row_starts(step * block, ends) // block
    lax.fori_loop(first, step + 1, one_block, 0)
    log_ref[0] = jnp.log(sums[...])
    outs = (total[:, :head_dim] / total[:, head_dim:]).astype(jnp.bfloat16)
    for h in range(heads):
        heads_ref[:, h * head_dim : (h + 1) * head_dim] = outs[h * block : (h + 1) * block]
    partial[...] = jnp.dot(
        heads_ref[...], out_w_ref[...], preferred_element_type=jnp.float32
    ).astype(jnp.bfloat16)
    share = kept_ref.shape[0]
    kept = pl.multiple_of(place_ref[0] * share, share)
    sent = pl.multiple_of((1 - place_ref[0]) * share, share)
    kept_ref[...] = partial[pl.ds(kept, share), :]
    sent_ref[...] = partial[pl.ds(sent, share), :]


def attend_rows(ends, place, rows, w_query, w_kv, w_out, q_gain, k_gain, cosine, sine, block):
    slots, width = rows.shape
    head_dim = q_gain.shape[0]
    head_width = w_query.shape[1]
    heads = head_width // head_dim
    count = slots // block

    def tile(columns):
        return pl.BlockSpec((block, columns), lambda i: (i, 0))

    def whole(array):
        return pl.BlockSpec(array.shape, lambda i: (0, 0))

    def half(columns):
        return pl.BlockSpec((block // 2, columns), lambda i: (i, 0))

    shape = pltpu.HBM
    q_gain = q_gain[None]
    k_gain = k_gain[None]
    return pl.pallas_call(
        functools.partial(attend_kernel, head_dim=head_dim),
        grid=(count,),
        in_specs=[
            pl.BlockSpec(memory_space=pltpu.SMEM),
            pl.BlockSpec(memory_space=pltpu.SMEM),
            tile(width),
            whole(w_query),
            whole(w_kv),
            whole(w_out),
            whole(q_gain),
            whole(k_gain),
            tile(head_dim),
            tile(head_dim),
        ],
        out_specs=[
            half(width),
            half(width),
            tile(head_width),
            tile(head_dim),
            tile(head_dim),
            tile(head_width),
            pl.BlockSpec((1, 8, heads * block), lambda i: (i, 0, 0)),
            tile(head_dim),
        ],
        out_shape=[
            shape((slots // 2, width), jnp.bfloat16),
            shape((slots // 2, width), jnp.bfloat16),
            shape((slots, head_width), jnp.bfloat16),
            shape((slots, head_dim), jnp.bfloat16),
            shape((slots, head_dim), jnp.bfloat16),
            shape((slots, head_width), jnp.bfloat16),
            shape((count, 8, heads * block), jnp.float32),
            shape((slots, head_dim), jnp.float32),
        ],
        scratch_shapes=[
            pltpu.VMEM((slots, head_dim), jnp.bfloat16),
            pltpu.VMEM((slots, 2 * head_dim), jnp.bfloat16),
            pltpu.VMEM((heads * block, 2 * head_dim), jnp.float32),
            pltpu.VMEM((8, heads * block), jnp.float32),
            pltpu.VMEM((block, width), jnp.bfloat16),
        ],
        compiler_params=pltpu.CompilerParams(vmem_limit_bytes=kernel_vmem),
        cost_estimate=pl.CostEstimate(
            flops=2 * slots * width * (2 * head_width + 2 * head_dim)
            + 3 * slots * slots * head_width,
            bytes_accessed=4 * slots * width + 4 * width * head_width,
            transcendentals=slots * slots * heads // 2,
        ),
        name="attend_rows",
    )(
        ends,
        place,
        keep(rows),
        keep(w_query),
        keep(w_kv),
        keep(w_out),
        q_gain,
        k_gain,
        keep(cosine),
        keep(sine),
    )


def attend_back_kernel(
    ends_ref,
    grad_ref,
    out_w_ref,
    query_ref,
    heads_ref,
    key_ref,
    value_ref,
    log_ref,
    scale_ref,
    query_gain_ref,
    key_gain_ref,
    cosine_ref,
    sine_ref,
    grad_query_ref,
    grad_kv_ref,
    grad_query_gain_ref,
    grad_key_gain_ref,
    grad_keys,
    grad_values,
    grad_queries,
    *,
    head_dim,
):
    step = pl.program_id(0)
    block = query_ref.shape[0]
    heads = query_ref.shape[1] // head_dim
    ends = [ends_ref[k] for k in range(ends_ref.shape[0])]
    softmax_scale = head_dim ** (-0.5)

    @pl.when(step == 0)
    def _():
        grad_keys[...] = jnp.zeros_like(grad_keys)
        grad_values[...] = jnp.zeros_like(grad_values)
        grad_query_gain_ref[...] = jnp.zeros_like(grad_query_gain_ref)

    grad_heads = lanes_dot(grad_ref[...], out_w_ref[...]).astype(jnp.bfloat16)
    query = query_ref[...]
    out = heads_ref[...]
    cuts = [slice(h * head_dim, (h + 1) * head_dim) for h in range(heads)]
    queries = jnp.concatenate([query[:, cut] for cut in cuts], axis=0)
    grads = jnp.concatenate([grad_heads[:, cut] for cut in cuts], axis=0)
    outs = jnp.concatenate([out[:, cut] for cut in cuts], axis=0)
    products = grads.astype(jnp.float32) * outs.astype(jnp.float32)
    high = products.astype(jnp.bfloat16)
    rest = (products - high.astype(jnp.float32)).astype(jnp.bfloat16)
    ones = jnp.ones((8, head_dim), jnp.bfloat16)
    centre = (lanes_dot(ones, high) + lanes_dot(ones, rest))[:1]
    logs = log_ref[0, :1, :]
    column_ids = step * block + lax.broadcasted_iota(jnp.int32, (1, block), 1)
    starts = row_starts(column_ids, ends)
    grad_queries[...] = jnp.zeros_like(grad_queries)

    def one_block(j, carry):
        there = pl.ds(pl.multiple_of(j * block, block), block)
        key = key_ref[there, :]
        value = value_ref[there, :]
        scores = lanes_dot(key, queries) * softmax_scale - logs
        grad_probs = lanes_dot(value, grads) - centre
        row_ids = j * block + lax.broadcasted_iota(jnp.int32, (block, block), 0)
        allowed = (row_ids <= column_ids) & (row_ids >= starts)
        probs = jnp.concatenate(
            [
                jnp.where(allowed, jnp.exp(scores[:, h * block : (h + 1) * block]), 0.0)
                for h in range(heads)
            ],
            axis=1,
        )
        probs_low = probs.astype(jnp.bfloat16)
        grad_scores = (probs * grad_probs).astype(jnp.bfloat16)
        grad_values[there, :] += jnp.dot(probs_low, grads, preferred_element_type=jnp.float32)
        grad_keys[there, :] += jnp.dot(grad_scores, queries, preferred_element_type=jnp.float32)
        grad_queries[...] += lax.dot_general(
            grad_scores, key, (((0,), (0,)), ((), ())), preferred_element_type=jnp.float32
        )
        return carry

    first = row_starts(step * block, ends) // block
    lax.fori_loop(first, step + 1, one_block, 0)

    def prep_back(grad, low, gain, cosine, sine, scale):
        grad = grad * softmax_scale
        low = low.astype(jnp.float32)
        grad_gained = grad * cosine - turn_halves(grad) * sine
        normed = (low * cosine - turn_halves(low) * sine) / gain
        grad_gain = jnp.sum(grad_gained * normed, axis=0, keepdims=True)
        grad_normed = grad_gained * gain
        mean = jnp.mean(grad_normed * normed, axis=-1, keepdims=True)
        return scale * (grad_normed - normed * mean), grad_gain

    own = pl.ds(pl.multiple_of(step * block, block), block)
    cosine = cosine_ref[own, :]
    sine = sine_ref[own, :]
    scales = scale_ref[own, :]
    for h, cut in enumerate(cuts):
        grad_pre, grad_gain = prep_back(
            grad_queries[h * block : (h + 1) * block, :],
            query[:, cut],
            query_gain_ref[...],
            cosine,
            sine,
            scales[:, h : h + 1],
        )
        grad_query_ref[:, cut] = grad_pre.astype(jnp.bfloat16)
        grad_query_gain_ref[...] += grad_gain

    @pl.when(step == pl.num_programs(0) - 1)
    def _():
        grad_pre, grad_gain = prep_back(
            grad_keys[...],
            key_ref[...],
            key_gain_ref[...],
            cosine_ref[...],
            sine_ref[...],
            scale_ref[:, heads : heads + 1],
        )
        grad_kv_ref[:, :head_dim] = grad_pre.astype(jnp.bfloat16)
        grad_kv_ref[:, head_dim:] = grad_values[...].astype(jnp.bfloat16)
        grad_key_gain_ref[...] = grad_gain


def attend_rows_back(
    ends, grad, w_out, query, heads_low, key, value, logs, scales, q_gain, k_gain, cosine, sine, block
):
    slots, width = grad.shape
    head_dim = q_gain.shape[0]
    head_width = query.shape[1]
    heads = head_width // head_dim
    count = slots // block

    def tile(columns):
        return pl.BlockSpec((block, columns), lambda i: (i, 0))

    def whole(array):
        return pl.BlockSpec(array.shape, lambda i: (0, 0))

    shape = pltpu.HBM
    q_gain = q_gain[None]
    k_gain = k_gain[None]
    return pl.pallas_call(
        functools.partial(attend_back_kernel, head_dim=head_dim),
        grid=(count,),
        in_specs=[
            pl.BlockSpec(memory_space=pltpu.SMEM),
            tile(width),
            whole(w_out),
            tile(head_width),
            tile(head_width),
            whole(key),
            whole(value),
            pl.BlockSpec((1, 8, heads * block), lambda i: (i, 0, 0)),
            whole(scales),
            whole(q_gain),
            whole(k_gain),
            whole(cosine),
            whole(sine),
        ],
        out_specs=[
            tile(head_width),
            pl.BlockSpec((slots, 2 * head_dim), lambda i: (0, 0)),
            pl.BlockSpec((1, head_dim), lambda i: (0, 0)),
            pl.BlockSpec((1, head_dim), lambda i: (0, 0)),
        ],
        out_shape=[
            shape((slots, head_width), jnp.bfloat16),
            shape((slots, 2 * head_dim), jnp.bfloat16),
            shape((1, head_dim), jnp.float32),
            shape((1, head_dim), jnp.float32),
        ],
        scratch_shapes=[
            pltpu.VMEM((slots, head_dim), jnp.float32),
            pltpu.VMEM((slots, head_dim), jnp.float32),
            pltpu.VMEM((heads * block, head_dim), jnp.float32),
        ],
        compiler_params=pltpu.CompilerParams(vmem_limit_bytes=kernel_vmem),
        cost_estimate=pl.CostEstimate(
            flops=2 * slots * width * head_width + 6 * slots * slots * head_width,
            bytes_accessed=2 * slots * width + 2 * width * head_width,
            transcendentals=slots * slots * heads // 2,
        ),
        name="attend_rows_back",
    )(
        ends,
        keep(grad),
        keep(w_out),
        keep(query),
        keep(heads_low),
        keep(key),
        keep(value),
        keep(logs),
        keep(scales),
        q_gain,
        k_gain,
        keep(cosine),
        keep(sine),
    )


def transposed_times(left, right):
    return lax.dot_general(
        left, right, (((0,), (0,)), ((), ())), preferred_element_type=jnp.float32
    )


plane_axes = ("row", "col")


def move_plane(parts):
    return lax.all_to_all(parts, plane_axes, split_axis=0, concat_axis=0, tiled=True)


def rotate(block, axis, step):
    size = lax.axis_size(axis)
    return lax.ppermute(block, axis, [(i, (i + step) % size) for i in range(size)])


def gather_planes(block):
    planes = lax.axis_size("expert")
    return jnp.stack([block] + [rotate(block, "expert", k) for k in range(1, planes)], axis=0)


def return_planes(parts):
    return [parts[0]] + [rotate(parts[k], "expert", -k) for k in range(1, parts.shape[0])]


def parts_of(width, sixteenths):
    return [width * sixteenths // 16, width - width * sixteenths // 16]


def together(*values):
    return lax.optimization_barrier(values)


def move_all(parts):
    return lax.all_to_all(
        parts, ("expert",) + plane_axes, split_axis=0, concat_axis=0, tiled=True
    )


def sum_all(values):
    devices = lax.axis_size(("expert",) + plane_axes)
    padded = jnp.pad(values, (0, -values.shape[0] % (devices * 128)))
    total = jnp.sum(move_all(padded.reshape(devices, -1, 128)), axis=0)
    return move_all(jnp.broadcast_to(total[None], (devices,) + total.shape)).reshape(-1)


def line_step(value, step, hop):
    planes = lax.axis_size("expert")
    if hop > 0:
        pairs = [(i, i + 1) for i in range(*step)]
    else:
        pairs = [(planes - 1 - i, planes - 2 - i) for i in range(*step)]
    return lax.ppermute(value, "expert", pairs)


def send_planes(product):
    planes = lax.axis_size("expert")
    plane = lax.axis_index("expert")
    shares = product.reshape(planes, -1, product.shape[1])

    def share(k):
        return lax.dynamic_index_in_dim(shares, (plane + k) % planes, 0, keepdims=False)

    return [share(0)] + [rotate(share(k), "expert", k) for k in range(1, planes)]


def spread_planes(total):
    planes = lax.axis_size("expert")
    arrived = []
    for hop in (1, -1):
        message = total
        for k in range(1, planes):
            message = line_step(message, (k - 1, planes - 1), hop)
            arrived.append((k, hop, message))
    arrived.sort(key=lambda entry: -entry[0])
    return [message for _, _, message in arrived] + [total]


def in_plane_order(parts):
    planes = lax.axis_size("expert")
    plane = lax.axis_index("expert")
    rows = parts[0].shape[0]
    result = jnp.zeros((planes * rows, parts[0].shape[1]), jnp.float32)
    places = [plane - hop * k for k in range(planes - 1, 0, -1) for hop in (1, -1)] + [plane]
    for place, part in zip(places, parts):
        result = lax.dynamic_update_slice_in_dim(
            result, part.astype(jnp.float32), jnp.clip(place, 0, planes - 1) * rows, axis=0
        )
    return result


def scatter_cols(product):
    col = lax.axis_index("col")
    cols = lax.axis_size("col")
    moved = [rotate(product((col + k) % cols).astype(jnp.bfloat16), "col", k) for k in range(1, cols)]
    total = product(col)
    for part in moved:
        total = total + part.astype(jnp.float32)
    return total.astype(jnp.bfloat16)


def scatter_rows(parts):
    row = lax.axis_index("row")
    rows = lax.axis_size("row")

    def piece(k):
        return lax.dynamic_index_in_dim(parts, (row + k) % rows, 0, keepdims=False)

    arrived = [rotate(piece(k), "row", k) for k in range(1, rows)]
    result = piece(0).astype(jnp.float32)
    for part in arrived:
        result = result + part.astype(jnp.float32)
    return result


def split_columns(refs, widths, low, high):
    base = 0
    for ref, width in zip(refs, widths):
        first, last = max(low, base), min(high, base + width)
        if first < last:
            yield ref, slice(first - base, last - base), slice(first - low, last - low)
        base += width


def expert_kernel(
    ids_ref,
    router_ref,
    gate_ref,
    up_ref,
    down_ref,
    *refs,
    count,
    grads_widths,
    weighted_widths,
    experts,
):
    rows_refs, refs = refs[:count], refs[count:]
    grads_refs, refs = refs[: len(grads_widths)], refs[len(grads_widths) :]
    sends, refs = refs[:count], refs[count:]
    weighted, refs = refs[: len(weighted_widths)], refs[len(weighted_widths) :]
    rows_out, grads_out, hidden_out, grad_gate_out, grad_up_out = refs
    width = rows_refs[0].shape[1]
    cuts = [slice(i * width, (i + 1) * width) for i in range(count)]
    rows = [ref[...] for ref in rows_refs]
    chosen = grads_refs[0][:, grads_widths[0] :].astype(jnp.float32) > 0.5
    lanes = lax.broadcasted_iota(jnp.int32, chosen.shape, 1)

    def times(weights_ref):
        return sum(
            jnp.dot(part, weights_ref[cut, :], preferred_element_type=jnp.float32)
            for part, cut in zip(rows, cuts)
        )

    logits = times(router_ref)
    top = jnp.max(jnp.where(chosen, logits, -3e38), axis=1, keepdims=True)
    raised = jnp.where(chosen, jnp.exp(jnp.where(chosen, logits - top, 0.0)), 0.0)
    own = jnp.sum(jnp.where(lanes == ids_ref[0], raised, 0.0), axis=1, keepdims=True)
    gates = own / jnp.maximum(jnp.sum(raised, axis=1, keepdims=True), 1e-30)
    gate_pre = times(gate_ref)
    up_pre = times(up_ref)
    sigmoid = 1.0 / (1.0 + jnp.exp(-gate_pre))
    silu = gate_pre * sigmoid
    hidden = (silu * up_pre).astype(jnp.bfloat16)
    hidden_out[...] = hidden
    dots = jnp.zeros(gates.shape, jnp.float32)
    grad_hidden = jnp.zeros(gate_pre.shape, jnp.float32)
    for i, cut in enumerate(cuts):
        out = jnp.dot(hidden, down_ref[:, cut], preferred_element_type=jnp.float32)
        out = out.astype(jnp.bfloat16).astype(jnp.float32)
        grads = jnp.concatenate(
            [
                ref[:, part].astype(jnp.float32)
                for ref, part, _ in split_columns(grads_refs, grads_widths, cut.start, cut.stop)
            ],
            axis=1,
        )
        dots = dots + jnp.sum(out * grads, axis=1, keepdims=True)
        gated = (out * gates).astype(jnp.bfloat16)
        for ref, part, own in split_columns(weighted, weighted_widths, cut.start, cut.stop):
            ref[:, part] = gated[:, own]
        grads_low = (grads * gates).astype(jnp.bfloat16)
        grads_out[:, cut] = grads_low
        rows_out[:, cut] = rows[i]
        grad_hidden = grad_hidden + lanes_dot(grads_low, down_ref[:, cut])
    grad_gate = (grad_hidden * up_pre * sigmoid * (1.0 + gate_pre * (1.0 - sigmoid))).astype(
        jnp.bfloat16
    )
    grad_up = (grad_hidden * silu).astype(jnp.bfloat16)
    grad_gate_out[...] = grad_gate
    grad_up_out[...] = grad_up
    for i, cut in enumerate(cuts):
        sends[i][:, :width] = (
            lanes_dot(grad_gate, gate_ref[cut, :]) + lanes_dot(grad_up, up_ref[cut, :])
        ).astype(jnp.bfloat16)
    dots_high = dots.astype(jnp.bfloat16).astype(jnp.float32)
    side = jnp.where(lanes == ids_ref[1], dots_high, 0.0) + jnp.where(
        lanes == ids_ref[1] + experts, dots - dots_high, 0.0
    )
    sends[0][:, width:] = side.astype(jnp.bfloat16)


def expert_rows(
    ids, w_router, w_gate, w_up, w_down, rows, grads, grads_widths, weighted_widths, plane_size
):
    count = len(rows)
    slots, width = rows[0].shape
    model_width, hidden = w_gate.shape
    side = grads[0].shape[1] - grads_widths[0]
    block = slots // expert_steps

    def tile(columns):
        return pl.BlockSpec((block, columns), lambda i: (i, 0))

    def whole(array):
        return pl.BlockSpec(array.shape, lambda i: (0, 0), pipeline_mode=pl.Buffered(1))

    def shape(columns):
        return pltpu.HBM((slots, columns), jnp.bfloat16)

    sides = [width + side] + [width] * (count - 1)
    outs = sides + list(weighted_widths) + [model_width, model_width, hidden, hidden, hidden]
    flops = 2 * slots * model_width * hidden * 6
    return pl.pallas_call(
        functools.partial(
            expert_kernel,
            count=count,
            grads_widths=tuple(grads_widths),
            weighted_widths=tuple(weighted_widths),
            experts=plane_size,
        ),
        grid=(expert_steps,),
        in_specs=[pl.BlockSpec(memory_space=pltpu.SMEM)]
        + [whole(array) for array in (w_router, w_gate, w_up, w_down)]
        + [tile(width)] * count
        + [tile(array.shape[1]) for array in grads],
        out_specs=[tile(columns) for columns in outs],
        out_shape=[shape(columns) for columns in outs],
        compiler_params=pltpu.CompilerParams(vmem_limit_bytes=expert_vmem),
        cost_estimate=pl.CostEstimate(
            flops=flops, bytes_accessed=6 * model_width * hidden, transcendentals=slots * hidden
        ),
        name="expert_rows",
    )(ids, w_router, w_gate, w_up, w_down, *rows, *grads)


def local(
    layer_input,
    norm_attn,
    w_query,
    w_key,
    w_value,
    q_gain,
    k_gain,
    w_out,
    norm_moe,
    w_router,
    w_gate,
    w_up,
    w_down,
    seq_lengths,
    routes,
    out_grad,
):
    tok_dev = layer_input.shape[0]
    model_width = layer_input.shape[1]
    group_tok = tok_dev * lax.axis_size(("row", "col"))
    head_dim = q_gain.shape[0]
    experts = w_router.shape[1]
    top_count = routes.shape[1]
    capacity = tok_dev * top_count * 17 // (16 * experts)
    planes = lax.axis_size("expert")
    plane_size = lax.axis_size(plane_axes)
    plane_index = lax.axis_index("expert")
    plane_cap = planes * capacity
    chosen_here = jnp.any(
        routes[:, :, None] == jnp.arange(experts, dtype=jnp.int32)[None, None, :], axis=1
    )
    plane_routes = gather_planes(routes.T)
    plane_experts = plane_index * plane_size + jnp.arange(plane_size, dtype=jnp.int32)
    chosen_plane = jnp.any(
        plane_routes[None] == plane_experts[:, None, None, None], axis=2
    )
    token_ids = jnp.arange(tok_dev, dtype=jnp.int32)
    earlier = (token_ids[:, None] < token_ids[None, :]).astype(jnp.bfloat16)
    slot_rank = jnp.dot(
        chosen_plane.astype(jnp.bfloat16).reshape(plane_size * planes, tok_dev),
        earlier,
        preferred_element_type=jnp.float32,
    ).astype(jnp.int32).reshape(plane_size, planes, tok_dev)
    plane_slot = jnp.where(
        chosen_plane,
        slot_rank + (jnp.arange(planes, dtype=jnp.int32) * capacity)[None, :, None],
        -1,
    ).reshape(plane_size, 1, planes * tok_dev)
    dispatch = (
        plane_slot == jnp.arange(plane_cap, dtype=jnp.int32)[None, :, None]
    ).astype(jnp.bfloat16)
    chosen_all = jnp.any(
        plane_routes[:, :, :, None] == jnp.arange(experts, dtype=jnp.int32), axis=1
    ).reshape(planes * tok_dev, experts).astype(jnp.bfloat16)

    def gather_rows(block):
        return gather_planes(block).reshape(planes * tok_dev, block.shape[1])

    def select_slots(rows_all):
        return jnp.dot(
            dispatch.reshape(plane_size * plane_cap, -1),
            rows_all,
            preferred_element_type=jnp.float32,
        ).astype(jnp.bfloat16)

    def to_plane(slot_values):
        width = slot_values.shape[1]
        moved = move_plane(slot_values.reshape(plane_size, plane_cap, width))
        return moved.reshape(plane_size * plane_cap, width)

    chunk_width = model_width // chunk_count
    chunks = [slice(i * chunk_width, (i + 1) * chunk_width) for i in range(chunk_count)]
    side_width = 128
    grads_widths = parts_of(model_width, grads_first)
    weighted_widths = parts_of(model_width, weighted_first)
    grad_planes = [gather_rows(part) for part in jnp.split(out_grad, [grads_widths[0]], axis=1)]
    grad_planes[0] = jnp.concatenate(
        [grad_planes[0], jnp.pad(chosen_all, ((0, 0), (0, side_width - experts)))], axis=1
    )
    slot_sends = [select_slots(part) for part in grad_planes]
    def gates_of(all_logits, chosen):
        top = jnp.max(jnp.where(chosen, all_logits, -3e38), axis=1, keepdims=True)
        raised = jnp.where(chosen, jnp.exp(jnp.where(chosen, all_logits - top, 0.0)), 0.0)
        return raised / jnp.maximum(jnp.sum(raised, axis=1, keepdims=True), 1e-30)

    input_rows = layer_input.astype(jnp.float32)
    normed_one, norm_one_back = jax.vjp(rms_scale, input_rows, norm_attn)
    normed_low = normed_one.astype(jnp.bfloat16)
    group_rows = lax.all_gather(normed_low, ("row", "col"), axis=0, tiled=True)
    ends = jnp.cumsum(seq_lengths[0], dtype=jnp.int32)
    cosine_table, sine_table = rope_tables(slot_positions(ends, group_tok), head_dim)
    key_value_w = jnp.concatenate([w_key, w_value], axis=1)
    cosine_table, sine_table, key_value_w, slot_sends[0] = together(
        cosine_table, sine_table, key_value_w, slot_sends[0]
    )
    grad_slot_chunks = [to_plane(slot_sends[0])]
    col = lax.axis_index("col")
    kept, sent, query_low, key_low, value_low, heads_low, log_totals, head_scales = attend_rows(
        ends, col.astype(jnp.int32)[None], group_rows, w_query, key_value_w, w_out, q_gain, k_gain, cosine_table, sine_table,
        2 * tok_dev,
    )
    sent, kept, grad_slot_chunks[0] = together(sent, kept, grad_slot_chunks[0])
    col_sums = kept.astype(jnp.float32) + rotate(sent, "col", 1).astype(jnp.float32)
    attn_rows = scatter_rows(col_sums.astype(jnp.bfloat16).reshape(-1, tok_dev, model_width))
    attn_rows, *late_sends = together(attn_rows, *slot_sends[1:])
    grad_slot_chunks += [to_plane(part) for part in late_sends]
    attn_rows = attn_rows.astype(jnp.float32)
    mixed_rows = input_rows + attn_rows
    normed_two, norm_two_back = jax.vjp(rms_scale, mixed_rows, norm_moe)
    moe_input = normed_two.astype(jnp.bfloat16)
    router_logits = jnp.dot(moe_input, w_router, preferred_element_type=jnp.float32)
    source_gates = gates_of(router_logits, chosen_here)

    moe_planes = [gather_rows(moe_input[:, cut]) for cut in chunks]
    moe_sends = [select_slots(part) for part in moe_planes]
    moe_sends[0], *grad_slot_chunks[1:] = together(moe_sends[0], *grad_slot_chunks[1:])
    slot_chunks = [to_plane(part) for part in moe_sends]
    place = lax.axis_index(plane_axes)
    ids = jnp.stack([plane_index * plane_size + place, place]).astype(jnp.int32)
    expert_outs = expert_rows(
        ids,
        jnp.pad(w_router, ((0, 0), (0, side_width - experts))),
        w_gate[0],
        w_up[0],
        w_down[0],
        slot_chunks,
        grad_slot_chunks,
        grads_widths,
        weighted_widths,
        plane_size,
    )
    grad_sends = expert_outs[:chunk_count]
    out_sends = expert_outs[chunk_count : chunk_count + len(weighted_widths)]
    moe_slots, grad_out_slots, hidden_low, grad_gate_pre, grad_up_pre = expert_outs[
        chunk_count + len(weighted_widths) :
    ]

    def to_source(returned):
        summed = lax.dot_general(
            dispatch.reshape(plane_size * plane_cap, -1),
            returned,
            (((0,), (0,)), ((), ())),
            preferred_element_type=jnp.float32,
        ).astype(jnp.bfloat16)
        return return_planes(summed.reshape(planes, tok_dev, returned.shape[1]))

    def add_parts(parts):
        return sum(part.astype(jnp.float32) for part in parts)

    grad_rows = out_grad.astype(jnp.float32)
    grad_down = transposed_times(hidden_low, grad_out_slots)
    grad_gate = transposed_times(moe_slots, grad_gate_pre)
    grad_up = transposed_times(moe_slots, grad_up_pre)
    grad_returns = [to_plane(part) for part in grad_sends]
    grad_returns[0], grad_down = together(grad_returns[0], grad_down)
    grad_returns[-1], grad_gate, *out_sends = together(grad_returns[-1], grad_gate, *out_sends)
    out_returns = [to_plane(out_sends[0])]
    grad_parts = [to_source(part) for part in grad_returns]
    grad_parts[-1][-1], grad_up = together(grad_parts[-1][-1], grad_up)
    side_parts = jnp.stack(
        [part[:, chunk_width:].astype(jnp.float32) for part in grad_parts[0]], axis=0
    )
    dot_parts = side_parts[:, :, :plane_size] + side_parts[:, :, plane_size : 2 * plane_size]
    dot_parts = lax.dynamic_slice_in_dim(
        jnp.concatenate([dot_parts, dot_parts], axis=0), planes - plane_index, planes, axis=0
    )
    grad_gates = jnp.swapaxes(dot_parts, 0, 1).reshape(tok_dev, experts)
    grad_logits = source_gates * (
        grad_gates - jnp.sum(source_gates * grad_gates, axis=1, keepdims=True)
    )
    grad_parts[0] = [part[:, :chunk_width] for part in grad_parts[0]]
    grad_moe_input = jnp.concatenate([add_parts(parts) for parts in grad_parts], axis=1)
    grad_router = lax.dot_general(
        grad_logits,
        moe_input.astype(jnp.float32),
        (((0,), (0,)), ((), ())),
        precision=highest,
        preferred_element_type=jnp.float32,
    )
    grad_moe_input = grad_moe_input + jnp.einsum(
        "te,de->td", grad_logits, w_router, precision=highest, preferred_element_type=jnp.float32
    )
    grad_mixed_norm, grad_norm_moe = norm_two_back(grad_moe_input)
    grad_mixed = grad_rows + grad_mixed_norm
    grad_attn_low = grad_mixed.astype(jnp.bfloat16)
    grad_attn_low, out_returns[0] = together(grad_attn_low, out_returns[0])
    grad_group = lax.all_gather(grad_attn_low, ("row", "col"), axis=0, tiled=True)
    out_first = add_parts(to_source(out_returns[0]))
    grad_group, out_first, *out_late = together(grad_group, out_first, *out_sends[1:])
    out_returns += [to_plane(part) for part in out_late]
    grad_out_proj = transposed_times(heads_low, grad_group).astype(jnp.bfloat16)
    grad_out_proj, grad_group = together(grad_out_proj, grad_group)
    out_terms = send_planes(grad_out_proj)
    grad_query_low, grad_kv, grad_q_gain, grad_k_gain = attend_rows_back(
        ends,
        grad_group,
        w_out,
        query_low,
        heads_low,
        key_low,
        value_low,
        log_totals,
        head_scales,
        q_gain,
        k_gain,
        cosine_table,
        sine_table,
        2 * tok_dev,
    )
    grad_query_low, grad_kv, out_terms[1], out_terms[-1] = together(
        grad_query_low, grad_kv, out_terms[1], out_terms[-1]
    )
    grad_query = transposed_times(group_rows, grad_query_low)
    grad_key_value = transposed_times(group_rows, grad_kv)
    norm_terms = (
        jnp.sum(grad_query * w_query.astype(jnp.float32), axis=1)
        + jnp.sum(grad_key_value * key_value_w.astype(jnp.float32), axis=1)
    ) / norm_attn
    cols = lax.axis_size("col")
    col = lax.axis_index("col")
    kv_low = grad_key_value.astype(jnp.bfloat16).reshape(cols, -1, 2 * head_dim)
    kv_part = lax.dynamic_index_in_dim(kv_low, col, 0, keepdims=False).astype(jnp.float32)
    for k in range(1, cols):
        kv_part = kv_part + rotate(
            lax.dynamic_index_in_dim(kv_low, (col + k) % cols, 0, keepdims=False), "col", k
        ).astype(jnp.float32)
    lane_parts = grad_query.shape[1] // (2 * head_dim)
    query_kv = jnp.concatenate(
        [
            grad_query.astype(jnp.bfloat16),
            *[
                jnp.concatenate(jnp.split(kv_part.astype(jnp.bfloat16), lane_parts), axis=1)
            ],
        ],
        axis=0,
    )
    query_kv = lax.psum(query_kv, "expert")
    left_parts = jnp.concatenate([grad_query_low, grad_kv], axis=1).reshape(
        -1, cols, tok_dev, grad_query_low.shape[1] + 2 * head_dim
    )
    right_all = jnp.concatenate([w_query, key_value_w], axis=1)

    def grad_normed_rows(place):
        left = lax.dynamic_index_in_dim(left_parts, place, 1, keepdims=False)
        return lax.dot_general(
            left, right_all, (((2,), (1,)), ((), ())), preferred_element_type=jnp.float32
        )

    out_share = add_parts(out_terms).astype(jnp.bfloat16)
    summed_values = jnp.concatenate(
        [grad_router.reshape(-1), grad_norm_moe, norm_terms, grad_q_gain[0], grad_k_gain[0]]
    )
    left_parts, out_share, summed_values = together(left_parts, out_share, summed_values)
    sums = sum_all(summed_values)
    out_shares = spread_planes(out_share)
    col_sums = scatter_cols(grad_normed_rows)
    col_sums, *out_returns[1:] = together(col_sums, *out_returns[1:])
    out_parts = [out_first] + [add_parts(to_source(part)) for part in out_returns[1:]]
    grad_normed = scatter_rows(col_sums)
    grad_input_norm = norm_one_back(grad_normed)[0]
    grad_x = (grad_mixed + grad_input_norm).astype(jnp.bfloat16)
    out_rows = (mixed_rows + jnp.concatenate(out_parts, axis=1)).astype(jnp.bfloat16)
    grad_out_proj = in_plane_order(out_shares)
    places = (0, experts * model_width, model_width, model_width, head_dim, head_dim)
    ends_at = [sum(places[: k + 1]) for k in range(len(places))]
    grad_router, grad_norm_moe, grad_norm_attn, grad_q_gain, grad_k_gain = [
        sums[low:high] for low, high in zip(ends_at[:-1], ends_at[1:])
    ]
    grad_router = grad_router.reshape(experts, model_width).T
    grad_x, out_rows, grad_router, query_kv = together(grad_x, out_rows, grad_router, query_kv)
    grad_query = query_kv[:model_width].astype(jnp.float32)
    kv_part = query_kv[model_width:]
    kv_parts = [kv_part] + [rotate(kv_part, "col", k) for k in range(1, cols)]
    kv_blocks = []
    for place in range(cols):
        block = kv_parts[0]
        for k in range(1, cols):
            block = jnp.where((col - k) % cols == place, kv_parts[k], block)
        kv_blocks += jnp.split(block.astype(jnp.float32), lane_parts, axis=1)
    grad_key = jnp.concatenate([block[:, :head_dim] for block in kv_blocks], axis=0)
    grad_value = jnp.concatenate([block[:, head_dim:] for block in kv_blocks], axis=0)
    return (
        out_rows,
        grad_x,
        grad_norm_attn,
        grad_query,
        grad_key,
        grad_value,
        grad_q_gain,
        grad_k_gain,
        grad_out_proj,
        grad_norm_moe,
        grad_router,
        grad_gate[None],
        grad_up[None],
        grad_down[None],
    )


def solution(mesh):
    placed = (
        P(("expert", "row", "col"), None),
        P(),
        P(None, ("row", "col")),
        P(None, "row"),
        P(None, "row"),
        P(),
        P(),
        P(("row", "col"), None),
        P(),
        P(),
        P(("expert", "row", "col"), None, None),
        P(("expert", "row", "col"), None, None),
        P(("expert", "row", "col"), None, None),
        P("expert", None),
        P(("expert", "row", "col"), None),
        P(("expert", "row", "col"), None),
    )
    return jax.shard_map(
        local,
        mesh=mesh,
        in_specs=placed,
        out_specs=(
            P(("expert", "row", "col"), None),
            P(("expert", "row", "col"), None),
            P(),
            P(None, ("row", "col")),
            P(None, "row"),
            P(None, "row"),
            P(),
            P(),
            P(("row", "col"), None),
            P(),
            P(),
            P(("expert", "row", "col"), None, None),
            P(("expert", "row", "col"), None, None),
            P(("expert", "row", "col"), None, None),
        ),
        check_vma=False,
    )
```

```python
import functools

import jax
import jax.numpy as jnp
from jax import lax
from jax.experimental import pallas as pl
from jax.experimental.pallas import tpu as pltpu
from jax.sharding import PartitionSpec as P

eps_norm = 1e-06
rope_base = 1000000.0
highest = lax.Precision.HIGHEST
chunk_count = 2
grads_first = 7
weighted_first = 13
expert_steps = 2
expert_vmem = 56 * 1024 * 1024
kernel_vmem = 40 * 1024 * 1024


def rms_scale(values, norm_gain):
    return (
        values * lax.rsqrt(jnp.mean(values * values, axis=-1, keepdims=True) + eps_norm) * norm_gain
    )


def rope_tables(positions, head_dim):
    half_dim = head_dim // 2
    inverse = rope_base ** (-(jnp.arange(half_dim, dtype=jnp.float32) * 2.0 / head_dim))
    angles = positions.astype(jnp.float32)[:, None] * inverse[None, :]
    cosine = jnp.cos(angles)
    sine = jnp.sin(angles)
    return (jnp.concatenate([cosine, cosine], axis=1), jnp.concatenate([-sine, sine], axis=1))


def slot_positions(ends, slot_count):
    slot_ids = jnp.arange(slot_count, dtype=jnp.int32)
    starts = row_starts(slot_ids, [ends[k] for k in range(ends.shape[0])])
    return slot_ids - starts


def row_starts(row_ids, ends):
    starts = jnp.zeros_like(row_ids)
    for end in ends:
        starts = jnp.where(row_ids >= end, end, starts)
    return jnp.where(row_ids >= ends[-1], row_ids, starts)


def lanes_dot(left, right):
    return lax.dot_general(
        left, right, (((1,), (1,)), ((), ())), preferred_element_type=jnp.float32
    )


def turn_halves(values):
    return pltpu.roll(values, values.shape[-1] // 2, axis=1)


def keep(array):
    return pltpu.with_memory_space_constraint(array, pltpu.HBM)


def attend_kernel(
    ends_ref,
    place_ref,
    rows_ref,
    query_w_ref,
    kv_w_ref,
    out_w_ref,
    query_gain_ref,
    key_gain_ref,
    cosine_ref,
    sine_ref,
    kept_ref,
    sent_ref,
    query_ref,
    key_ref,
    value_ref,
    heads_ref,
    log_ref,
    scale_ref,
    keys,
    values,
    total,
    sums,
    partial,
    *,
    head_dim,
):
    step = pl.program_id(0)
    block = rows_ref.shape[0]
    heads = query_w_ref.shape[1] // head_dim
    ends = [ends_ref[k] for k in range(ends_ref.shape[0])]
    softmax_scale = head_dim ** (-0.5)
    rows = rows_ref[...]
    query_pre = jnp.dot(rows, query_w_ref[...], preferred_element_type=jnp.float32)
    kv_pre = jnp.dot(rows, kv_w_ref[...], preferred_element_type=jnp.float32)
    cosine = cosine_ref[...]
    sine = sine_ref[...]
    lanes = lax.broadcasted_iota(jnp.int32, (block, head_dim), 1)
    scales = jnp.zeros((block, head_dim), jnp.float32)

    def prep(vectors, gain):
        scale = lax.rsqrt(jnp.mean(vectors * vectors, axis=-1, keepdims=True) + eps_norm)
        gained = vectors * scale * gain
        return (gained * cosine + turn_halves(gained) * sine).astype(jnp.bfloat16), scale

    stacked = []
    for h in range(heads):
        cut = slice(h * head_dim, (h + 1) * head_dim)
        low, scale = prep(query_pre[:, cut], query_gain_ref[...])
        query_ref[:, cut] = low
        stacked.append(low)
        scales = jnp.where(lanes == h, scale, scales)
    key_low, scale = prep(kv_pre[:, :head_dim], key_gain_ref[...])
    scale_ref[...] = jnp.where(lanes == heads, scale, scales)
    value_low = kv_pre[:, head_dim:].astype(jnp.bfloat16)
    key_ref[...] = key_low
    value_ref[...] = value_low
    own = pl.ds(pl.multiple_of(step * block, block), block)
    keys[own, :] = key_low
    values[own, :head_dim] = value_low
    values[own, head_dim:] = jnp.ones((block, head_dim), jnp.bfloat16)
    queries = jnp.concatenate(stacked, axis=0)
    row_ids = step * block + lax.broadcasted_iota(jnp.int32, (block, 1), 0)
    starts = row_starts(row_ids, ends)
    total[...] = jnp.zeros_like(total)
    sums[...] = jnp.zeros_like(sums)
    ones = jnp.ones((8, block), jnp.bfloat16)

    def one_block(j, carry):
        there = pl.ds(pl.multiple_of(j * block, block), block)
        scores = lanes_dot(queries, keys[there, :]) * softmax_scale
        column_ids = j * block + lax.broadcasted_iota(jnp.int32, (block, block), 1)
        allowed = (column_ids <= row_ids) & (column_ids >= starts)
        weights = jnp.concatenate(
            [
                jnp.where(allowed, jnp.exp(scores[h * block : (h + 1) * block]), 0.0).astype(
                    jnp.bfloat16
                )
                for h in range(heads)
            ],
            axis=0,
        )
        total[...] += jnp.dot(weights, values[there, :], preferred_element_type=jnp.float32)
        sums[...] += lanes_dot(ones, weights)
        return carry

    first = row_starts(step * block, ends) // block
    lax.fori_loop(first, step + 1, one_block, 0)
    log_ref[0] = jnp.log(sums[...])
    outs = (total[:, :head_dim] / total[:, head_dim:]).astype(jnp.bfloat16)
    for h in range(heads):
        heads_ref[:, h * head_dim : (h + 1) * head_dim] = outs[h * block : (h + 1) * block]
    partial[...] = jnp.dot(
        heads_ref[...], out_w_ref[...], preferred_element_type=jnp.float32
    ).astype(jnp.bfloat16)
    share = kept_ref.shape[0]
    kept = pl.multiple_of(place_ref[0] * share, share)
    sent = pl.multiple_of((1 - place_ref[0]) * share, share)
    kept_ref[...] = partial[pl.ds(kept, share), :]
    sent_ref[...] = partial[pl.ds(sent, share), :]


def attend_rows(ends, place, rows, w_query, w_kv, w_out, q_gain, k_gain, cosine, sine, block):
    slots, width = rows.shape
    head_dim = q_gain.shape[0]
    head_width = w_query.shape[1]
    heads = head_width // head_dim
    count = slots // block

    def tile(columns):
        return pl.BlockSpec((block, columns), lambda i: (i, 0))

    def whole(array):
        return pl.BlockSpec(array.shape, lambda i: (0, 0))

    def half(columns):
        return pl.BlockSpec((block // 2, columns), lambda i: (i, 0))

    shape = pltpu.HBM
    q_gain = q_gain[None]
    k_gain = k_gain[None]
    return pl.pallas_call(
        functools.partial(attend_kernel, head_dim=head_dim),
        grid=(count,),
        in_specs=[
            pl.BlockSpec(memory_space=pltpu.SMEM),
            pl.BlockSpec(memory_space=pltpu.SMEM),
            tile(width),
            whole(w_query),
            whole(w_kv),
            whole(w_out),
            whole(q_gain),
            whole(k_gain),
            tile(head_dim),
            tile(head_dim),
        ],
        out_specs=[
            half(width),
            half(width),
            tile(head_width),
            tile(head_dim),
            tile(head_dim),
            tile(head_width),
            pl.BlockSpec((1, 8, heads * block), lambda i: (i, 0, 0)),
            tile(head_dim),
        ],
        out_shape=[
            shape((slots // 2, width), jnp.bfloat16),
            shape((slots // 2, width), jnp.bfloat16),
            shape((slots, head_width), jnp.bfloat16),
            shape((slots, head_dim), jnp.bfloat16),
            shape((slots, head_dim), jnp.bfloat16),
            shape((slots, head_width), jnp.bfloat16),
            shape((count, 8, heads * block), jnp.float32),
            shape((slots, head_dim), jnp.float32),
        ],
        scratch_shapes=[
            pltpu.VMEM((slots, head_dim), jnp.bfloat16),
            pltpu.VMEM((slots, 2 * head_dim), jnp.bfloat16),
            pltpu.VMEM((heads * block, 2 * head_dim), jnp.float32),
            pltpu.VMEM((8, heads * block), jnp.float32),
            pltpu.VMEM((block, width), jnp.bfloat16),
        ],
        compiler_params=pltpu.CompilerParams(vmem_limit_bytes=kernel_vmem),
        cost_estimate=pl.CostEstimate(
            flops=2 * slots * width * (2 * head_width + 2 * head_dim)
            + 3 * slots * slots * head_width,
            bytes_accessed=4 * slots * width + 4 * width * head_width,
            transcendentals=slots * slots * heads // 2,
        ),
        name="attend_rows",
    )(
        ends,
        place,
        keep(rows),
        keep(w_query),
        keep(w_kv),
        keep(w_out),
        q_gain,
        k_gain,
        keep(cosine),
        keep(sine),
    )


def attend_back_kernel(
    ends_ref,
    grad_ref,
    out_w_ref,
    query_ref,
    heads_ref,
    key_ref,
    value_ref,
    log_ref,
    scale_ref,
    query_gain_ref,
    key_gain_ref,
    cosine_ref,
    sine_ref,
    grad_query_ref,
    grad_kv_ref,
    grad_query_gain_ref,
    grad_key_gain_ref,
    grad_keys,
    grad_values,
    grad_queries,
    *,
    head_dim,
):
    step = pl.program_id(0)
    block = query_ref.shape[0]
    heads = query_ref.shape[1] // head_dim
    ends = [ends_ref[k] for k in range(ends_ref.shape[0])]
    softmax_scale = head_dim ** (-0.5)

    @pl.when(step == 0)
    def _():
        grad_keys[...] = jnp.zeros_like(grad_keys)
        grad_values[...] = jnp.zeros_like(grad_values)
        grad_query_gain_ref[...] = jnp.zeros_like(grad_query_gain_ref)

    grad_heads = lanes_dot(grad_ref[...], out_w_ref[...]).astype(jnp.bfloat16)
    query = query_ref[...]
    out = heads_ref[...]
    cuts = [slice(h * head_dim, (h + 1) * head_dim) for h in range(heads)]
    queries = jnp.concatenate([query[:, cut] for cut in cuts], axis=0)
    grads = jnp.concatenate([grad_heads[:, cut] for cut in cuts], axis=0)
    outs = jnp.concatenate([out[:, cut] for cut in cuts], axis=0)
    products = grads.astype(jnp.float32) * outs.astype(jnp.float32)
    high = products.astype(jnp.bfloat16)
    rest = (products - high.astype(jnp.float32)).astype(jnp.bfloat16)
    ones = jnp.ones((8, head_dim), jnp.bfloat16)
    centre = (lanes_dot(ones, high) + lanes_dot(ones, rest))[:1]
    logs = log_ref[0, :1, :]
    column_ids = step * block + lax.broadcasted_iota(jnp.int32, (1, block), 1)
    starts = row_starts(column_ids, ends)
    grad_queries[...] = jnp.zeros_like(grad_queries)

    def one_block(j, carry):
        there = pl.ds(pl.multiple_of(j * block, block), block)
        key = key_ref[there, :]
        value = value_ref[there, :]
        scores = lanes_dot(key, queries) * softmax_scale - logs
        grad_probs = lanes_dot(value, grads) - centre
        row_ids = j * block + lax.broadcasted_iota(jnp.int32, (block, block), 0)
        allowed = (row_ids <= column_ids) & (row_ids >= starts)
        probs = jnp.concatenate(
            [
                jnp.where(allowed, jnp.exp(scores[:, h * block : (h + 1) * block]), 0.0)
                for h in range(heads)
            ],
            axis=1,
        )
        probs_low = probs.astype(jnp.bfloat16)
        grad_scores = (probs * grad_probs).astype(jnp.bfloat16)
        grad_values[there, :] += jnp.dot(probs_low, grads, preferred_element_type=jnp.float32)
        grad_keys[there, :] += jnp.dot(grad_scores, queries, preferred_element_type=jnp.float32)
        grad_queries[...] += lax.dot_general(
            grad_scores, key, (((0,), (0,)), ((), ())), preferred_element_type=jnp.float32
        )
        return carry

    first = row_starts(step * block, ends) // block
    lax.fori_loop(first, step + 1, one_block, 0)

    def prep_back(grad, low, gain, cosine, sine, scale):
        grad = grad * softmax_scale
        low = low.astype(jnp.float32)
        grad_gained = grad * cosine - turn_halves(grad) * sine
        normed = (low * cosine - turn_halves(low) * sine) / gain
        grad_gain = jnp.sum(grad_gained * normed, axis=0, keepdims=True)
        grad_normed = grad_gained * gain
        mean = jnp.mean(grad_normed * normed, axis=-1, keepdims=True)
        return scale * (grad_normed - normed * mean), grad_gain

    own = pl.ds(pl.multiple_of(step * block, block), block)
    cosine = cosine_ref[own, :]
    sine = sine_ref[own, :]
    scales = scale_ref[own, :]
    for h, cut in enumerate(cuts):
        grad_pre, grad_gain = prep_back(
            grad_queries[h * block : (h + 1) * block, :],
            query[:, cut],
            query_gain_ref[...],
            cosine,
            sine,
            scales[:, h : h + 1],
        )
        grad_query_ref[:, cut] = grad_pre.astype(jnp.bfloat16)
        grad_query_gain_ref[...] += grad_gain

    @pl.when(step == pl.num_programs(0) - 1)
    def _():
        grad_pre, grad_gain = prep_back(
            grad_keys[...],
            key_ref[...],
            key_gain_ref[...],
            cosine_ref[...],
            sine_ref[...],
            scale_ref[:, heads : heads + 1],
        )
        grad_kv_ref[:, :head_dim] = grad_pre.astype(jnp.bfloat16)
        grad_kv_ref[:, head_dim:] = grad_values[...].astype(jnp.bfloat16)
        grad_key_gain_ref[...] = grad_gain


def attend_rows_back(
    ends, grad, w_out, query, heads_low, key, value, logs, scales, q_gain, k_gain, cosine, sine, block
):
    slots, width = grad.shape
    head_dim = q_gain.shape[0]
    head_width = query.shape[1]
    heads = head_width // head_dim
    count = slots // block

    def tile(columns):
        return pl.BlockSpec((block, columns), lambda i: (i, 0))

    def whole(array):
        return pl.BlockSpec(array.shape, lambda i: (0, 0))

    shape = pltpu.HBM
    q_gain = q_gain[None]
    k_gain = k_gain[None]
    return pl.pallas_call(
        functools.partial(attend_back_kernel, head_dim=head_dim),
        grid=(count,),
        in_specs=[
            pl.BlockSpec(memory_space=pltpu.SMEM),
            tile(width),
            whole(w_out),
            tile(head_width),
            tile(head_width),
            whole(key),
            whole(value),
            pl.BlockSpec((1, 8, heads * block), lambda i: (i, 0, 0)),
            whole(scales),
            whole(q_gain),
            whole(k_gain),
            whole(cosine),
            whole(sine),
        ],
        out_specs=[
            tile(head_width),
            pl.BlockSpec((slots, 2 * head_dim), lambda i: (0, 0)),
            pl.BlockSpec((1, head_dim), lambda i: (0, 0)),
            pl.BlockSpec((1, head_dim), lambda i: (0, 0)),
        ],
        out_shape=[
            shape((slots, head_width), jnp.bfloat16),
            shape((slots, 2 * head_dim), jnp.bfloat16),
            shape((1, head_dim), jnp.float32),
            shape((1, head_dim), jnp.float32),
        ],
        scratch_shapes=[
            pltpu.VMEM((slots, head_dim), jnp.float32),
            pltpu.VMEM((slots, head_dim), jnp.float32),
            pltpu.VMEM((heads * block, head_dim), jnp.float32),
        ],
        compiler_params=pltpu.CompilerParams(vmem_limit_bytes=kernel_vmem),
        cost_estimate=pl.CostEstimate(
            flops=2 * slots * width * head_width + 6 * slots * slots * head_width,
            bytes_accessed=2 * slots * width + 2 * width * head_width,
            transcendentals=slots * slots * heads // 2,
        ),
        name="attend_rows_back",
    )(
        ends,
        keep(grad),
        keep(w_out),
        keep(query),
        keep(heads_low),
        keep(key),
        keep(value),
        keep(logs),
        keep(scales),
        q_gain,
        k_gain,
        keep(cosine),
        keep(sine),
    )


def transposed_times(left, right):
    return lax.dot_general(
        left, right, (((0,), (0,)), ((), ())), preferred_element_type=jnp.float32
    )


plane_axes = ("row", "col")


def move_plane(parts):
    return lax.all_to_all(parts, plane_axes, split_axis=0, concat_axis=0, tiled=True)


def rotate(block, axis, step):
    size = lax.axis_size(axis)
    return lax.ppermute(block, axis, [(i, (i + step) % size) for i in range(size)])


def gather_planes(block):
    planes = lax.axis_size("expert")
    return jnp.stack([block] + [rotate(block, "expert", k) for k in range(1, planes)], axis=0)


def return_planes(parts):
    return [parts[0]] + [rotate(parts[k], "expert", -k) for k in range(1, parts.shape[0])]


def parts_of(width, sixteenths):
    return [width * sixteenths // 16, width - width * sixteenths // 16]


def together(*values):
    return lax.optimization_barrier(values)


def move_all(parts):
    return lax.all_to_all(
        parts, ("expert",) + plane_axes, split_axis=0, concat_axis=0, tiled=True
    )


def sum_all(values):
    devices = lax.axis_size(("expert",) + plane_axes)
    padded = jnp.pad(values, (0, -values.shape[0] % (devices * 128)))
    total = jnp.sum(move_all(padded.reshape(devices, -1, 128)), axis=0)
    return move_all(jnp.broadcast_to(total[None], (devices,) + total.shape)).reshape(-1)


def line_step(value, step, hop):
    planes = lax.axis_size("expert")
    if hop > 0:
        pairs = [(i, i + 1) for i in range(*step)]
    else:
        pairs = [(planes - 1 - i, planes - 2 - i) for i in range(*step)]
    return lax.ppermute(value, "expert", pairs)


def send_planes(product):
    planes = lax.axis_size("expert")
    plane = lax.axis_index("expert")
    shares = product.reshape(planes, -1, product.shape[1])

    def share(k):
        return lax.dynamic_index_in_dim(shares, (plane + k) % planes, 0, keepdims=False)

    return [share(0)] + [rotate(share(k), "expert", k) for k in range(1, planes)]


def spread_planes(total):
    planes = lax.axis_size("expert")
    arrived = []
    for hop in (1, -1):
        message = total
        for k in range(1, planes):
            message = line_step(message, (k - 1, planes - 1), hop)
            arrived.append((k, hop, message))
    arrived.sort(key=lambda entry: -entry[0])
    return [message for _, _, message in arrived] + [total]


def in_plane_order(parts):
    planes = lax.axis_size("expert")
    plane = lax.axis_index("expert")
    rows = parts[0].shape[0]
    result = jnp.zeros((planes * rows, parts[0].shape[1]), jnp.float32)
    places = [plane - hop * k for k in range(planes - 1, 0, -1) for hop in (1, -1)] + [plane]
    for place, part in zip(places, parts):
        result = lax.dynamic_update_slice_in_dim(
            result, part.astype(jnp.float32), jnp.clip(place, 0, planes - 1) * rows, axis=0
        )
    return result


def scatter_cols(product):
    col = lax.axis_index("col")
    cols = lax.axis_size("col")
    moved = [rotate(product((col + k) % cols).astype(jnp.bfloat16), "col", k) for k in range(1, cols)]
    total = product(col)
    for part in moved:
        total = total + part.astype(jnp.float32)
    return total.astype(jnp.bfloat16)


def scatter_rows(parts):
    row = lax.axis_index("row")
    rows = lax.axis_size("row")

    def piece(k):
        return lax.dynamic_index_in_dim(parts, (row + k) % rows, 0, keepdims=False)

    arrived = [rotate(piece(k), "row", k) for k in range(1, rows)]
    result = piece(0).astype(jnp.float32)
    for part in arrived:
        result = result + part.astype(jnp.float32)
    return result


def split_columns(refs, widths, low, high):
    base = 0
    for ref, width in zip(refs, widths):
        first, last = max(low, base), min(high, base + width)
        if first < last:
            yield ref, slice(first - base, last - base), slice(first - low, last - low)
        base += width


def expert_kernel(
    ids_ref,
    router_ref,
    gate_ref,
    up_ref,
    down_ref,
    *refs,
    count,
    grads_widths,
    weighted_widths,
    experts,
):
    rows_refs, refs = refs[:count], refs[count:]
    grads_refs, refs = refs[: len(grads_widths)], refs[len(grads_widths) :]
    sends, refs = refs[:count], refs[count:]
    weighted, refs = refs[: len(weighted_widths)], refs[len(weighted_widths) :]
    rows_out, grads_out, hidden_out, grad_gate_out, grad_up_out = refs
    width = rows_refs[0].shape[1]
    cuts = [slice(i * width, (i + 1) * width) for i in range(count)]
    rows = [ref[...] for ref in rows_refs]
    chosen = grads_refs[0][:, grads_widths[0] :].astype(jnp.float32) > 0.5
    lanes = lax.broadcasted_iota(jnp.int32, chosen.shape, 1)

    def times(weights_ref):
        return sum(
            jnp.dot(part, weights_ref[cut, :], preferred_element_type=jnp.float32)
            for part, cut in zip(rows, cuts)
        )

    logits = times(router_ref)
    top = jnp.max(jnp.where(chosen, logits, -3e38), axis=1, keepdims=True)
    raised = jnp.where(chosen, jnp.exp(jnp.where(chosen, logits - top, 0.0)), 0.0)
    own = jnp.sum(jnp.where(lanes == ids_ref[0], raised, 0.0), axis=1, keepdims=True)
    gates = own / jnp.maximum(jnp.sum(raised, axis=1, keepdims=True), 1e-30)
    gate_pre = times(gate_ref)
    up_pre = times(up_ref)
    sigmoid = 1.0 / (1.0 + jnp.exp(-gate_pre))
    silu = gate_pre * sigmoid
    hidden = (silu * up_pre).astype(jnp.bfloat16)
    hidden_out[...] = hidden
    dots = jnp.zeros(gates.shape, jnp.float32)
    grad_hidden = jnp.zeros(gate_pre.shape, jnp.float32)
    for i, cut in enumerate(cuts):
        out = jnp.dot(hidden, down_ref[:, cut], preferred_element_type=jnp.float32)
        out = out.astype(jnp.bfloat16).astype(jnp.float32)
        grads = jnp.concatenate(
            [
                ref[:, part].astype(jnp.float32)
                for ref, part, _ in split_columns(grads_refs, grads_widths, cut.start, cut.stop)
            ],
            axis=1,
        )
        dots = dots + jnp.sum(out * grads, axis=1, keepdims=True)
        gated = (out * gates).astype(jnp.bfloat16)
        for ref, part, own in split_columns(weighted, weighted_widths, cut.start, cut.stop):
            ref[:, part] = gated[:, own]
        grads_low = (grads * gates).astype(jnp.bfloat16)
        grads_out[:, cut] = grads_low
        rows_out[:, cut] = rows[i]
        grad_hidden = grad_hidden + lanes_dot(grads_low, down_ref[:, cut])
    grad_gate = (grad_hidden * up_pre * sigmoid * (1.0 + gate_pre * (1.0 - sigmoid))).astype(
        jnp.bfloat16
    )
    grad_up = (grad_hidden * silu).astype(jnp.bfloat16)
    grad_gate_out[...] = grad_gate
    grad_up_out[...] = grad_up
    for i, cut in enumerate(cuts):
        sends[i][:, :width] = (
            lanes_dot(grad_gate, gate_ref[cut, :]) + lanes_dot(grad_up, up_ref[cut, :])
        ).astype(jnp.bfloat16)
    dots_high = dots.astype(jnp.bfloat16).astype(jnp.float32)
    side = jnp.where(lanes == ids_ref[1], dots_high, 0.0) + jnp.where(
        lanes == ids_ref[1] + experts, dots - dots_high, 0.0
    )
    sends[0][:, width:] = side.astype(jnp.bfloat16)


def expert_rows(
    ids, w_router, w_gate, w_up, w_down, rows, grads, grads_widths, weighted_widths, plane_size
):
    count = len(rows)
    slots, width = rows[0].shape
    model_width, hidden = w_gate.shape
    side = grads[0].shape[1] - grads_widths[0]
    block = slots // expert_steps

    def tile(columns):
        return pl.BlockSpec((block, columns), lambda i: (i, 0))

    def whole(array):
        return pl.BlockSpec(array.shape, lambda i: (0, 0), pipeline_mode=pl.Buffered(1))

    def shape(columns):
        return pltpu.HBM((slots, columns), jnp.bfloat16)

    sides = [width + side] + [width] * (count - 1)
    outs = sides + list(weighted_widths) + [model_width, model_width, hidden, hidden, hidden]
    flops = 2 * slots * model_width * hidden * 6
    return pl.pallas_call(
        functools.partial(
            expert_kernel,
            count=count,
            grads_widths=tuple(grads_widths),
            weighted_widths=tuple(weighted_widths),
            experts=plane_size,
        ),
        grid=(expert_steps,),
        in_specs=[pl.BlockSpec(memory_space=pltpu.SMEM)]
        + [whole(array) for array in (w_router, w_gate, w_up, w_down)]
        + [tile(width)] * count
        + [tile(array.shape[1]) for array in grads],
        out_specs=[tile(columns) for columns in outs],
        out_shape=[shape(columns) for columns in outs],
        compiler_params=pltpu.CompilerParams(vmem_limit_bytes=expert_vmem),
        cost_estimate=pl.CostEstimate(
            flops=flops, bytes_accessed=6 * model_width * hidden, transcendentals=slots * hidden
        ),
        name="expert_rows",
    )(ids, w_router, w_gate, w_up, w_down, *rows, *grads)


def local(
    layer_input,
    norm_attn,
    w_query,
    w_key,
    w_value,
    q_gain,
    k_gain,
    w_out,
    norm_moe,
    w_router,
    w_gate,
    w_up,
    w_down,
    seq_lengths,
    routes,
    out_grad,
):
    tok_dev = layer_input.shape[0]
    model_width = layer_input.shape[1]
    group_tok = tok_dev * lax.axis_size(("row", "col"))
    head_dim = q_gain.shape[0]
    experts = w_router.shape[1]
    top_count = routes.shape[1]
    capacity = tok_dev * top_count * 17 // (16 * experts)
    planes = lax.axis_size("expert")
    plane_size = lax.axis_size(plane_axes)
    plane_index = lax.axis_index("expert")
    plane_cap = planes * capacity
    chosen_here = jnp.any(
        routes[:, :, None] == jnp.arange(experts, dtype=jnp.int32)[None, None, :], axis=1
    )
    plane_routes = gather_planes(routes.T)
    plane_experts = plane_index * plane_size + jnp.arange(plane_size, dtype=jnp.int32)
    chosen_plane = jnp.any(
        plane_routes[None] == plane_experts[:, None, None, None], axis=2
    )
    token_ids = jnp.arange(tok_dev, dtype=jnp.int32)
    earlier = (token_ids[:, None] < token_ids[None, :]).astype(jnp.bfloat16)
    slot_rank = jnp.dot(
        chosen_plane.astype(jnp.bfloat16).reshape(plane_size * planes, tok_dev),
        earlier,
        preferred_element_type=jnp.float32,
    ).astype(jnp.int32).reshape(plane_size, planes, tok_dev)
    plane_slot = jnp.where(
        chosen_plane,
        slot_rank + (jnp.arange(planes, dtype=jnp.int32) * capacity)[None, :, None],
        -1,
    ).reshape(plane_size, 1, planes * tok_dev)
    dispatch = (
        plane_slot == jnp.arange(plane_cap, dtype=jnp.int32)[None, :, None]
    ).astype(jnp.bfloat16)
    chosen_all = jnp.any(
        plane_routes[:, :, :, None] == jnp.arange(experts, dtype=jnp.int32), axis=1
    ).reshape(planes * tok_dev, experts).astype(jnp.bfloat16)

    def gather_rows(block):
        return gather_planes(block).reshape(planes * tok_dev, block.shape[1])

    def select_slots(rows_all):
        return jnp.dot(
            dispatch.reshape(plane_size * plane_cap, -1),
            rows_all,
            preferred_element_type=jnp.float32,
        ).astype(jnp.bfloat16)

    def to_plane(slot_values):
        width = slot_values.shape[1]
        moved = move_plane(slot_values.reshape(plane_size, plane_cap, width))
        return moved.reshape(plane_size * plane_cap, width)

    chunk_width = model_width // chunk_count
    chunks = [slice(i * chunk_width, (i + 1) * chunk_width) for i in range(chunk_count)]
    side_width = 128
    grads_widths = parts_of(model_width, grads_first)
    weighted_widths = parts_of(model_width, weighted_first)
    grad_planes = [gather_rows(part) for part in jnp.split(out_grad, [grads_widths[0]], axis=1)]
    grad_planes[0] = jnp.concatenate(
        [grad_planes[0], jnp.pad(chosen_all, ((0, 0), (0, side_width - experts)))], axis=1
    )
    slot_sends = [select_slots(part) for part in grad_planes]
    def gates_of(all_logits, chosen):
        top = jnp.max(jnp.where(chosen, all_logits, -3e38), axis=1, keepdims=True)
        raised = jnp.where(chosen, jnp.exp(jnp.where(chosen, all_logits - top, 0.0)), 0.0)
        return raised / jnp.maximum(jnp.sum(raised, axis=1, keepdims=True), 1e-30)

    input_rows = layer_input.astype(jnp.float32)
    normed_one, norm_one_back = jax.vjp(rms_scale, input_rows, norm_attn)
    normed_low = normed_one.astype(jnp.bfloat16)
    group_rows = lax.all_gather(normed_low, ("row", "col"), axis=0, tiled=True)
    ends = jnp.cumsum(seq_lengths[0], dtype=jnp.int32)
    cosine_table, sine_table = rope_tables(slot_positions(ends, group_tok), head_dim)
    key_value_w = jnp.concatenate([w_key, w_value], axis=1)
    cosine_table, sine_table, key_value_w, slot_sends[0] = together(
        cosine_table, sine_table, key_value_w, slot_sends[0]
    )
    grad_slot_chunks = [to_plane(slot_sends[0])]
    col = lax.axis_index("col")
    kept, sent, query_low, key_low, value_low, heads_low, log_totals, head_scales = attend_rows(
        ends, col.astype(jnp.int32)[None], group_rows, w_query, key_value_w, w_out, q_gain, k_gain, cosine_table, sine_table,
        2 * tok_dev,
    )
    sent, kept, grad_slot_chunks[0] = together(sent, kept, grad_slot_chunks[0])
    col_sums = kept.astype(jnp.float32) + rotate(sent, "col", 1).astype(jnp.float32)
    attn_rows = scatter_rows(col_sums.astype(jnp.bfloat16).reshape(-1, tok_dev, model_width))
    attn_rows, *late_sends = together(attn_rows, *slot_sends[1:])
    grad_slot_chunks += [to_plane(part) for part in late_sends]
    attn_rows = attn_rows.astype(jnp.float32)
    mixed_rows = input_rows + attn_rows
    normed_two, norm_two_back = jax.vjp(rms_scale, mixed_rows, norm_moe)
    moe_input = normed_two.astype(jnp.bfloat16)
    router_logits = jnp.dot(moe_input, w_router, preferred_element_type=jnp.float32)
    source_gates = gates_of(router_logits, chosen_here)

    moe_planes = [gather_rows(moe_input[:, cut]) for cut in chunks]
    moe_sends = [select_slots(part) for part in moe_planes]
    moe_sends[0], *grad_slot_chunks[1:] = together(moe_sends[0], *grad_slot_chunks[1:])
    slot_chunks = [to_plane(part) for part in moe_sends]
    place = lax.axis_index(plane_axes)
    ids = jnp.stack([plane_index * plane_size + place, place]).astype(jnp.int32)
    expert_outs = expert_rows(
        ids,
        jnp.pad(w_router, ((0, 0), (0, side_width - experts))),
        w_gate[0],
        w_up[0],
        w_down[0],
        slot_chunks,
        grad_slot_chunks,
        grads_widths,
        weighted_widths,
        plane_size,
    )
    grad_sends = expert_outs[:chunk_count]
    out_sends = expert_outs[chunk_count : chunk_count + len(weighted_widths)]
    moe_slots, grad_out_slots, hidden_low, grad_gate_pre, grad_up_pre = expert_outs[
        chunk_count + len(weighted_widths) :
    ]

    def to_source(returned):
        summed = lax.dot_general(
            dispatch.reshape(plane_size * plane_cap, -1),
            returned,
            (((0,), (0,)), ((), ())),
            preferred_element_type=jnp.float32,
        ).astype(jnp.bfloat16)
        return return_planes(summed.reshape(planes, tok_dev, returned.shape[1]))

    def add_parts(parts):
        return sum(part.astype(jnp.float32) for part in parts)

    grad_rows = out_grad.astype(jnp.float32)
    grad_down = transposed_times(hidden_low, grad_out_slots)
    grad_gate = transposed_times(moe_slots, grad_gate_pre)
    grad_up = transposed_times(moe_slots, grad_up_pre)
    grad_returns = [to_plane(part) for part in grad_sends]
    grad_returns[0], grad_down = together(grad_returns[0], grad_down)
    grad_returns[-1], grad_gate, *out_sends = together(grad_returns[-1], grad_gate, *out_sends)
    out_returns = [to_plane(out_sends[0])]
    grad_parts = [to_source(part) for part in grad_returns]
    grad_parts[-1][-1], grad_up = together(grad_parts[-1][-1], grad_up)
    side_parts = jnp.stack(
        [part[:, chunk_width:].astype(jnp.float32) for part in grad_parts[0]], axis=0
    )
    dot_parts = side_parts[:, :, :plane_size] + side_parts[:, :, plane_size : 2 * plane_size]
    dot_parts = lax.dynamic_slice_in_dim(
        jnp.concatenate([dot_parts, dot_parts], axis=0), planes - plane_index, planes, axis=0
    )
    grad_gates = jnp.swapaxes(dot_parts, 0, 1).reshape(tok_dev, experts)
    grad_logits = source_gates * (
        grad_gates - jnp.sum(source_gates * grad_gates, axis=1, keepdims=True)
    )
    grad_parts[0] = [part[:, :chunk_width] for part in grad_parts[0]]
    grad_moe_input = jnp.concatenate([add_parts(parts) for parts in grad_parts], axis=1)
    grad_router = lax.dot_general(
        grad_logits,
        moe_input.astype(jnp.float32),
        (((0,), (0,)), ((), ())),
        precision=highest,
        preferred_element_type=jnp.float32,
    )
    grad_moe_input = grad_moe_input + jnp.einsum(
        "te,de->td", grad_logits, w_router, precision=highest, preferred_element_type=jnp.float32
    )
    grad_mixed_norm, grad_norm_moe = norm_two_back(grad_moe_input)
    grad_mixed = grad_rows + grad_mixed_norm
    grad_attn_low = grad_mixed.astype(jnp.bfloat16)
    grad_attn_low, out_returns[0] = together(grad_attn_low, out_returns[0])
    grad_group = lax.all_gather(grad_attn_low, ("row", "col"), axis=0, tiled=True)
    out_first = add_parts(to_source(out_returns[0]))
    grad_group, out_first, *out_late = together(grad_group, out_first, *out_sends[1:])
    out_returns += [to_plane(part) for part in out_late]
    grad_out_proj = transposed_times(heads_low, grad_group).astype(jnp.bfloat16)
    grad_out_proj, grad_group = together(grad_out_proj, grad_group)
    out_terms = send_planes(grad_out_proj)
    grad_query_low, grad_kv, grad_q_gain, grad_k_gain = attend_rows_back(
        ends,
        grad_group,
        w_out,
        query_low,
        heads_low,
        key_low,
        value_low,
        log_totals,
        head_scales,
        q_gain,
        k_gain,
        cosine_table,
        sine_table,
        2 * tok_dev,
    )
    grad_query_low, grad_kv, out_terms[1], out_terms[-1] = together(
        grad_query_low, grad_kv, out_terms[1], out_terms[-1]
    )
    grad_query = transposed_times(group_rows, grad_query_low)
    grad_key_value = transposed_times(group_rows, grad_kv)
    norm_terms = (
        jnp.sum(grad_query * w_query.astype(jnp.float32), axis=1)
        + jnp.sum(grad_key_value * key_value_w.astype(jnp.float32), axis=1)
    ) / norm_attn
    cols = lax.axis_size("col")
    col = lax.axis_index("col")
    kv_low = grad_key_value.astype(jnp.bfloat16).reshape(cols, -1, 2 * head_dim)
    kv_part = lax.dynamic_index_in_dim(kv_low, col, 0, keepdims=False).astype(jnp.float32)
    for k in range(1, cols):
        kv_part = kv_part + rotate(
            lax.dynamic_index_in_dim(kv_low, (col + k) % cols, 0, keepdims=False), "col", k
        ).astype(jnp.float32)
    lane_parts = grad_query.shape[1] // (2 * head_dim)
    query_kv = jnp.concatenate(
        [
            grad_query.astype(jnp.bfloat16),
            *[
                jnp.concatenate(jnp.split(kv_part.astype(jnp.bfloat16), lane_parts), axis=1)
            ],
        ],
        axis=0,
    )
    query_kv = lax.psum(query_kv, "expert")
    left_parts = jnp.concatenate([grad_query_low, grad_kv], axis=1).reshape(
        -1, cols, tok_dev, grad_query_low.shape[1] + 2 * head_dim
    )
    right_all = jnp.concatenate([w_query, key_value_w], axis=1)

    def grad_normed_rows(place):
        left = lax.dynamic_index_in_dim(left_parts, place, 1, keepdims=False)
        return lax.dot_general(
            left, right_all, (((2,), (1,)), ((), ())), preferred_element_type=jnp.float32
        )

    out_share = add_parts(out_terms).astype(jnp.bfloat16)
    summed_values = jnp.concatenate(
        [grad_router.reshape(-1), grad_norm_moe, norm_terms, grad_q_gain[0], grad_k_gain[0]]
    )
    left_parts, out_share, summed_values = together(left_parts, out_share, summed_values)
    sums = sum_all(summed_values)
    out_shares = spread_planes(out_share)
    col_sums = scatter_cols(grad_normed_rows)
    col_sums, *out_returns[1:] = together(col_sums, *out_returns[1:])
    out_parts = [out_first] + [add_parts(to_source(part)) for part in out_returns[1:]]
    grad_normed = scatter_rows(col_sums)
    grad_input_norm = norm_one_back(grad_normed)[0]
    grad_x = (grad_mixed + grad_input_norm).astype(jnp.bfloat16)
    out_rows = (mixed_rows + jnp.concatenate(out_parts, axis=1)).astype(jnp.bfloat16)
    grad_out_proj = in_plane_order(out_shares)
    places = (0, experts * model_width, model_width, model_width, head_dim, head_dim)
    ends_at = [sum(places[: k + 1]) for k in range(len(places))]
    grad_router, grad_norm_moe, grad_norm_attn, grad_q_gain, grad_k_gain = [
        sums[low:high] for low, high in zip(ends_at[:-1], ends_at[1:])
    ]
    grad_router = grad_router.reshape(experts, model_width).T
    grad_x, out_rows, grad_router, query_kv = together(grad_x, out_rows, grad_router, query_kv)
    grad_query = query_kv[:model_width].astype(jnp.float32)
    kv_part = query_kv[model_width:]
    kv_parts = [kv_part] + [rotate(kv_part, "col", k) for k in range(1, cols)]
    kv_blocks = []
    for place in range(cols):
        block = kv_parts[0]
        for k in range(1, cols):
            block = jnp.where((col - k) % cols == place, kv_parts[k], block)
        kv_blocks += jnp.split(block.astype(jnp.float32), lane_parts, axis=1)
    grad_key = jnp.concatenate([block[:, :head_dim] for block in kv_blocks], axis=0)
    grad_value = jnp.concatenate([block[:, head_dim:] for block in kv_blocks], axis=0)
    return (
        out_rows,
        grad_x,
        grad_norm_attn,
        grad_query,
        grad_key,
        grad_value,
        grad_q_gain,
        grad_k_gain,
        grad_out_proj,
        grad_norm_moe,
        grad_router,
        grad_gate[None],
        grad_up[None],
        grad_down[None],
    )


def solution(mesh):
    placed = (
        P(("expert", "row", "col"), None),
        P(),
        P(None, ("row", "col")),
        P(None, "row"),
        P(None, "row"),
        P(),
        P(),
        P(("row", "col"), None),
        P(),
        P(),
        P(("expert", "row", "col"), None, None),
        P(("expert", "row", "col"), None, None),
        P(("expert", "row", "col"), None, None),
        P("expert", None),
        P(("expert", "row", "col"), None),
        P(("expert", "row", "col"), None),
    )
    return jax.shard_map(
        local,
        mesh=mesh,
        in_specs=placed,
        out_specs=(
            P(("expert", "row", "col"), None),
            P(("expert", "row", "col"), None),
            P(),
            P(None, ("row", "col")),
            P(None, "row"),
            P(None, "row"),
            P(),
            P(),
            P(("row", "col"), None),
            P(),
            P(),
            P(("expert", "row", "col"), None, None),
            P(("expert", "row", "col"), None, None),
            P(("expert", "row", "col"), None, None),
        ),
        check_vma=False,
    )
```
